32 devices in a mesh: member: 2 (over y), lon: 4 (over z), lat: 2 (over x), lev: 2 (over core).
Axes of the slice: x: 2, y: 2, z: 4, core: 2. Of those that a mesh axis runs over, the one named last changes fastest.
Arguments:
- tracers: float32 [20, 8, 720, 1440], P('member', 'lev', 'lat', 'lon'), parts along dimension 0, may hold values from -6 to 6
- thickness: float32 [16, 720, 1440], P(('member', 'lev'), 'lat', 'lon'), parts along dimension 0, may hold values from 0.5 to 1.5
- zonal: float32 [16, 720, 1440], P(('member', 'lev'), 'lat', 'lon'), parts along dimension 0, may hold values from -6 to 6
- meridional: float32 [16, 720, 1440], P(('member', 'lev'), 'lat', 'lon'), parts along dimension 0, may hold values from -6 to 6
- cutoff: int32 [2, 60], replicated, may hold values from 1 to 191, as said below
Outputs:
- tracers_out: float32 [20, 8, 720, 1440], P('member', 'lev', 'lat', 'lon'), parts along dimension 0
- thickness_out: float32 [16, 720, 1440], P(('member', 'lev'), 'lat', 'lon'), parts along dimension 0
- zonal_out: float32 [16, 720, 1440], P(('member', 'lev'), 'lat', 'lon'), parts along dimension 0
- meridional_out: float32 [16, 720, 1440], P(('member', 'lev'), 'lat', 'lon'), parts along dimension 0
The draws below stay inside these ranges and needn't reach their ends.
There are 2 independent parts, one for each index of `member`. The reference program is written for one: setup_inputs(seed, part) draws one part's arguments, and reference() takes and returns one part's arrays. A program takes and returns all parts, laid end to end along the dimension named above; an argument that names none is the same for every part. Nothing has to cross between parts.
Inputs may be any that keep to these rules, and one draw needn't show every extreme that they name: `cutoff`: one entry equals 191 in every draw.
All inputs are finite; a program needn't handle non-finite values.
Results may differ from the reference program's by a relative error of at most 0.00011.
Values sent between devices are 32-bit elements; how exact they have to be, the bound alone decides.
No kernel may reach another device: no remote copies, remote signals or barrier semaphores. Data moves between devices by JAX's collectives and lax.ppermute only.
A program may use at most 320 MiB of HBM per device.

```python
import jax
import jax.numpy as jnp
from jax import lax

NLON = 1440
NLAT = 720
NTRAC = 10
NSUB = 2
POLAR = 60
KMAX = 191
LEV = 8


def draw_cutoff(key, part):
    key = jax.random.fold_in(key, 11)
    limits = jax.random.randint(key, (2, POLAR), 1, KMAX + 1).astype(jnp.int32)
    return limits.at[0, 0].set(KMAX)


def level_of(key, dims, split, least, largest):
    loudness, own = 1.0, jax.random.fold_in(key, 6)
    for axis_at, blocks in split:
        draws = jnp.exp(jax.random.uniform(jax.random.fold_in(own, axis_at), (blocks,), jnp.float32, least / len(split), largest / len(split)))
        loudness = loudness * jnp.repeat(draws, dims[axis_at] // blocks).reshape([-1 if axis == axis_at else 1 for axis in range(len(dims))])
    return loudness


def centred(key, dims, width, reach, split=(), kind=jnp.bfloat16):
    loudness = level_of(key, dims, split, -0.22, 0.18) if split else 1.0
    values = jax.random.normal(key, dims, jnp.float32) * width * loudness
    return jnp.minimum(jnp.maximum(values, -reach), reach).astype(kind)


def setup_inputs(seed: int = 0, part: int = 0) -> dict:
    streams_of = jax.random.split(jax.random.key(seed), 6)
    own_keys = jax.random.split(jax.random.fold_in(streams_of[5], part), 6)
    tracers = centred(own_keys[0], (NTRAC, LEV, NLAT, NLON), 1.0, 6.0, ((1, 2), (2, 2), (3, 4)), jnp.float32)
    thickness = jnp.clip(0.5 + 1.0 * jax.random.uniform(own_keys[1], (LEV, NLAT, NLON), jnp.float32) ** level_of(own_keys[1], (LEV, NLAT, NLON), ((0, 2), (1, 2), (2, 4)), -0.2, 0.2), 0.5, 1.5)
    zonal = centred(own_keys[2], (LEV, NLAT, NLON), 1.0, 6.0, ((0, 2), (1, 2), (2, 4)), jnp.float32)
    meridional = centred(own_keys[3], (LEV, NLAT, NLON), 1.0, 6.0, ((0, 2), (1, 2), (2, 4)), jnp.float32)
    cutoff = draw_cutoff(jax.random.fold_in(streams_of[5], 71), part)
    return {"tracers": tracers, "thickness": thickness, "zonal": zonal, "meridional": meridional, "cutoff": cutoff}


COURANT_CAP = 0.15
GRADIENT_COEF = 0.1


def advance_level(extended, pressure):
    tracer_count = extended.shape[0] - 3
    thick = extended[tracer_count]
    east_wind = extended[tracer_count + 1]
    north_wind = extended[tracer_count + 2]
    masses = jnp.concatenate([thick[None], extended[:tracer_count] * thick[None]], 0)
    east_courant = COURANT_CAP * jnp.tanh(0.5 * (east_wind[1:-1, :-1] + east_wind[1:-1, 1:]))
    east_flux = jnp.maximum(east_courant, 0.0) * masses[:, 1:-1, :-1] + jnp.minimum(east_courant, 0.0) * masses[:, 1:-1, 1:]
    south_courant = COURANT_CAP * jnp.tanh(0.5 * (north_wind[:-1, 1:-1] + north_wind[1:, 1:-1]))
    south_flux = jnp.maximum(south_courant, 0.0) * masses[:, :-1, 1:-1] + jnp.minimum(south_courant, 0.0) * masses[:, 1:, 1:-1]
    updated = masses[:, 1:-1, 1:-1] - (east_flux[:, :, 1:] - east_flux[:, :, :-1]) - (south_flux[:, 1:] - south_flux[:, :-1])
    new_thick = updated[0]
    new_mixing = updated[1:] / new_thick[None]
    new_east = east_wind[1:-1, 1:-1] - GRADIENT_COEF * (pressure[1:-1, 2:] - pressure[1:-1, :-2])
    new_north = north_wind[1:-1, 1:-1] - GRADIENT_COEF * (pressure[2:, 1:-1] - pressure[:-2, 1:-1])
    return new_mixing, new_thick, new_east, new_north


def lowpass(values, limits):
    spectrum = jnp.fft.rfft(values, axis=-1)
    wavenumber = jnp.arange(spectrum.shape[-1])
    spectrum = jnp.where(wavenumber[None, None, :] <= limits[None, :, None], spectrum, 0)
    return jnp.fft.irfft(spectrum, n=values.shape[-1], axis=-1).astype(values.dtype)


def filter_field(field, cutoff):
    north_part = lowpass(field[:, :POLAR], cutoff[0])
    south_part = lowpass(field[:, NLAT - POLAR:], cutoff[1])
    return field.at[:, :POLAR].set(north_part).at[:, NLAT - POLAR:].set(south_part)


def extend(field, flip_sign):
    north_rim = jnp.roll(field[..., 0, :], NLON // 2, axis=-1) * flip_sign
    south_rim = jnp.roll(field[..., -1, :], NLON // 2, axis=-1) * flip_sign
    padded = jnp.concatenate([north_rim[..., None, :], field, south_rim[..., None, :]], -2)
    return jnp.concatenate([padded[..., -1:], padded, padded[..., :1]], -1)


def reference(tracers, thickness, zonal, meridional, cutoff):
    flip_sign = jnp.concatenate([jnp.ones((NTRAC + 1,), jnp.float32), -jnp.ones((2,), jnp.float32)])[:, None, None]
    for substep in range(NSUB):
        zonal = filter_field(zonal, cutoff)
        meridional = filter_field(meridional, cutoff)
        state = jnp.concatenate([tracers, thickness[None], zonal[None], meridional[None]], 0)
        extended = extend(state, flip_sign)
        thick_ext = extended[NTRAC]
        pressure = jnp.cumsum(thick_ext, axis=0) - 0.5 * thick_ext
        mixing, thickness, zonal, meridional = lax.map(
            lambda level_pair: advance_level(level_pair[0], level_pair[1]),
            (jnp.moveaxis(extended, 1, 0), pressure))
        tracers = jnp.moveaxis(mixing, 0, 1)
    return tracers, thickness, zonal, meridional
```

```python
import functools
import math

import jax
import jax.numpy as jnp
import numpy as np
from jax import lax
from jax.experimental import pallas as pl
from jax.experimental.pallas import tpu as pltpu
from jax.sharding import PartitionSpec as P

NSUB = 2
POLAR = 60
KMAX = 191


COURANT_CAP = 0.15
GRADIENT_COEF = 0.1


def extended_2(block, sides, width):
    for axis, dim in sides:
        count = lax.axis_size(axis)
        forward = [(i, i + 1) for i in range(count - 1)]
        forward.append((count - 1, 0))
        backward = [(target, source) for source, target in forward]
        low = lax.ppermute(
            lax.slice_in_dim(block, block.shape[dim] - width, None, axis=dim), axis, forward
        )
        high = lax.ppermute(lax.slice_in_dim(block, 0, width, axis=dim), axis, backward)
        block = jnp.concatenate([low, block, high], axis=dim)
    return block


def shifted(block, axis, distance):
    devices = range(lax.axis_size(axis))
    route = [((i - distance) % len(devices), i) for i in devices]
    return lax.ppermute(block, axis, route)


def entering(value, axis, join, neutral):
    count, mine = (lax.axis_size(axis), lax.axis_index(axis))
    pieces = lax.all_gather(value, axis)
    running = jnp.full_like(value, 0) + jnp.asarray(neutral, value.dtype)

    def step(position, running):
        longer = join(running, pieces[position])
        return jnp.where(position < mine, longer, running)

    return lax.fori_loop(0, count - 1, step, running)


def advance_level(extended, pressure):
    tracer_count = extended.shape[0] - 3
    thick = extended[tracer_count]
    east_wind = extended[tracer_count + 1]
    north_wind = extended[tracer_count + 2]
    masses = jnp.concatenate([thick[None], extended[:tracer_count] * thick[None]], 0)
    east_courant = COURANT_CAP * jnp.tanh(0.5 * (east_wind[1:-1, :-1] + east_wind[1:-1, 1:]))
    east_flux = (
        jnp.maximum(east_courant, 0.0) * masses[:, 1:-1, :-1]
        + jnp.minimum(east_courant, 0.0) * masses[:, 1:-1, 1:]
    )
    south_courant = COURANT_CAP * jnp.tanh(0.5 * (north_wind[:-1, 1:-1] + north_wind[1:, 1:-1]))
    south_flux = (
        jnp.maximum(south_courant, 0.0) * masses[:, :-1, 1:-1]
        + jnp.minimum(south_courant, 0.0) * masses[:, 1:, 1:-1]
    )
    updated = (
        masses[:, 1:-1, 1:-1]
        - (east_flux[:, :, 1:] - east_flux[:, :, :-1])
        - (south_flux[:, 1:] - south_flux[:, :-1])
    )
    new_thick = updated[0]
    new_mixing = updated[1:] / new_thick[None]
    new_east = east_wind[1:-1, 1:-1] - GRADIENT_COEF * (pressure[1:-1, 2:] - pressure[1:-1, :-2])
    new_north = north_wind[1:-1, 1:-1] - GRADIENT_COEF * (pressure[2:, 1:-1] - pressure[:-2, 1:-1])
    return (new_mixing, new_thick, new_east, new_north)


def wave_basis(anchor, length, lon_total):
    cells = anchor + jnp.arange(length, dtype=jnp.int32)
    waves = jnp.arange(KMAX + 1, dtype=jnp.int32)
    phase = (cells[:, None] * waves[None, :] % lon_total).astype(jnp.float32) * (
        2.0 * math.pi / lon_total
    )
    return jnp.concatenate([jnp.cos(phase), jnp.sin(phase)], 1)


def wave_weights(limits, lon_total):
    waves = jnp.arange(KMAX + 1, dtype=jnp.int32)
    scaled = jnp.where(waves == 0, 1.0, 2.0).astype(jnp.float32) / lon_total
    kept = jnp.where(waves[None, :] <= limits[:, None], scaled[None, :], 0.0)
    return jnp.concatenate([kept, kept], 1)


def smooth_winds(zonal, meridional, cutoff, is_north, is_south):
    level_count, row_count, col_count = zonal.shape
    lon_count = lax.axis_size("lon")
    lon_total = col_count * lon_count
    north_rows = jnp.stack([zonal[:, :POLAR], meridional[:, :POLAR]], 0)
    south_rows = jnp.stack([zonal[:, row_count - POLAR :], meridional[:, row_count - POLAR :]], 0)
    selected = jnp.where(is_north, north_rows, south_rows).reshape(-1, col_count)
    limits = jnp.tile(jnp.where(is_north, cutoff[0], cutoff[1]), 2 * level_count)
    fragment = lax.all_gather(selected, "lon", axis=1, tiled=True)
    basis = wave_basis(jnp.int32(0), fragment.shape[1], lon_total)
    spectrum = jnp.dot(
        fragment, basis, precision=lax.Precision.HIGHEST, preferred_element_type=jnp.float32
    )
    own_basis = wave_basis(lax.axis_index("lon") * col_count, col_count, lon_total)
    filtered = jnp.dot(
        spectrum * wave_weights(limits, lon_total),
        own_basis.T,
        precision=lax.Precision.HIGHEST,
        preferred_element_type=jnp.float32,
    )
    filtered = filtered.reshape(2, level_count, POLAR, col_count)
    row_start = jnp.where(is_north, 0, row_count - POLAR).astype(jnp.int32)
    polar_band = jnp.logical_or(is_north, is_south)
    new_zonal = lax.dynamic_update_slice_in_dim(zonal, filtered[0], row_start, 1)
    new_merid = lax.dynamic_update_slice_in_dim(meridional, filtered[1], row_start, 1)
    return (jnp.where(polar_band, new_zonal, zonal), jnp.where(polar_band, new_merid, meridional))


def shards(tracers, thickness, zonal, meridional, cutoff):
    tracer_count = tracers.shape[0]
    lat_index = lax.axis_index("lat")
    is_north = lat_index == 0
    is_south = lat_index == lax.axis_size("lat") - 1
    lon_count = lax.axis_size("lon")
    flip_sign = jnp.concatenate(
        [jnp.ones((tracer_count + 1,), jnp.float32), -jnp.ones((2,), jnp.float32)]
    )[:, None, None]
    advance_all = jax.vmap(advance_level, in_axes=(1, 0), out_axes=(1, 0, 0, 0))
    for substep in range(NSUB):
        zonal, meridional = smooth_winds(zonal, meridional, cutoff, is_north, is_south)
        state = jnp.concatenate([tracers, thickness[None], zonal[None], meridional[None]], 0)
        extended = extended_2(state, (("lat", 2), ("lon", 3)), 1)
        edges = jnp.stack([state[:, :, 0], state[:, :, -1]], 2)
        opposite = shifted(edges, "lon", lon_count // 2)
        north_rim = jnp.where(is_north, opposite[:, :, 0] * flip_sign, extended[:, :, 0, 1:-1])
        south_rim = jnp.where(is_south, opposite[:, :, 1] * flip_sign, extended[:, :, -1, 1:-1])
        extended = extended.at[:, :, 0, 1:-1].set(north_rim)
        extended = extended.at[:, :, -1, 1:-1].set(south_rim)
        thick_ext = extended[tracer_count]
        column_above = entering(
            jnp.sum(thick_ext, 0),
            "lev",
            lambda earlier, later: earlier + later,
            jnp.zeros(thick_ext.shape[1:], jnp.float32),
        )
        pressure = jnp.cumsum(thick_ext, axis=0) - 0.5 * thick_ext + column_above[None]
        tracers, thickness, zonal, meridional = advance_all(extended, pressure)
    return (tracers, thickness, zonal, meridional)


LANE = 128
PAD = 16
BAND = 64


def cost(flops, moved):
    return pl.CostEstimate(flops=int(flops), bytes_accessed=int(moved), transcendentals=0)


def params(mib=56):
    return pltpu.CompilerParams(vmem_limit_bytes=mib * 1024 * 1024)


def lanes():
    return lax.broadcasted_iota(jnp.int32, (8, LANE), 1)


def eight(index):
    return pl.ds(pl.multiple_of(8 * index, 8), 8)


def from_east(tiles, lane):
    turned = [pltpu.roll(t, LANE - 1, 1) for t in tiles]
    n = len(tiles)
    return [jnp.where(lane < LANE - 1, turned[c], turned[(c + 1) % n]) for c in range(n)]


def from_west(tiles, lane):
    turned = [pltpu.roll(t, 1, 1) for t in tiles]
    n = len(tiles)
    return [jnp.where(lane > 0, turned[c], turned[(c - 1) % n]) for c in range(n)]


def courant(a, b):
    return COURANT_CAP * jnp.tanh(0.5 * (a + b))


def rim_lanes(east, west, plane, last, lane):
    to_east = lax.rem(last + LANE - 2 * plane, LANE)
    to_west = lax.rem(2 * LANE - 2 - 2 * plane, LANE)
    return jnp.where(lane < last + 2, pltpu.roll(east, to_east, 1), pltpu.roll(west, to_west, 1))


def inflows(h, u, v, h_n, h_s, v_n, v_s, lane):
    count = range(len(h))
    u_e, h_e = from_east(u, lane), from_east(h, lane)
    c_e = [courant(u[c], u_e[c]) for c in count]
    out_e = [jnp.maximum(c_e[c], 0.0) * h[c] for c in count]
    in_e = [jnp.maximum(-c_e[c], 0.0) * h_e[c] for c in count]
    in_w, out_w = from_west(out_e, lane), from_west(in_e, lane)
    c_s = [courant(v[c], v_s[c]) for c in count]
    c_n = [courant(v_n[c], v[c]) for c in count]
    in_s = [jnp.maximum(-c_s[c], 0.0) * h_s[c] for c in count]
    out_s = [jnp.maximum(c_s[c], 0.0) * h[c] for c in count]
    in_n = [jnp.maximum(c_n[c], 0.0) * h_n[c] for c in count]
    out_n = [jnp.maximum(-c_n[c], 0.0) * h[c] for c in count]
    new = [
        h[c] - (out_e[c] - in_e[c]) + (in_w[c] - out_w[c]) - (out_s[c] - in_s[c]) + (in_n[c] - out_n[c])
        for c in count
    ]
    return in_e, in_w, in_n, in_s, new


def tiles_at(ref, base, count, lead=()):
    return [ref[lead + (c, base, slice(None))] for c in range(count)]


def inflows_at(h, u, v, row, count, lead, lane):
    mid = pl.ds(pl.multiple_of(row, 8), 8)
    up, down = pl.ds(row - 1, 8), pl.ds(row + 1, 8)
    hl, vl = lead
    return inflows(
        tiles_at(h, mid, count, hl),
        tiles_at(u, mid, count, vl),
        tiles_at(v, mid, count, vl),
        tiles_at(h, up, count, hl),
        tiles_at(h, down, count, hl),
        tiles_at(v, up, count, vl),
        tiles_at(v, down, count, vl),
        lane,
    )


def band_kernel(n, s, *refs):
    ins, outs = refs[: 3 * n], refs[3 * n :]
    for north in (True, False):

        @pl.when(s[0] == int(north))
        def _():
            lo = 0 if north else BAND - POLAR
            for d in range(n):
                u, v, h = ins[3 * d : 3 * d + 3]
                outs[d][0:POLAR, :] = u[0, lo : lo + POLAR, :]
                outs[d][POLAR : 2 * POLAR, :] = v[0, lo : lo + POLAR, :]
                first = 0 if north else BAND - POLAR - 1
                outs[d][2 * POLAR : 3 * POLAR + 1, :] = h[0, first : first + POLAR + 1, :]
                outs[d][3 * POLAR + 1 :, :] = jnp.zeros((3, h.shape[2]), jnp.float32)


def band_rows(scalars, u, v, h, n):
    levels, _, cols = u.shape

    def spec(d):
        return pl.BlockSpec(
            (pl.Element(1), pl.Element(BAND), pl.Element(cols)),
            lambda i, s: (lax.rem(s[1] + d, n), s[2] * 8, 0),
        )

    rows = 3 * POLAR + 4
    return pl.pallas_call(
        functools.partial(band_kernel, n),
        grid_spec=pltpu.PrefetchScalarGridSpec(
            num_scalar_prefetch=1,
            grid=(1,),
            in_specs=[spec(d) for d in range(n) for _ in range(3)],
            out_specs=[pl.BlockSpec((rows, cols), lambda i, s: (0, 0))] * n,
        ),
        out_shape=[jax.ShapeDtypeStruct((rows, cols), jnp.float32)] * n,
        cost_estimate=cost(1e6, 8 * n * rows * cols),
        compiler_params=params(),
        name="band_rows",
    )(scalars, *([u, v, h] * n))


def spectrum_kernel(n, s, *refs):
    total = None
    for d in range(n):
        part = jnp.dot(
            refs[d][...],
            refs[n + d][0],
            precision=lax.Precision.HIGHEST,
            preferred_element_type=jnp.float32,
        )
        total = part if total is None else total + part
    refs[2 * n][...] = total


def spectra(scalars, pieces, basis):
    n = len(pieces)
    rows, cols = pieces[0].shape
    waves = basis.shape[2]

    def spec(d):
        return pl.BlockSpec((1, cols, waves), lambda i, s: (lax.rem(s[1] + n - d, n), 0, 0))

    return pl.pallas_call(
        functools.partial(spectrum_kernel, n),
        grid_spec=pltpu.PrefetchScalarGridSpec(
            num_scalar_prefetch=1,
            grid=(1,),
            in_specs=[pl.BlockSpec((rows, cols), lambda i, s: (0, 0))] * n + [spec(d) for d in range(n)],
            out_specs=pl.BlockSpec((rows, waves), lambda i, s: (0, 0)),
        ),
        out_shape=jax.ShapeDtypeStruct((rows, waves), jnp.float32),
        cost_estimate=cost(12 * n * rows * cols * waves, 4 * n * cols * (rows + waves)),
        compiler_params=params(),
        name="spectra",
    )(scalars, *pieces, *([basis] * n))


def pack_kernel(fields, last, t_lo, t_hi, h_lo, h_hi, u_lo, u_hi, v_lo, v_hi, west, east):
    level = pl.program_id(0)
    lane = lanes()
    lows = [(t_lo, (f, 0)) for f in range(fields - 3)] + [(h_lo, (0,)), (u_lo, (0,)), (v_lo, (0,))]
    highs = [(t_hi, (f, 0)) for f in range(fields - 3)] + [(h_hi, (0,)), (u_hi, (0,)), (v_hi, (0,))]
    begin = 2 * fields * level
    mine = jnp.logical_and(lane >= begin, lane < begin + 2 * fields)

    def step(i, _):
        rows = eight(i)
        got_w = got_e = jnp.zeros((8, LANE), jnp.float32)
        for f in range(fields):
            here = lane // 2 == f
            ref, lead = lows[f]
            tile = ref[lead + (rows, slice(None))]
            got_w = jnp.where(here, pltpu.roll(tile, 2 * f, 1) if f else tile, got_w)
            ref, lead = highs[f]
            tile = ref[lead + (rows, slice(None))]
            got_e = jnp.where(here, pltpu.roll(tile, (2 * f - last + 2) % LANE, 1), got_e)
        west[rows, :] = jnp.where(mine, pltpu.roll(got_w, begin, 1), west[rows, :])
        east[rows, :] = jnp.where(mine, pltpu.roll(got_e, begin, 1), east[rows, :])
        return 0

    lax.fori_loop(0, west.shape[0] // 8, step, 0)


def pack_columns(tracers, h, u, v):
    count, levels, rows, cols = tracers.shape
    high = (cols - 1) // LANE
    t_spec = [pl.BlockSpec((count, 1, rows, LANE), lambda l, c=c: (0, l, 0, c)) for c in (0, high)]
    f_spec = [pl.BlockSpec((1, rows, LANE), lambda l, c=c: (l, 0, c)) for c in (0, high)]
    out = jax.ShapeDtypeStruct((rows, LANE), jnp.float32)
    return pl.pallas_call(
        functools.partial(pack_kernel, count + 3, cols - LANE * high),
        grid=(levels,),
        in_specs=t_spec + f_spec * 3,
        out_specs=[pl.BlockSpec((rows, LANE), lambda l: (0, 0))] * 2,
        out_shape=[out, out],
        cost_estimate=cost(1e7, 8 * (count + 3) * levels * rows * LANE),
        compiler_params=params(),
        name="pack_columns",
    )(tracers, tracers, h, h, u, u, v, v)


def rows_kernel(fields, s, t_top, t_bot, h_top, h_bot, u_top, u_bot, v_top, v_bot,
                e_top, e_bot, w_top, w_bot, pole, facing, top, bot):
    level = pl.program_id(0)
    lane = lanes()
    cols = h_top.shape[2]
    tail = top.shape[1] - LANE
    last = cols - tail
    refs = [(t_top, t_bot, (f, 0)) for f in range(fields - 3)]
    refs += [(h_top, h_bot, (0,)), (u_top, u_bot, (0,)), (v_top, v_bot, (0,))]
    for f in range(fields):
        plane = fields * level + f
        a, b, lead = refs[f]
        top[:, 0:cols] = a[lead]
        bot[:, 0:cols] = b[lead]
        top[:, cols:] = rim_lanes(e_top[...], w_top[...], plane, last, lane)[:, last:]
        bot[:, cols:] = rim_lanes(e_bot[...], w_bot[...], plane, last, lane)[:, last:]
        flip = -1.0 if f == fields - 1 else 1.0

        @pl.when(s[0] == 1)
        def _():
            pole[0, f, 0:1, :] = flip * top[1:2, :]
            pole[0, f, 1:2, :] = flip * top[0:1, :]
            facing[0, f] = bot[6:8, :]

        @pl.when(s[0] == 0)
        def _():
            pole[0, f, 0:1, :] = flip * bot[7:8, :]
            pole[0, f, 1:2, :] = flip * bot[6:7, :]
            facing[0, f] = top[0:2, :]


def edge_rows(scalars, tracers, h, u, v, east, west):
    count, levels, rows, cols = tracers.shape
    fields = count + 3
    width = LANE * ((cols - 1) // LANE + 1)
    ends = (0, rows // 8 - 1)
    t_spec = [pl.BlockSpec((count, 1, 8, cols), lambda l, s, r=r: (0, l, r, 0)) for r in ends]
    f_spec = [pl.BlockSpec((1, 8, cols), lambda l, s, r=r: (l, r, 0)) for r in ends]
    c_spec = [pl.BlockSpec((8, LANE), lambda l, s, r=r: (r, 0)) for r in ends]
    out = jax.ShapeDtypeStruct((levels, fields, 2, width), jnp.float32)
    return pl.pallas_call(
        functools.partial(rows_kernel, fields),
        grid_spec=pltpu.PrefetchScalarGridSpec(
            num_scalar_prefetch=1,
            grid=(levels,),
            in_specs=t_spec + f_spec * 3 + c_spec * 2,
            out_specs=[pl.BlockSpec((1, fields, 2, width), lambda l, s: (l, 0, 0, 0))] * 2,
            scratch_shapes=[pltpu.VMEM((8, width), jnp.float32)] * 2,
        ),
        out_shape=[out, out],
        cost_estimate=cost(1e6, 100 * levels * fields * width),
        compiler_params=params(),
        name="edge_rows",
    )(scalars, tracers, tracers, h, h, u, u, v, v, east, east, west, west)


def extend_kernel(fields, s, h, u, v, east, west, pole, facing, h_out, u_out, v_out, total):
    level = pl.program_id(0)
    lane = lanes()
    rows, cols = h.shape[1:]
    count = h_out.shape[1]
    last = cols - LANE * (count - 1)
    for f, (ref, out) in enumerate(((h, h_out), (u, u_out), (v, v_out))):
        plane = fields * level + fields - 3 + f

        def step(i, _):
            here, there = eight(i), pl.ds(pl.multiple_of(8 * i, 8) + PAD, 8)
            for c in range(count - 1):
                out[0, c, there, :] = ref[0, here, c * LANE : (c + 1) * LANE]
            out[0, count - 1, there, 0:last] = ref[0, here, LANE * (count - 1) : cols]
            rim = rim_lanes(east[here, :], west[here, :], plane, last, lane)
            out[0, count - 1, there, last:] = rim[:, last:]
            return 0

        lax.fori_loop(0, rows // 8, step, 0)
        for c in range(count):
            part = slice(c * LANE, (c + 1) * LANE)
            a = pole[0, fields - 3 + f, :, part]
            b = facing[0, fields - 3 + f, :, part]
            out[0, c, PAD - 2 : PAD, :] = jnp.where(s[0] == 1, a, b)
            out[0, c, PAD + rows : PAD + rows + 2, :] = jnp.where(s[0] == 1, b, a)

    def add(i, _):
        here = eight(i)
        for c in range(count):
            now = h_out[0, c, here, :]
            total[c, here, :] = jnp.where(level == 0, now, total[c, here, :] + now)
        return 0

    lax.fori_loop(0, h_out.shape[2] // 8, add, 0)


def extend_fields(scalars, h, u, v, east, west, pole, facing):
    levels, rows, cols = h.shape
    fields = pole.shape[1]
    count = (cols - 1) // LANE + 1
    tall = rows + 2 * PAD
    f_spec = pl.BlockSpec((1, rows, cols), lambda l, s: (l, 0, 0))
    c_spec = pl.BlockSpec((rows, LANE), lambda l, s: (0, 0))
    r_spec = pl.BlockSpec((1, fields, 2, count * LANE), lambda l, s: (l, 0, 0, 0))
    out = jax.ShapeDtypeStruct((levels, count, tall, LANE), jnp.float32)
    return pl.pallas_call(
        functools.partial(extend_kernel, fields),
        grid_spec=pltpu.PrefetchScalarGridSpec(
            num_scalar_prefetch=1,
            grid=(levels,),
            in_specs=[f_spec] * 3 + [c_spec] * 2 + [r_spec] * 2,
            out_specs=[pl.BlockSpec((1, count, tall, LANE), lambda l, s: (l, 0, 0, 0))] * 3
            + [pl.BlockSpec((count, tall, LANE), lambda l, s: (0, 0, 0))],
        ),
        out_shape=[out] * 3 + [jax.ShapeDtypeStruct((count, tall, LANE), jnp.float32)],
        cost_estimate=cost(1e6, 28 * levels * tall * count * LANE),
        compiler_params=params(),
        name="extend_fields",
    )(scalars, h, u, v, east, west, pole, facing)


def first_kernel(h, u, v, above, u_out, v_out, h_out, total, cum, press):
    level = pl.program_id(0)
    lane = lanes()
    count, tall = h.shape[1:3]

    def column(i, _):
        here = eight(i)
        for c in range(count):
            before = jnp.where(level == 0, above[c, here, :], cum[c, here, :])
            now = h[0, c, here, :]
            press[c, here, :] = before + 0.5 * now
            cum[c, here, :] = before + now
        return 0

    lax.fori_loop(0, tall // 8, column, 0)

    def step(i, _):
        row = 8 * i
        here = eight(i)
        p = tiles_at(press, here, count)
        p_e, p_w = from_east(p, lane), from_west(p, lane)
        p_n, p_s = tiles_at(press, pl.ds(row - 1, 8), count), tiles_at(press, pl.ds(row + 1, 8), count)
        new = inflows_at(h, u, v, row, count, ((0,), (0,)), lane)[4]
        for c in range(count):
            u_out[0, c, here, :] = u[0, c, here, :] - GRADIENT_COEF * (p_e[c] - p_w[c])
            v_out[0, c, here, :] = v[0, c, here, :] - GRADIENT_COEF * (p_s[c] - p_n[c])
            h_out[0, c, here, :] = new[c]
            total[c, here, :] = jnp.where(level == 0, new[c], total[c, here, :] + new[c])
        return 0

    lax.fori_loop(1, tall // 8 - 1, step, 0)


def first_substep(h, u, v, above):
    levels, count, tall, _ = h.shape
    spec = pl.BlockSpec((1, count, tall, LANE), lambda l: (l, 0, 0, 0))
    flat = pl.BlockSpec((count, tall, LANE), lambda l: (0, 0, 0))
    out = jax.ShapeDtypeStruct(h.shape, jnp.float32)
    return pl.pallas_call(
        first_kernel,
        grid=(levels,),
        in_specs=[spec] * 3 + [flat],
        out_specs=[spec] * 3 + [flat],
        out_shape=[out] * 3 + [jax.ShapeDtypeStruct((count, tall, LANE), jnp.float32)],
        scratch_shapes=[pltpu.VMEM((count, tall, LANE), jnp.float32)] * 2,
        cost_estimate=cost(80 * h.size, 30 * h.size),
        compiler_params=params(),
        name="first_substep",
    )(h, u, v, above)


def filter_kernel(n, s, *refs):
    pieces = refs[:n]
    above, limits, basis, slope, h0, u0, v0, u1, v1 = refs[n : n + 9]
    u0_out, v0_out, u1_out, v1_out, h1_out, total = refs[n + 9 : n + 15]
    held, lhs, rhs = refs[n + 15 :]
    levels, count, slab = u0.shape[:3]
    waves = basis.shape[1]
    for d in range(n):
        held[lax.rem(s[1] + n - d, n)] = pieces[d][...]
    for raw, out in ((u0, u0_out), (v0, v0_out), (u1, u1_out), (v1, v1_out)):
        out[...] = raw[...]
    half = waves // 2
    wave = lax.broadcasted_iota(jnp.int32, (POLAR, waves), 1)
    wave = jnp.where(wave < half, wave, wave - half)
    scale = jnp.where(wave == 0, 1.0, 2.0) / (n * s[3]).astype(jnp.float32)
    keep = jnp.where(wave <= limits[0:POLAR, 0:1], scale, 0.0)
    turn = jnp.where(lax.rem(wave[0:2], 2) == 0, 1.0, -1.0)
    one = turn[0:1]
    for north in (True, False):

        @pl.when(s[0] == int(north))
        def _():
            first = PAD if north else PAD + BAND - POLAR
            rim = PAD - 2 if north else PAD + BAND

            def level_step(l, cum):
                u = held[l, 0:POLAR, :] * keep
                v = held[l, POLAR : 2 * POLAR, :] * keep
                thick = held[l, 2 * POLAR : 3 * POLAR + 1, :]
                p = cum + 0.5 * thick
                if north:
                    before = jnp.concatenate([one * p[0:1], p[0 : POLAR - 1]], 0)
                    diff = (p[1:] - before) * keep
                    rhs[0:POLAR, :] = p[0:POLAR] * keep
                else:
                    after = jnp.concatenate([p[2:], one * p[POLAR:]], 0)
                    diff = (after - p[0:POLAR]) * keep
                    rhs[0:POLAR, :] = p[1:] * keep
                w = v - GRADIENT_COEF * diff
                lhs[0:POLAR, :] = u
                lhs[POLAR : 2 * POLAR, :] = v
                lhs[2 * POLAR : 3 * POLAR, :] = w
                for k, (x, sign) in enumerate(((u, 1.0), (v, -1.0), (w, -1.0))):
                    a, b = (x[1:2], x[0:1]) if north else (x[POLAR - 1 :], x[POLAR - 2 : POLAR - 1])
                    at = 3 * POLAR + 2 * k
                    lhs[at : at + 1, :] = sign * one * a
                    lhs[at + 1 : at + 2, :] = sign * one * b
                back = jnp.dot(
                    lhs[...], basis[0], precision=lax.Precision.HIGHEST, preferred_element_type=jnp.float32
                )
                grad = jnp.dot(
                    rhs[...], slope[0], precision=lax.Precision.HIGHEST, preferred_element_type=jnp.float32
                )
                zonal = back[0:POLAR]
                later = zonal - GRADIENT_COEF * grad[0:POLAR]
                for c in range(count):
                    part = slice(c * LANE, (c + 1) * LANE)
                    u0_out[l, c, first : first + POLAR, :] = zonal[:, part]
                    v0_out[l, c, first : first + POLAR, :] = back[POLAR : 2 * POLAR, part]
                    u1_out[l, c, first : first + POLAR, :] = later[:, part]
                    v1_out[l, c, first : first + POLAR, :] = back[2 * POLAR : 3 * POLAR, part]
                    u0_out[l, c, rim : rim + 2, :] = back[3 * POLAR : 3 * POLAR + 2, part]
                    v0_out[l, c, rim : rim + 2, :] = back[3 * POLAR + 2 : 3 * POLAR + 4, part]
                    v1_out[l, c, rim : rim + 2, :] = back[3 * POLAR + 4 : 3 * POLAR + 6, part]
                return cum + thick

            lax.fori_loop(0, levels, level_step, above[0 : POLAR + 1, :])

    lane = lanes()

    def step(k, _):
        l, i = k // (slab // 8 - 2), lax.rem(k, slab // 8 - 2) + 1
        here = eight(i)
        new = inflows_at(h0, u0_out, v0_out, 8 * i, count, ((l,), (l,)), lane)[4]
        for c in range(count):
            h1_out[l, c, here, :] = new[c]
            total[c, here, :] = jnp.where(l == 0, new[c], total[c, here, :] + new[c])
        return 0

    lax.fori_loop(0, levels * (slab // 8 - 2), step, 0)


def filtered_band(scalars, pieces, above, limits, basis, slope, fields):
    n = len(pieces)
    rows, waves = pieces[0].shape
    width = basis.shape[2]
    levels, count = fields[0].shape[:2]
    slab = BAND + 2 * PAD
    window = pl.BlockSpec(
        (pl.Element(levels), pl.Element(count), pl.Element(slab), pl.Element(LANE)),
        lambda i, s: (0, 0, s[2] * 8, 0),
    )
    out = jax.ShapeDtypeStruct((levels, count, slab, LANE), jnp.float32)
    whole = pl.BlockSpec((levels, count, slab, LANE), lambda i, s: (0, 0, 0, 0))
    return pl.pallas_call(
        functools.partial(filter_kernel, n),
        grid_spec=pltpu.PrefetchScalarGridSpec(
            num_scalar_prefetch=1,
            grid=(1,),
            in_specs=[pl.BlockSpec((rows, waves), lambda i, s: (0, 0))] * n
            + [
                pl.BlockSpec(above.shape, lambda i, s: (0, 0)),
                pl.BlockSpec(limits.shape, lambda i, s: (0, 0)),
                pl.BlockSpec((1, waves, width), lambda i, s: (s[1], 0, 0)),
                pl.BlockSpec((1, waves, width), lambda i, s: (s[1], 0, 0)),
            ]
            + [window] * 5,
            out_specs=[whole] * 5 + [pl.BlockSpec((count, slab, LANE), lambda i, s: (0, 0, 0))],
            scratch_shapes=[
                pltpu.VMEM((n, rows, waves), jnp.float32),
                pltpu.VMEM((3 * POLAR + 12, waves), jnp.float32),
                pltpu.VMEM((BAND, waves), jnp.float32),
            ],
        ),
        out_shape=[out] * 5 + [jax.ShapeDtypeStruct((count, slab, LANE), jnp.float32)],
        cost_estimate=cost(12 * levels * 256 * waves * width, 40 * levels * count * slab * LANE),
        compiler_params=params(),
        name="filtered_band",
    )(scalars, *pieces, above, limits, basis, slope, *fields)


def slab_kernel(fields, group, rows, has_base, s, *refs):
    (tr, h0, u0, v0, u1, v1, east, west, rim) = refs[:9]
    refs = refs[11:] if has_base else refs[9:]
    tr_out, h_out, early, late, first_h, t0, t1 = refs
    level, part = pl.program_id(0), pl.program_id(1)
    lane = lanes()
    count = h0.shape[1]
    cols = h_out.shape[2]
    last = cols - LANE * (count - 1)
    tiles = rows // 8

    @pl.when(part == 0)
    def _():
        def one(i, _):
            here = eight(i)
            in_e, in_w, in_n, in_s, new = inflows_at(
                h0, u0, v0, 8 * i + PAD - 8, count, ((0,), (0,)), lane
            )
            for c in range(count):
                inv = 1.0 / new[c]
                w = [x[c] * inv for x in (in_e, in_w, in_n, in_s)]
                for k in range(4):
                    early[k + 1, c, here, :] = w[k]
                early[0, c, here, :] = 1.0 - ((w[0] + w[1]) + (w[2] + w[3]))
                first_h[c, pl.ds(pl.multiple_of(8 * i, 8) + PAD - 8, 8), :] = new[c]
            return 0

        lax.fori_loop(0, tiles + 2, one, 0)

        def two(i, _):
            here = eight(i)
            in_e, in_w, in_n, in_s, new = inflows_at(
                first_h, u1, v1, 8 * i + PAD, count, ((), (0,)), lane
            )
            for c in range(count):
                inv = 1.0 / new[c]
                w = [x[c] * inv for x in (in_e, in_w, in_n, in_s)]
                for k in range(4):
                    late[k + 1, c, here, :] = w[k]
                late[0, c, here, :] = 1.0 - ((w[0] + w[1]) + (w[2] + w[3]))
                wide = min(LANE, cols - c * LANE)
                h_out[0, here, c * LANE : c * LANE + wide] = new[c][:, 0:wide]
            return 0

        lax.fori_loop(0, tiles, two, 0)

    def bring(i, _):
        here = eight(i)
        there = pl.ds(pl.multiple_of(8 * (i + s[4]), 8), 8)
        rim_rows = eight(i + s[3])
        e, w = east[rim_rows, :], west[rim_rows, :]
        for j in range(group):
            plane = fields * level + part * group + j
            for c in range(count - 1):
                t0[j, c, there, :] = tr[j, 0, here, c * LANE : (c + 1) * LANE]
            t0[j, count - 1, there, 0:last] = tr[j, 0, here, LANE * (count - 1) : cols]
            t0[j, count - 1, there, last:] = rim_lanes(e, w, plane, last, lane)[:, last:]
        return 0

    lax.fori_loop(0, tiles + 1, bring, 0)
    for ends in (True, False):

        @pl.when(s[5] == int(ends))
        def _():
            at = PAD + rows if ends else PAD - 2
            for j in range(group):
                for c in range(count):
                    t0[j, c, at : at + 2, :] = rim[0, part * group + j, :, c * LANE : (c + 1) * LANE]

    def advance(source, j, row, weights):
        mid = tiles_at(source, pl.ds(pl.multiple_of(row, 8), 8), count, (j,))
        up = tiles_at(source, pl.ds(row - 1, 8), count, (j,))
        down = tiles_at(source, pl.ds(row + 1, 8), count, (j,))
        right, left = from_east(mid, lane), from_west(mid, lane)
        return [
            weights[0][c] * mid[c]
            + weights[1][c] * right[c]
            + weights[2][c] * left[c]
            + weights[3][c] * up[c]
            + weights[4][c] * down[c]
            for c in range(count)
        ]

    def one(i, _):
        weights = [tiles_at(early, eight(i), count, (k,)) for k in range(5)]
        for j in range(group):
            new = advance(t0, j, 8 * i + PAD - 8, weights)
            for c in range(count):
                t1[j, c, pl.ds(pl.multiple_of(8 * i, 8) + PAD - 8, 8), :] = new[c]
        return 0

    lax.fori_loop(0, tiles + 2, one, 0)

    def two(i, _):
        here = eight(i)
        weights = [tiles_at(late, here, count, (k,)) for k in range(5)]
        for j in range(group):
            new = advance(t1, j, 8 * i + PAD, weights)
            for c in range(count):
                wide = min(LANE, cols - c * LANE)
                tr_out[j, 0, here, c * LANE : c * LANE + wide] = new[c][:, 0:wide]
        return 0

    lax.fori_loop(0, tiles, two, 0)


def tracer_slab(scalars, tracers, slabs, offsets, east, west, rim, rows, base, group, name):
    count, levels, height, cols = tracers.shape
    tiles = slabs[0].shape[1]
    slab = rows + 2 * PAD
    E = pl.Element

    def spec(moves):
        return pl.BlockSpec(
            (E(1), E(tiles), E(slab), E(LANE)), lambda l, g, s: (l, 0, s[2] * 8 if moves else 0, 0)
        )

    in_specs = [
        pl.BlockSpec((E(group), E(1), E(rows + 8), E(cols)), lambda l, g, s: (g * group, l, s[3] * 8, 0))
    ]
    in_specs += [spec(m) for m in offsets]
    in_specs += [pl.BlockSpec((height, LANE), lambda l, g, s: (0, 0))] * 2
    in_specs += [pl.BlockSpec((1,) + rim.shape[1:], lambda l, g, s: (l, 0, 0, 0))]
    operands = [tracers, *slabs, east, west, rim]
    aliases = {}
    if base is not None:
        in_specs += [pl.BlockSpec(memory_space=pl.ANY)] * 2
        operands += list(base)
        aliases = {len(operands) - 1: 0, len(operands): 1}
    return pl.pallas_call(
        functools.partial(slab_kernel, rim.shape[1], group, rows, base is not None),
        grid_spec=pltpu.PrefetchScalarGridSpec(
            num_scalar_prefetch=1,
            grid=(levels, count // group),
            in_specs=in_specs,
            out_specs=[
                pl.BlockSpec((E(group), E(1), E(rows), E(cols)), lambda l, g, s: (g * group, l, s[2] * 8, 0)),
                pl.BlockSpec((E(1), E(rows), E(cols)), lambda l, g, s: (l, s[2] * 8, 0)),
            ],
            scratch_shapes=[
                pltpu.VMEM((5, tiles, rows + 16, LANE), jnp.float32),
                pltpu.VMEM((5, tiles, rows, LANE), jnp.float32),
                pltpu.VMEM((tiles, slab, LANE), jnp.float32),
                pltpu.VMEM((group, tiles, slab, LANE), jnp.float32),
                pltpu.VMEM((group, tiles, slab, LANE), jnp.float32),
            ],
        ),
        out_shape=[
            jax.ShapeDtypeStruct(tracers.shape, jnp.float32),
            jax.ShapeDtypeStruct((levels, height, cols), jnp.float32),
        ],
        input_output_aliases=aliases,
        cost_estimate=cost(60 * count * levels * rows * cols, 8 * count * levels * rows * cols),
        compiler_params=params(),
        name=name,
    )(scalars, *operands)


def winds_kernel(rows, has_base, s, h, u, v, above, *refs):
    u_out, v_out, cum, press = refs[2:] if has_base else refs
    level = pl.program_id(0)
    lane = lanes()
    count, slab = h.shape[1:3]
    cols = u_out.shape[2]

    def column(i, _):
        here = eight(i)
        for c in range(count):
            before = jnp.where(level == 0, above[c, here, :], cum[c, here, :])
            now = h[0, c, here, :]
            press[c, here, :] = before + 0.5 * now
            cum[c, here, :] = before + now
        return 0

    lax.fori_loop(0, slab // 8, column, 0)

    def step(i, _):
        row = 8 * i + PAD
        mid = pl.ds(pl.multiple_of(row, 8), 8)
        p = tiles_at(press, mid, count)
        p_e, p_w = from_east(p, lane), from_west(p, lane)
        p_n, p_s = tiles_at(press, pl.ds(row - 1, 8), count), tiles_at(press, pl.ds(row + 1, 8), count)
        for c in range(count):
            wide = min(LANE, cols - c * LANE)
            part = slice(c * LANE, c * LANE + wide)
            east = u[0, c, mid, :] - GRADIENT_COEF * (p_e[c] - p_w[c])
            north = v[0, c, mid, :] - GRADIENT_COEF * (p_s[c] - p_n[c])
            u_out[0, eight(i), part] = east[:, 0:wide]
            v_out[0, eight(i), part] = north[:, 0:wide]
        return 0

    lax.fori_loop(0, rows // 8, step, 0)


def last_winds(scalars, h, u, v, above, moves, rows, height, cols, base, name):
    levels, tiles = h.shape[:2]
    slab = rows + 2 * PAD
    E = pl.Element
    spec = pl.BlockSpec(
        (E(1), E(tiles), E(slab), E(LANE)), lambda l, s: (l, 0, s[2] * 8 if moves else 0, 0)
    )
    flat = pl.BlockSpec((E(tiles), E(slab), E(LANE)), lambda l, s: (0, s[2] * 8 if moves else 0, 0))
    out_spec = pl.BlockSpec((E(1), E(rows), E(cols)), lambda l, s: (l, s[2] * 8, 0))
    out = jax.ShapeDtypeStruct((levels, height, cols), jnp.float32)
    in_specs, operands, aliases = [spec] * 3 + [flat], [h, u, v, above], {}
    if base is not None:
        in_specs += [pl.BlockSpec(memory_space=pl.ANY)] * 2
        operands += list(base)
        aliases = {5: 0, 6: 1}
    return pl.pallas_call(
        functools.partial(winds_kernel, rows, base is not None),
        grid_spec=pltpu.PrefetchScalarGridSpec(
            num_scalar_prefetch=1,
            grid=(levels,),
            in_specs=in_specs,
            out_specs=[out_spec] * 2,
            scratch_shapes=[pltpu.VMEM((tiles, slab, LANE), jnp.float32)] * 2,
        ),
        out_shape=[out, out],
        input_output_aliases=aliases,
        cost_estimate=cost(20 * levels * rows * cols, 24 * levels * rows * cols),
        compiler_params=params(),
        name=name,
    )(scalars, *operands)


def bases(n, cols):
    total = n * cols
    wave = np.arange(KMAX + 1)
    cell = np.arange(total).reshape(n, cols)
    angle = (cell[:, :, None] * wave % total) * (2.0 * math.pi / total)
    forward = np.concatenate([np.cos(angle), np.sin(angle)], 2)
    width = LANE * ((cols - 1) // LANE + 1)
    lane = np.arange(width)
    lane = np.where(lane < width - 2, lane, lane - width)
    cell = np.arange(n)[:, None] * cols + lane[None, :]
    angle = (cell[:, None, :] * wave[:, None] % total) * (2.0 * math.pi / total)
    inverse = np.concatenate([np.cos(angle), np.sin(angle)], 1)
    steep = 2.0 * np.sin(wave * (2.0 * math.pi / total))[:, None]
    slope = np.concatenate([-steep * np.sin(angle), steep * np.cos(angle)], 1)
    return [jnp.asarray(x.astype(np.float32)) for x in (forward, inverse, slope)]


def shards_tiled(tracers, thickness, zonal, meridional, cutoff):
    count, levels, rows, cols = tracers.shape
    n = lax.axis_size("lon")
    me = lax.axis_index("lon").astype(jnp.int32)
    north = (lax.axis_index("lat") == 0).astype(jnp.int32)
    inner = rows - BAND

    def pick(a, b):
        return jnp.where(north == 1, a, b).astype(jnp.int32)

    bandwise = jnp.stack([north, me, pick(0, inner // 8), jnp.int32(cols), jnp.int32(0), jnp.int32(0)])
    polar = jnp.stack(
        [north, me, pick(0, inner // 8), pick(0, inner // 8 - 1), pick(PAD // 8, PAD // 8 - 1), 1 - north]
    )
    middle = jnp.stack(
        [north, me, pick(BAND // 8, 0), pick(BAND // 8 - 1, 0), pick(PAD // 8 - 1, PAD // 8), north]
    )
    forward, inverse, slope = bases(n, cols)

    def along(value, d):
        return lax.ppermute(value, "lon", [(i, (i + d) % n) for i in range(n)])

    def to_lower(value):
        return lax.ppermute(value, "lev", [(0, 1)])

    sent = band_rows(bandwise, zonal, meridional, thickness, n)
    pieces = [sent[0]] + [along(sent[d], d) for d in range(1, n)]
    west_cols, east_cols = pack_columns(tracers, thickness, zonal, meridional)
    east, west = along(west_cols, n - 1), along(east_cols, 1)
    pole, facing = edge_rows(bandwise, tracers, thickness, zonal, meridional, east, west)
    pole = along(pole, n // 2)
    facing = lax.ppermute(facing, "lat", [(0, 1), (1, 0)])

    own = spectra(bandwise, pieces, forward)
    pieces = [own] + [along(own, d) for d in range(1, n)]
    above_band = to_lower(sum(p[2 * POLAR :] for p in pieces))

    h0, u0, v0, column = extend_fields(bandwise, thickness, zonal, meridional, east, west, pole, facing)
    u1, v1, h1, column = first_substep(h0, u0, v0, to_lower(column))
    tr, h2 = tracer_slab(
        middle, tracers, (h0, u0, v0, u1, v1), (True,) * 5, east, west, facing, inner, None, 5, "tracers_inner"
    )
    winds = last_winds(middle, h1, u1, v1, to_lower(column), True, inner, rows, cols, None, "winds_inner")

    limits = jnp.where(north == 1, cutoff[0], cutoff[1])
    limits = jnp.broadcast_to(jnp.pad(limits, (0, BAND - POLAR))[:, None], (BAND, LANE))
    u0b, v0b, u1b, v1b, h1b, column = filtered_band(
        bandwise, pieces, above_band, limits, inverse, slope, (h0, u0, v0, u1, v1)
    )
    above = to_lower(column)
    tr, h2 = tracer_slab(
        polar, tracers, (h0, u0b, v0b, u1b, v1b), (True,) + (False,) * 4, east, west, pole, BAND, (tr, h2), 10,
        "tracers_polar",
    )
    u2, v2 = last_winds(polar, h1b, u1b, v1b, above, False, BAND, rows, cols, winds, "winds_polar")
    return (tr, h2, u2, v2)


def tiles_fit(mesh, tracers):
    count, levels, rows, cols = tracers.shape
    rows, cols = rows // mesh.shape["lat"], cols // mesh.shape["lon"]
    count, levels = count // mesh.shape["member"], levels // mesh.shape["lev"]
    last = (cols - 1) % LANE + 1
    return (
        mesh.shape["lat"] == 2
        and mesh.shape["lev"] == 2
        and levels == mesh.shape["lon"]
        and mesh.shape["lon"] % 2 == 0
        and rows % 8 == 0
        and rows >= 2 * BAND + 8
        and last + 4 <= LANE
        and last >= 2
        and cols > LANE
        and 2 * (count + 3) * levels <= LANE
        and count % 5 == 0
    )


def solution(mesh):
    placed = (
        P("member", "lev", "lat", "lon"),
        P(("member", "lev"), "lat", "lon"),
        P(("member", "lev"), "lat", "lon"),
        P(("member", "lev"), "lat", "lon"),
        P(),
    )
    outs = (
        P("member", "lev", "lat", "lon"),
        P(("member", "lev"), "lat", "lon"),
        P(("member", "lev"), "lat", "lon"),
        P(("member", "lev"), "lat", "lon"),
    )

    def program(*args):
        part = shards_tiled if tiles_fit(mesh, args[0]) else shards
        return jax.shard_map(part, mesh=mesh, in_specs=placed, out_specs=outs, check_vma=False)(*args)

    return program
```

```python
import functools
import math

import jax
import jax.numpy as jnp
import numpy as np
from jax import lax
from jax.experimental import pallas as pl
from jax.experimental.pallas import tpu as pltpu
from jax.sharding import PartitionSpec as P

NSUB = 2
POLAR = 60
KMAX = 191


COURANT_CAP = 0.15
GRADIENT_COEF = 0.1


def extended_2(block, sides, width):
    for axis, dim in sides:
        count = lax.axis_size(axis)
        forward = [(i, i + 1) for i in range(count - 1)]
        forward.append((count - 1, 0))
        backward = [(target, source) for source, target in forward]
        low = lax.ppermute(
            lax.slice_in_dim(block, block.shape[dim] - width, None, axis=dim), axis, forward
        )
        high = lax.ppermute(lax.slice_in_dim(block, 0, width, axis=dim), axis, backward)
        block = jnp.concatenate([low, block, high], axis=dim)
    return block


def shifted(block, axis, distance):
    devices = range(lax.axis_size(axis))
    route = [((i - distance) % len(devices), i) for i in devices]
    return lax.ppermute(block, axis, route)


def entering(value, axis, join, neutral):
    count, mine = (lax.axis_size(axis), lax.axis_index(axis))
    pieces = lax.all_gather(value, axis)
    running = jnp.full_like(value, 0) + jnp.asarray(neutral, value.dtype)

    def step(position, running):
        longer = join(running, pieces[position])
        return jnp.where(position < mine, longer, running)

    return lax.fori_loop(0, count - 1, step, running)


def advance_level(extended, pressure):
    tracer_count = extended.shape[0] - 3
    thick = extended[tracer_count]
    east_wind = extended[tracer_count + 1]
    north_wind = extended[tracer_count + 2]
    masses = jnp.concatenate([thick[None], extended[:tracer_count] * thick[None]], 0)
    east_courant = COURANT_CAP * jnp.tanh(0.5 * (east_wind[1:-1, :-1] + east_wind[1:-1, 1:]))
    east_flux = (
        jnp.maximum(east_courant, 0.0) * masses[:, 1:-1, :-1]
        + jnp.minimum(east_courant, 0.0) * masses[:, 1:-1, 1:]
    )
    south_courant = COURANT_CAP * jnp.tanh(0.5 * (north_wind[:-1, 1:-1] + north_wind[1:, 1:-1]))
    south_flux = (
        jnp.maximum(south_courant, 0.0) * masses[:, :-1, 1:-1]
        + jnp.minimum(south_courant, 0.0) * masses[:, 1:, 1:-1]
    )
    updated = (
        masses[:, 1:-1, 1:-1]
        - (east_flux[:, :, 1:] - east_flux[:, :, :-1])
        - (south_flux[:, 1:] - south_flux[:, :-1])
    )
    new_thick = updated[0]
    new_mixing = updated[1:] / new_thick[None]
    new_east = east_wind[1:-1, 1:-1] - GRADIENT_COEF * (pressure[1:-1, 2:] - pressure[1:-1, :-2])
    new_north = north_wind[1:-1, 1:-1] - GRADIENT_COEF * (pressure[2:, 1:-1] - pressure[:-2, 1:-1])
    return (new_mixing, new_thick, new_east, new_north)


def wave_basis(anchor, length, lon_total):
    cells = anchor + jnp.arange(length, dtype=jnp.int32)
    waves = jnp.arange(KMAX + 1, dtype=jnp.int32)
    phase = (cells[:, None] * waves[None, :] % lon_total).astype(jnp.float32) * (
        2.0 * math.pi / lon_total
    )
    return jnp.concatenate([jnp.cos(phase), jnp.sin(phase)], 1)


def wave_weights(limits, lon_total):
    waves = jnp.arange(KMAX + 1, dtype=jnp.int32)
    scaled = jnp.where(waves == 0, 1.0, 2.0).astype(jnp.float32) / lon_total
    kept = jnp.where(waves[None, :] <= limits[:, None], scaled[None, :], 0.0)
    return jnp.concatenate([kept, kept], 1)


def smooth_winds(zonal, meridional, cutoff, is_north, is_south):
    level_count, row_count, col_count = zonal.shape
    lon_count = lax.axis_size("lon")
    lon_total = col_count * lon_count
    north_rows = jnp.stack([zonal[:, :POLAR], meridional[:, :POLAR]], 0)
    south_rows = jnp.stack([zonal[:, row_count - POLAR :], meridional[:, row_count - POLAR :]], 0)
    selected = jnp.where(is_north, north_rows, south_rows).reshape(-1, col_count)
    limits = jnp.tile(jnp.where(is_north, cutoff[0], cutoff[1]), 2 * level_count)
    fragment = lax.all_gather(selected, "lon", axis=1, tiled=True)
    basis = wave_basis(jnp.int32(0), fragment.shape[1], lon_total)
    spectrum = jnp.dot(
        fragment, basis, precision=lax.Precision.HIGHEST, preferred_element_type=jnp.float32
    )
    own_basis = wave_basis(lax.axis_index("lon") * col_count, col_count, lon_total)
    filtered = jnp.dot(
        spectrum * wave_weights(limits, lon_total),
        own_basis.T,
        precision=lax.Precision.HIGHEST,
        preferred_element_type=jnp.float32,
    )
    filtered = filtered.reshape(2, level_count, POLAR, col_count)
    row_start = jnp.where(is_north, 0, row_count - POLAR).astype(jnp.int32)
    polar_band = jnp.logical_or(is_north, is_south)
    new_zonal = lax.dynamic_update_slice_in_dim(zonal, filtered[0], row_start, 1)
    new_merid = lax.dynamic_update_slice_in_dim(meridional, filtered[1], row_start, 1)
    return (jnp.where(polar_band, new_zonal, zonal), jnp.where(polar_band, new_merid, meridional))


def shards(tracers, thickness, zonal, meridional, cutoff):
    tracer_count = tracers.shape[0]
    lat_index = lax.axis_index("lat")
    is_north = lat_index == 0
    is_south = lat_index == lax.axis_size("lat") - 1
    lon_count = lax.axis_size("lon")
    flip_sign = jnp.concatenate(
        [jnp.ones((tracer_count + 1,), jnp.float32), -jnp.ones((2,), jnp.float32)]
    )[:, None, None]
    advance_all = jax.vmap(advance_level, in_axes=(1, 0), out_axes=(1, 0, 0, 0))
    for substep in range(NSUB):
        zonal, meridional = smooth_winds(zonal, meridional, cutoff, is_north, is_south)
        state = jnp.concatenate([tracers, thickness[None], zonal[None], meridional[None]], 0)
        extended = extended_2(state, (("lat", 2), ("lon", 3)), 1)
        edges = jnp.stack([state[:, :, 0], state[:, :, -1]], 2)
        opposite = shifted(edges, "lon", lon_count // 2)
        north_rim = jnp.where(is_north, opposite[:, :, 0] * flip_sign, extended[:, :, 0, 1:-1])
        south_rim = jnp.where(is_south, opposite[:, :, 1] * flip_sign, extended[:, :, -1, 1:-1])
        extended = extended.at[:, :, 0, 1:-1].set(north_rim)
        extended = extended.at[:, :, -1, 1:-1].set(south_rim)
        thick_ext = extended[tracer_count]
        column_above = entering(
            jnp.sum(thick_ext, 0),
            "lev",
            lambda earlier, later: earlier + later,
            jnp.zeros(thick_ext.shape[1:], jnp.float32),
        )
        pressure = jnp.cumsum(thick_ext, axis=0) - 0.5 * thick_ext + column_above[None]
        tracers, thickness, zonal, meridional = advance_all(extended, pressure)
    return (tracers, thickness, zonal, meridional)


LANE = 128
UNROLL = dict(step=8, add=8, column=8, bring=8, one=8, two=8)
PAD = 16
BAND = 64


def cost(flops, moved):
    return pl.CostEstimate(flops=int(flops), bytes_accessed=int(moved), transcendentals=0)


def params(mib=56):
    return pltpu.CompilerParams(vmem_limit_bytes=mib * 1024 * 1024)


def lanes():
    return lax.broadcasted_iota(jnp.int32, (8, LANE), 1)


def at_row(row):
    return pl.ds(row if isinstance(row, int) else pl.multiple_of(row, 8), 8)


def eight(index):
    return at_row(8 * index)


def from_east(tiles, lane):
    turned = [pltpu.roll(t, LANE - 1, 1) for t in tiles]
    n = len(tiles)
    return [jnp.where(lane < LANE - 1, turned[c], turned[(c + 1) % n]) for c in range(n)]


def from_west(tiles, lane):
    turned = [pltpu.roll(t, 1, 1) for t in tiles]
    n = len(tiles)
    return [jnp.where(lane > 0, turned[c], turned[(c - 1) % n]) for c in range(n)]


def courant(a, b):
    return COURANT_CAP * jnp.tanh(0.5 * (a + b))


def rim_lanes(east, west, plane, last, lane):
    to_east = lax.rem(last + LANE - 2 * plane, LANE)
    to_west = lax.rem(2 * LANE - 2 - 2 * plane, LANE)
    return jnp.where(lane < last + 2, pltpu.roll(east, to_east, 1), pltpu.roll(west, to_west, 1))


def inflows(h, u, v, h_n, h_s, v_n, v_s, lane):
    count = range(len(h))
    u_e, h_e = from_east(u, lane), from_east(h, lane)
    c_e = [courant(u[c], u_e[c]) for c in count]
    out_e = [jnp.maximum(c_e[c], 0.0) * h[c] for c in count]
    in_e = [jnp.maximum(-c_e[c], 0.0) * h_e[c] for c in count]
    in_w, out_w = from_west(out_e, lane), from_west(in_e, lane)
    c_s = [courant(v[c], v_s[c]) for c in count]
    c_n = [courant(v_n[c], v[c]) for c in count]
    in_s = [jnp.maximum(-c_s[c], 0.0) * h_s[c] for c in count]
    out_s = [jnp.maximum(c_s[c], 0.0) * h[c] for c in count]
    in_n = [jnp.maximum(c_n[c], 0.0) * h_n[c] for c in count]
    out_n = [jnp.maximum(-c_n[c], 0.0) * h[c] for c in count]
    new = [
        h[c] - (out_e[c] - in_e[c]) + (in_w[c] - out_w[c]) - (out_s[c] - in_s[c]) + (in_n[c] - out_n[c])
        for c in count
    ]
    return in_e, in_w, in_n, in_s, new


def sweep(first, end, body, depth):
    whole = (end - first) // depth

    def step(k, _):
        for j in range(depth):
            body(first + k * depth + j)
        return 0

    lax.fori_loop(0, whole, step, 0)
    for i in range(first + whole * depth, end):
        body(i)


def tiles_at(ref, base, count, lead=()):
    return [ref[lead + (c, base, slice(None))] for c in range(count)]


def inflows_at(h, u, v, row, count, lead, lane):
    mid = at_row(row)
    up, down = pl.ds(row - 1, 8), pl.ds(row + 1, 8)
    hl, vl = lead
    return inflows(
        tiles_at(h, mid, count, hl),
        tiles_at(u, mid, count, vl),
        tiles_at(v, mid, count, vl),
        tiles_at(h, up, count, hl),
        tiles_at(h, down, count, hl),
        tiles_at(v, up, count, vl),
        tiles_at(v, down, count, vl),
        lane,
    )


def band_kernel(n, s, *refs):
    ins, outs = refs[: 3 * n], refs[3 * n :]
    for north in (True, False):

        @pl.when(s[0] == int(north))
        def _():
            lo = 0 if north else BAND - POLAR
            for d in range(n):
                u, v, h = ins[3 * d : 3 * d + 3]
                outs[d][0:POLAR, :] = u[0, lo : lo + POLAR, :]
                outs[d][POLAR : 2 * POLAR, :] = v[0, lo : lo + POLAR, :]
                first = 0 if north else BAND - POLAR - 1
                outs[d][2 * POLAR : 3 * POLAR + 1, :] = h[0, first : first + POLAR + 1, :]
                outs[d][3 * POLAR + 1 :, :] = jnp.zeros((3, h.shape[2]), jnp.float32)


def band_rows(scalars, u, v, h, n):
    levels, _, cols = u.shape

    def spec(d):
        return pl.BlockSpec(
            (pl.Element(1), pl.Element(BAND), pl.Element(cols)),
            lambda i, s: (lax.rem(s[1] + d, n), s[2] * 8, 0),
        )

    rows = 3 * POLAR + 4
    return pl.pallas_call(
        functools.partial(band_kernel, n),
        grid_spec=pltpu.PrefetchScalarGridSpec(
            num_scalar_prefetch=1,
            grid=(1,),
            in_specs=[spec(d) for d in range(n) for _ in range(3)],
            out_specs=[pl.BlockSpec((rows, cols), lambda i, s: (0, 0))] * n,
        ),
        out_shape=[jax.ShapeDtypeStruct((rows, cols), jnp.float32)] * n,
        cost_estimate=cost(1e6, 8 * n * rows * cols),
        compiler_params=params(),
        name="band_rows",
    )(scalars, *([u, v, h] * n))


def spectrum_kernel(n, s, *refs):
    total = None
    for d in range(n):
        part = jnp.dot(
            refs[d][...],
            refs[n + d][0],
            precision=lax.Precision.HIGHEST,
            preferred_element_type=jnp.float32,
        )
        total = part if total is None else total + part
    refs[2 * n][...] = total


def spectra(scalars, pieces, basis):
    n = len(pieces)
    rows, cols = pieces[0].shape
    waves = basis.shape[2]

    def spec(d):
        return pl.BlockSpec((1, cols, waves), lambda i, s: (lax.rem(s[1] + n - d, n), 0, 0))

    return pl.pallas_call(
        functools.partial(spectrum_kernel, n),
        grid_spec=pltpu.PrefetchScalarGridSpec(
            num_scalar_prefetch=1,
            grid=(1,),
            in_specs=[pl.BlockSpec((rows, cols), lambda i, s: (0, 0))] * n + [spec(d) for d in range(n)],
            out_specs=pl.BlockSpec((rows, waves), lambda i, s: (0, 0)),
        ),
        out_shape=jax.ShapeDtypeStruct((rows, waves), jnp.float32),
        cost_estimate=cost(12 * n * rows * cols * waves, 4 * n * cols * (rows + waves)),
        compiler_params=params(),
        name="spectra",
    )(scalars, *pieces, *([basis] * n))


def pack_kernel(fields, last, t_lo, t_hi, h_lo, h_hi, u_lo, u_hi, v_lo, v_hi, west, east):
    level = pl.program_id(0)
    lane = lanes()
    lows = [(t_lo, (f, 0)) for f in range(fields - 3)] + [(h_lo, (0,)), (u_lo, (0,)), (v_lo, (0,))]
    highs = [(t_hi, (f, 0)) for f in range(fields - 3)] + [(h_hi, (0,)), (u_hi, (0,)), (v_hi, (0,))]
    begin = 2 * fields * level
    mine = jnp.logical_and(lane >= begin, lane < begin + 2 * fields)

    def step(i):
        rows = eight(i)
        got_w = got_e = jnp.zeros((8, LANE), jnp.float32)
        for f in range(fields):
            here = lane // 2 == f
            ref, lead = lows[f]
            tile = ref[lead + (rows, slice(None))]
            got_w = jnp.where(here, pltpu.roll(tile, 2 * f, 1) if f else tile, got_w)
            ref, lead = highs[f]
            tile = ref[lead + (rows, slice(None))]
            got_e = jnp.where(here, pltpu.roll(tile, (2 * f - last + 2) % LANE, 1), got_e)
        west[rows, :] = jnp.where(mine, pltpu.roll(got_w, begin, 1), west[rows, :])
        east[rows, :] = jnp.where(mine, pltpu.roll(got_e, begin, 1), east[rows, :])

    sweep(0, west.shape[0] // 8, step, UNROLL["step"])


def pack_columns(tracers, h, u, v):
    count, levels, rows, cols = tracers.shape
    high = (cols - 1) // LANE
    t_spec = [pl.BlockSpec((count, 1, rows, LANE), lambda l, c=c: (0, l, 0, c)) for c in (0, high)]
    f_spec = [pl.BlockSpec((1, rows, LANE), lambda l, c=c: (l, 0, c)) for c in (0, high)]
    out = jax.ShapeDtypeStruct((rows, LANE), jnp.float32)
    return pl.pallas_call(
        functools.partial(pack_kernel, count + 3, cols - LANE * high),
        grid=(levels,),
        in_specs=t_spec + f_spec * 3,
        out_specs=[pl.BlockSpec((rows, LANE), lambda l: (0, 0))] * 2,
        out_shape=[out, out],
        cost_estimate=cost(1e7, 8 * (count + 3) * levels * rows * LANE),
        compiler_params=params(),
        name="pack_columns",
    )(tracers, tracers, h, h, u, u, v, v)


def rows_kernel(fields, s, t_top, t_bot, h_top, h_bot, u_top, u_bot, v_top, v_bot,
                e_top, e_bot, w_top, w_bot, pole, facing, top, bot):
    level = pl.program_id(0)
    lane = lanes()
    cols = h_top.shape[2]
    tail = top.shape[1] - LANE
    last = cols - tail
    refs = [(t_top, t_bot, (f, 0)) for f in range(fields - 3)]
    refs += [(h_top, h_bot, (0,)), (u_top, u_bot, (0,)), (v_top, v_bot, (0,))]
    for f in range(fields):
        plane = fields * level + f
        a, b, lead = refs[f]
        top[:, 0:cols] = a[lead]
        bot[:, 0:cols] = b[lead]
        top[:, cols:] = rim_lanes(e_top[...], w_top[...], plane, last, lane)[:, last:]
        bot[:, cols:] = rim_lanes(e_bot[...], w_bot[...], plane, last, lane)[:, last:]
        flip = -1.0 if f == fields - 1 else 1.0

        @pl.when(s[0] == 1)
        def _():
            pole[0, f, 0:1, :] = flip * top[1:2, :]
            pole[0, f, 1:2, :] = flip * top[0:1, :]
            facing[0, f] = bot[6:8, :]

        @pl.when(s[0] == 0)
        def _():
            pole[0, f, 0:1, :] = flip * bot[7:8, :]
            pole[0, f, 1:2, :] = flip * bot[6:7, :]
            facing[0, f] = top[0:2, :]


def edge_rows(scalars, tracers, h, u, v, east, west):
    count, levels, rows, cols = tracers.shape
    fields = count + 3
    width = LANE * ((cols - 1) // LANE + 1)
    ends = (0, rows // 8 - 1)
    t_spec = [pl.BlockSpec((count, 1, 8, cols), lambda l, s, r=r: (0, l, r, 0)) for r in ends]
    f_spec = [pl.BlockSpec((1, 8, cols), lambda l, s, r=r: (l, r, 0)) for r in ends]
    c_spec = [pl.BlockSpec((8, LANE), lambda l, s, r=r: (r, 0)) for r in ends]
    out = jax.ShapeDtypeStruct((levels, fields, 2, width), jnp.float32)
    return pl.pallas_call(
        functools.partial(rows_kernel, fields),
        grid_spec=pltpu.PrefetchScalarGridSpec(
            num_scalar_prefetch=1,
            grid=(levels,),
            in_specs=t_spec + f_spec * 3 + c_spec * 2,
            out_specs=[pl.BlockSpec((1, fields, 2, width), lambda l, s: (l, 0, 0, 0))] * 2,
            scratch_shapes=[pltpu.VMEM((8, width), jnp.float32)] * 2,
        ),
        out_shape=[out, out],
        cost_estimate=cost(1e6, 100 * levels * fields * width),
        compiler_params=params(),
        name="edge_rows",
    )(scalars, tracers, tracers, h, h, u, u, v, v, east, east, west, west)


def extend_kernel(fields, s, h, u, v, east, west, pole, facing, h_out, u_out, v_out, total):
    level = pl.program_id(0)
    lane = lanes()
    rows, cols = h.shape[1:]
    count = h_out.shape[1]
    last = cols - LANE * (count - 1)
    for f, (ref, out) in enumerate(((h, h_out), (u, u_out), (v, v_out))):
        plane = fields * level + fields - 3 + f

        def step(i):
            here, there = eight(i), at_row(8 * i + PAD)
            for c in range(count - 1):
                out[0, c, there, :] = ref[0, here, c * LANE : (c + 1) * LANE]
            out[0, count - 1, there, 0:last] = ref[0, here, LANE * (count - 1) : cols]
            rim = rim_lanes(east[here, :], west[here, :], plane, last, lane)
            out[0, count - 1, there, last:] = rim[:, last:]

        sweep(0, rows // 8, step, UNROLL["step"])
        for c in range(count):
            part = slice(c * LANE, (c + 1) * LANE)
            a = pole[0, fields - 3 + f, :, part]
            b = facing[0, fields - 3 + f, :, part]
            out[0, c, PAD - 2 : PAD, :] = jnp.where(s[0] == 1, a, b)
            out[0, c, PAD + rows : PAD + rows + 2, :] = jnp.where(s[0] == 1, b, a)

    def add(i):
        here = eight(i)
        for c in range(count):
            now = h_out[0, c, here, :]
            total[c, here, :] = jnp.where(level == 0, now, total[c, here, :] + now)

    sweep(0, h_out.shape[2] // 8, add, UNROLL["add"])


def extend_fields(scalars, h, u, v, east, west, pole, facing):
    levels, rows, cols = h.shape
    fields = pole.shape[1]
    count = (cols - 1) // LANE + 1
    tall = rows + 2 * PAD
    f_spec = pl.BlockSpec((1, rows, cols), lambda l, s: (l, 0, 0))
    c_spec = pl.BlockSpec((rows, LANE), lambda l, s: (0, 0))
    r_spec = pl.BlockSpec((1, fields, 2, count * LANE), lambda l, s: (l, 0, 0, 0))
    out = jax.ShapeDtypeStruct((levels, count, tall, LANE), jnp.float32)
    return pl.pallas_call(
        functools.partial(extend_kernel, fields),
        grid_spec=pltpu.PrefetchScalarGridSpec(
            num_scalar_prefetch=1,
            grid=(levels,),
            in_specs=[f_spec] * 3 + [c_spec] * 2 + [r_spec] * 2,
            out_specs=[pl.BlockSpec((1, count, tall, LANE), lambda l, s: (l, 0, 0, 0))] * 3
            + [pl.BlockSpec((count, tall, LANE), lambda l, s: (0, 0, 0))],
        ),
        out_shape=[out] * 3 + [jax.ShapeDtypeStruct((count, tall, LANE), jnp.float32)],
        cost_estimate=cost(1e6, 28 * levels * tall * count * LANE),
        compiler_params=params(),
        name="extend_fields",
    )(scalars, h, u, v, east, west, pole, facing)


def first_kernel(h, u, v, above, u_out, v_out, h_out, total, cum, press):
    level = pl.program_id(0)
    lane = lanes()
    count, tall = h.shape[1:3]

    def column(i):
        here = eight(i)
        for c in range(count):
            before = jnp.where(level == 0, above[c, here, :], cum[c, here, :])
            now = h[0, c, here, :]
            press[c, here, :] = before + 0.5 * now
            cum[c, here, :] = before + now

    sweep(0, tall // 8, column, UNROLL["column"])

    def step(i):
        row = 8 * i
        here = eight(i)
        p = tiles_at(press, here, count)
        p_e, p_w = from_east(p, lane), from_west(p, lane)
        p_n, p_s = tiles_at(press, pl.ds(row - 1, 8), count), tiles_at(press, pl.ds(row + 1, 8), count)
        new = inflows_at(h, u, v, row, count, ((0,), (0,)), lane)[4]
        for c in range(count):
            u_out[0, c, here, :] = u[0, c, here, :] - GRADIENT_COEF * (p_e[c] - p_w[c])
            v_out[0, c, here, :] = v[0, c, here, :] - GRADIENT_COEF * (p_s[c] - p_n[c])
            h_out[0, c, here, :] = new[c]
            total[c, here, :] = jnp.where(level == 0, new[c], total[c, here, :] + new[c])

    sweep(1, tall // 8 - 1, step, UNROLL["step"])


def first_substep(h, u, v, above):
    levels, count, tall, _ = h.shape
    spec = pl.BlockSpec((1, count, tall, LANE), lambda l: (l, 0, 0, 0))
    flat = pl.BlockSpec((count, tall, LANE), lambda l: (0, 0, 0))
    out = jax.ShapeDtypeStruct(h.shape, jnp.float32)
    return pl.pallas_call(
        first_kernel,
        grid=(levels,),
        in_specs=[spec] * 3 + [flat],
        out_specs=[spec] * 3 + [flat],
        out_shape=[out] * 3 + [jax.ShapeDtypeStruct((count, tall, LANE), jnp.float32)],
        scratch_shapes=[pltpu.VMEM((count, tall, LANE), jnp.float32)] * 2,
        cost_estimate=cost(80 * h.size, 30 * h.size),
        compiler_params=params(),
        name="first_substep",
    )(h, u, v, above)


def filter_kernel(n, s, *refs):
    pieces = refs[:n]
    above, limits, basis, slope, h0, u0, v0, u1, v1 = refs[n : n + 9]
    u0_out, v0_out, u1_out, v1_out, h1_out, total = refs[n + 9 : n + 15]
    held, lhs, rhs = refs[n + 15 :]
    levels, count, slab = u0.shape[:3]
    waves = basis.shape[1]
    for d in range(n):
        held[lax.rem(s[1] + n - d, n)] = pieces[d][...]
    for raw, out in ((u0, u0_out), (v0, v0_out), (u1, u1_out), (v1, v1_out)):
        out[...] = raw[...]
    half = waves // 2
    wave = lax.broadcasted_iota(jnp.int32, (POLAR, waves), 1)
    wave = jnp.where(wave < half, wave, wave - half)
    scale = jnp.where(wave == 0, 1.0, 2.0) / (n * s[3]).astype(jnp.float32)
    keep = jnp.where(wave <= limits[0:POLAR, 0:1], scale, 0.0)
    turn = jnp.where(lax.rem(wave[0:2], 2) == 0, 1.0, -1.0)
    one = turn[0:1]
    for north in (True, False):

        @pl.when(s[0] == int(north))
        def _():
            first = PAD if north else PAD + BAND - POLAR
            rim = PAD - 2 if north else PAD + BAND

            def level_step(l, cum):
                u = held[l, 0:POLAR, :] * keep
                v = held[l, POLAR : 2 * POLAR, :] * keep
                thick = held[l, 2 * POLAR : 3 * POLAR + 1, :]
                p = cum + 0.5 * thick
                if north:
                    before = jnp.concatenate([one * p[0:1], p[0 : POLAR - 1]], 0)
                    diff = (p[1:] - before) * keep
                    rhs[0:POLAR, :] = p[0:POLAR] * keep
                else:
                    after = jnp.concatenate([p[2:], one * p[POLAR:]], 0)
                    diff = (after - p[0:POLAR]) * keep
                    rhs[0:POLAR, :] = p[1:] * keep
                w = v - GRADIENT_COEF * diff
                lhs[0:POLAR, :] = u
                lhs[POLAR : 2 * POLAR, :] = v
                lhs[2 * POLAR : 3 * POLAR, :] = w
                for k, (x, sign) in enumerate(((u, 1.0), (v, -1.0), (w, -1.0))):
                    a, b = (x[1:2], x[0:1]) if north else (x[POLAR - 1 :], x[POLAR - 2 : POLAR - 1])
                    at = 3 * POLAR + 2 * k
                    lhs[at : at + 1, :] = sign * one * a
                    lhs[at + 1 : at + 2, :] = sign * one * b
                back = jnp.dot(
                    lhs[...], basis[0], precision=lax.Precision.HIGHEST, preferred_element_type=jnp.float32
                )
                grad = jnp.dot(
                    rhs[...], slope[0], precision=lax.Precision.HIGHEST, preferred_element_type=jnp.float32
                )
                zonal = back[0:POLAR]
                later = zonal - GRADIENT_COEF * grad[0:POLAR]
                for c in range(count):
                    part = slice(c * LANE, (c + 1) * LANE)
                    u0_out[l, c, first : first + POLAR, :] = zonal[:, part]
                    v0_out[l, c, first : first + POLAR, :] = back[POLAR : 2 * POLAR, part]
                    u1_out[l, c, first : first + POLAR, :] = later[:, part]
                    v1_out[l, c, first : first + POLAR, :] = back[2 * POLAR : 3 * POLAR, part]
                    u0_out[l, c, rim : rim + 2, :] = back[3 * POLAR : 3 * POLAR + 2, part]
                    v0_out[l, c, rim : rim + 2, :] = back[3 * POLAR + 2 : 3 * POLAR + 4, part]
                    v1_out[l, c, rim : rim + 2, :] = back[3 * POLAR + 4 : 3 * POLAR + 6, part]
                return cum + thick

            lax.fori_loop(0, levels, level_step, above[0 : POLAR + 1, :])

    lane = lanes()

    def step(k):
        l, i = k // (slab // 8 - 2), lax.rem(k, slab // 8 - 2) + 1
        here = eight(i)
        new = inflows_at(h0, u0_out, v0_out, 8 * i, count, ((l,), (l,)), lane)[4]
        for c in range(count):
            h1_out[l, c, here, :] = new[c]
            total[c, here, :] = jnp.where(l == 0, new[c], total[c, here, :] + new[c])

    sweep(0, levels * (slab // 8 - 2), step, UNROLL["step"])


def filtered_band(scalars, pieces, above, limits, basis, slope, fields):
    n = len(pieces)
    rows, waves = pieces[0].shape
    width = basis.shape[2]
    levels, count = fields[0].shape[:2]
    slab = BAND + 2 * PAD
    window = pl.BlockSpec(
        (pl.Element(levels), pl.Element(count), pl.Element(slab), pl.Element(LANE)),
        lambda i, s: (0, 0, s[2] * 8, 0),
    )
    out = jax.ShapeDtypeStruct((levels, count, slab, LANE), jnp.float32)
    whole = pl.BlockSpec((levels, count, slab, LANE), lambda i, s: (0, 0, 0, 0))
    return pl.pallas_call(
        functools.partial(filter_kernel, n),
        grid_spec=pltpu.PrefetchScalarGridSpec(
            num_scalar_prefetch=1,
            grid=(1,),
            in_specs=[pl.BlockSpec((rows, waves), lambda i, s: (0, 0))] * n
            + [
                pl.BlockSpec(above.shape, lambda i, s: (0, 0)),
                pl.BlockSpec(limits.shape, lambda i, s: (0, 0)),
                pl.BlockSpec((1, waves, width), lambda i, s: (s[1], 0, 0)),
                pl.BlockSpec((1, waves, width), lambda i, s: (s[1], 0, 0)),
            ]
            + [window] * 5,
            out_specs=[whole] * 5 + [pl.BlockSpec((count, slab, LANE), lambda i, s: (0, 0, 0))],
            scratch_shapes=[
                pltpu.VMEM((n, rows, waves), jnp.float32),
                pltpu.VMEM((3 * POLAR + 12, waves), jnp.float32),
                pltpu.VMEM((BAND, waves), jnp.float32),
            ],
        ),
        out_shape=[out] * 5 + [jax.ShapeDtypeStruct((count, slab, LANE), jnp.float32)],
        cost_estimate=cost(12 * levels * 256 * waves * width, 40 * levels * count * slab * LANE),
        compiler_params=params(),
        name="filtered_band",
    )(scalars, *pieces, above, limits, basis, slope, *fields)


def slab_kernel(fields, group, rows, has_base, s, *refs):
    (tr, h0, u0, v0, u1, v1, east, west, rim) = refs[:9]
    refs = refs[11:] if has_base else refs[9:]
    tr_out, h_out, early, late, first_h, t0, t1 = refs
    level, part = pl.program_id(0), pl.program_id(1)
    lane = lanes()
    count = h0.shape[1]
    cols = h_out.shape[2]
    last = cols - LANE * (count - 1)
    tiles = rows // 8

    @pl.when(part == 0)
    def _():
        def one(i):
            here = eight(i)
            in_e, in_w, in_n, in_s, new = inflows_at(
                h0, u0, v0, 8 * i + PAD - 8, count, ((0,), (0,)), lane
            )
            for c in range(count):
                inv = 1.0 / new[c]
                w = [x[c] * inv for x in (in_e, in_w, in_n, in_s)]
                for k in range(4):
                    early[k + 1, c, here, :] = w[k]
                early[0, c, here, :] = 1.0 - ((w[0] + w[1]) + (w[2] + w[3]))
                first_h[c, at_row(8 * i + PAD - 8), :] = new[c]

        sweep(0, tiles + 2, one, UNROLL["one"])

        def two(i):
            here = eight(i)
            in_e, in_w, in_n, in_s, new = inflows_at(
                first_h, u1, v1, 8 * i + PAD, count, ((), (0,)), lane
            )
            for c in range(count):
                inv = 1.0 / new[c]
                w = [x[c] * inv for x in (in_e, in_w, in_n, in_s)]
                for k in range(4):
                    late[k + 1, c, here, :] = w[k]
                late[0, c, here, :] = 1.0 - ((w[0] + w[1]) + (w[2] + w[3]))
                wide = min(LANE, cols - c * LANE)
                h_out[0, here, c * LANE : c * LANE + wide] = new[c][:, 0:wide]

        sweep(0, tiles, two, UNROLL["two"])

    def bring(i):
        here = eight(i)
        there = at_row(8 * (i + s[4]))
        rim_rows = eight(i + s[3])
        e, w = east[rim_rows, :], west[rim_rows, :]
        for j in range(group):
            plane = fields * level + part * group + j
            for c in range(count - 1):
                t0[j, c, there, :] = tr[j, 0, here, c * LANE : (c + 1) * LANE]
            t0[j, count - 1, there, 0:last] = tr[j, 0, here, LANE * (count - 1) : cols]
            t0[j, count - 1, there, last:] = rim_lanes(e, w, plane, last, lane)[:, last:]

    sweep(0, tiles + 1, bring, UNROLL["bring"])
    for ends in (True, False):

        @pl.when(s[5] == int(ends))
        def _():
            at = PAD + rows if ends else PAD - 2
            for j in range(group):
                for c in range(count):
                    t0[j, c, at : at + 2, :] = rim[0, part * group + j, :, c * LANE : (c + 1) * LANE]

    def advance(source, j, row, weights):
        mid = tiles_at(source, at_row(row), count, (j,))
        up = tiles_at(source, pl.ds(row - 1, 8), count, (j,))
        down = tiles_at(source, pl.ds(row + 1, 8), count, (j,))
        right, left = from_east(mid, lane), from_west(mid, lane)
        return [
            weights[0][c] * mid[c]
            + weights[1][c] * right[c]
            + weights[2][c] * left[c]
            + weights[3][c] * up[c]
            + weights[4][c] * down[c]
            for c in range(count)
        ]

    def one(i):
        weights = [tiles_at(early, eight(i), count, (k,)) for k in range(5)]
        for j in range(group):
            new = advance(t0, j, 8 * i + PAD - 8, weights)
            for c in range(count):
                t1[j, c, at_row(8 * i + PAD - 8), :] = new[c]

    sweep(0, tiles + 2, one, UNROLL["one"])

    def two(i):
        here = eight(i)
        weights = [tiles_at(late, here, count, (k,)) for k in range(5)]
        for j in range(group):
            new = advance(t1, j, 8 * i + PAD, weights)
            for c in range(count):
                wide = min(LANE, cols - c * LANE)
                tr_out[j, 0, here, c * LANE : c * LANE + wide] = new[c][:, 0:wide]

    sweep(0, tiles, two, UNROLL["two"])


def tracer_slab(scalars, tracers, slabs, offsets, east, west, rim, rows, base, group, name):
    count, levels, height, cols = tracers.shape
    tiles = slabs[0].shape[1]
    slab = rows + 2 * PAD
    E = pl.Element

    def spec(moves):
        return pl.BlockSpec(
            (E(1), E(tiles), E(slab), E(LANE)), lambda l, g, s: (l, 0, s[2] * 8 if moves else 0, 0)
        )

    in_specs = [
        pl.BlockSpec((E(group), E(1), E(rows + 8), E(cols)), lambda l, g, s: (g * group, l, s[3] * 8, 0))
    ]
    in_specs += [spec(m) for m in offsets]
    in_specs += [pl.BlockSpec((height, LANE), lambda l, g, s: (0, 0))] * 2
    in_specs += [pl.BlockSpec((1,) + rim.shape[1:], lambda l, g, s: (l, 0, 0, 0))]
    operands = [tracers, *slabs, east, west, rim]
    aliases = {}
    if base is not None:
        in_specs += [pl.BlockSpec(memory_space=pl.ANY)] * 2
        operands += list(base)
        aliases = {len(operands) - 1: 0, len(operands): 1}
    return pl.pallas_call(
        functools.partial(slab_kernel, rim.shape[1], group, rows, base is not None),
        grid_spec=pltpu.PrefetchScalarGridSpec(
            num_scalar_prefetch=1,
            grid=(levels, count // group),
            in_specs=in_specs,
            out_specs=[
                pl.BlockSpec((E(group), E(1), E(rows), E(cols)), lambda l, g, s: (g * group, l, s[2] * 8, 0)),
                pl.BlockSpec((E(1), E(rows), E(cols)), lambda l, g, s: (l, s[2] * 8, 0)),
            ],
            scratch_shapes=[
                pltpu.VMEM((5, tiles, rows + 16, LANE), jnp.float32),
                pltpu.VMEM((5, tiles, rows, LANE), jnp.float32),
                pltpu.VMEM((tiles, slab, LANE), jnp.float32),
                pltpu.VMEM((group, tiles, slab, LANE), jnp.float32),
                pltpu.VMEM((group, tiles, slab, LANE), jnp.float32),
            ],
        ),
        out_shape=[
            jax.ShapeDtypeStruct(tracers.shape, jnp.float32),
            jax.ShapeDtypeStruct((levels, height, cols), jnp.float32),
        ],
        input_output_aliases=aliases,
        cost_estimate=cost(60 * count * levels * rows * cols, 8 * count * levels * rows * cols),
        compiler_params=params(),
        name=name,
    )(scalars, *operands)


def winds_kernel(rows, has_base, s, h, u, v, above, *refs):
    u_out, v_out, cum, press = refs[2:] if has_base else refs
    level = pl.program_id(0)
    lane = lanes()
    count, slab = h.shape[1:3]
    cols = u_out.shape[2]

    def column(i):
        here = eight(i)
        for c in range(count):
            before = jnp.where(level == 0, above[c, here, :], cum[c, here, :])
            now = h[0, c, here, :]
            press[c, here, :] = before + 0.5 * now
            cum[c, here, :] = before + now

    sweep(0, slab // 8, column, UNROLL["column"])

    def step(i):
        row = 8 * i + PAD
        mid = at_row(row)
        p = tiles_at(press, mid, count)
        p_e, p_w = from_east(p, lane), from_west(p, lane)
        p_n, p_s = tiles_at(press, pl.ds(row - 1, 8), count), tiles_at(press, pl.ds(row + 1, 8), count)
        for c in range(count):
            wide = min(LANE, cols - c * LANE)
            part = slice(c * LANE, c * LANE + wide)
            east = u[0, c, mid, :] - GRADIENT_COEF * (p_e[c] - p_w[c])
            north = v[0, c, mid, :] - GRADIENT_COEF * (p_s[c] - p_n[c])
            u_out[0, eight(i), part] = east[:, 0:wide]
            v_out[0, eight(i), part] = north[:, 0:wide]

    sweep(0, rows // 8, step, UNROLL["step"])


def last_winds(scalars, h, u, v, above, moves, rows, height, cols, base, name):
    levels, tiles = h.shape[:2]
    slab = rows + 2 * PAD
    E = pl.Element
    spec = pl.BlockSpec(
        (E(1), E(tiles), E(slab), E(LANE)), lambda l, s: (l, 0, s[2] * 8 if moves else 0, 0)
    )
    flat = pl.BlockSpec((E(tiles), E(slab), E(LANE)), lambda l, s: (0, s[2] * 8 if moves else 0, 0))
    out_spec = pl.BlockSpec((E(1), E(rows), E(cols)), lambda l, s: (l, s[2] * 8, 0))
    out = jax.ShapeDtypeStruct((levels, height, cols), jnp.float32)
    in_specs, operands, aliases = [spec] * 3 + [flat], [h, u, v, above], {}
    if base is not None:
        in_specs += [pl.BlockSpec(memory_space=pl.ANY)] * 2
        operands += list(base)
        aliases = {5: 0, 6: 1}
    return pl.pallas_call(
        functools.partial(winds_kernel, rows, base is not None),
        grid_spec=pltpu.PrefetchScalarGridSpec(
            num_scalar_prefetch=1,
            grid=(levels,),
            in_specs=in_specs,
            out_specs=[out_spec] * 2,
            scratch_shapes=[pltpu.VMEM((tiles, slab, LANE), jnp.float32)] * 2,
        ),
        out_shape=[out, out],
        input_output_aliases=aliases,
        cost_estimate=cost(20 * levels * rows * cols, 24 * levels * rows * cols),
        compiler_params=params(),
        name=name,
    )(scalars, *operands)


def bases(n, cols):
    total = n * cols
    wave = np.arange(KMAX + 1)
    cell = np.arange(total).reshape(n, cols)
    angle = (cell[:, :, None] * wave % total) * (2.0 * math.pi / total)
    forward = np.concatenate([np.cos(angle), np.sin(angle)], 2)
    width = LANE * ((cols - 1) // LANE + 1)
    lane = np.arange(width)
    lane = np.where(lane < width - 2, lane, lane - width)
    cell = np.arange(n)[:, None] * cols + lane[None, :]
    angle = (cell[:, None, :] * wave[:, None] % total) * (2.0 * math.pi / total)
    inverse = np.concatenate([np.cos(angle), np.sin(angle)], 1)
    steep = 2.0 * np.sin(wave * (2.0 * math.pi / total))[:, None]
    slope = np.concatenate([-steep * np.sin(angle), steep * np.cos(angle)], 1)
    return [jnp.asarray(x.astype(np.float32)) for x in (forward, inverse, slope)]


def shards_tiled(tracers, thickness, zonal, meridional, cutoff):
    count, levels, rows, cols = tracers.shape
    n = lax.axis_size("lon")
    me = lax.axis_index("lon").astype(jnp.int32)
    north = (lax.axis_index("lat") == 0).astype(jnp.int32)
    inner = rows - BAND

    def pick(a, b):
        return jnp.where(north == 1, a, b).astype(jnp.int32)

    bandwise = jnp.stack([north, me, pick(0, inner // 8), jnp.int32(cols), jnp.int32(0), jnp.int32(0)])
    polar = jnp.stack(
        [north, me, pick(0, inner // 8), pick(0, inner // 8 - 1), pick(PAD // 8, PAD // 8 - 1), 1 - north]
    )
    middle = jnp.stack(
        [north, me, pick(BAND // 8, 0), pick(BAND // 8 - 1, 0), pick(PAD // 8 - 1, PAD // 8), north]
    )
    forward, inverse, slope = bases(n, cols)

    def along(value, d):
        return lax.ppermute(value, "lon", [(i, (i + d) % n) for i in range(n)])

    def to_lower(value):
        return lax.ppermute(value, "lev", [(0, 1)])

    sent = band_rows(bandwise, zonal, meridional, thickness, n)
    pieces = [sent[0]] + [along(sent[d], d) for d in range(1, n)]
    west_cols, east_cols = pack_columns(tracers, thickness, zonal, meridional)
    east, west = along(west_cols, n - 1), along(east_cols, 1)
    pole, facing = edge_rows(bandwise, tracers, thickness, zonal, meridional, east, west)
    pole = along(pole, n // 2)
    facing = lax.ppermute(facing, "lat", [(0, 1), (1, 0)])

    own = spectra(bandwise, pieces, forward)
    pieces = [own] + [along(own, d) for d in range(1, n)]
    above_band = to_lower(sum(p[2 * POLAR :] for p in pieces))

    h0, u0, v0, column = extend_fields(bandwise, thickness, zonal, meridional, east, west, pole, facing)
    u1, v1, h1, column = first_substep(h0, u0, v0, to_lower(column))
    tr, h2 = tracer_slab(
        middle, tracers, (h0, u0, v0, u1, v1), (True,) * 5, east, west, facing, inner, None, 5, "tracers_inner"
    )
    winds = last_winds(middle, h1, u1, v1, to_lower(column), True, inner, rows, cols, None, "winds_inner")

    limits = jnp.where(north == 1, cutoff[0], cutoff[1])
    limits = jnp.broadcast_to(jnp.pad(limits, (0, BAND - POLAR))[:, None], (BAND, LANE))
    u0b, v0b, u1b, v1b, h1b, column = filtered_band(
        bandwise, pieces, above_band, limits, inverse, slope, (h0, u0, v0, u1, v1)
    )
    above = to_lower(column)
    tr, h2 = tracer_slab(
        polar, tracers, (h0, u0b, v0b, u1b, v1b), (True,) + (False,) * 4, east, west, pole, BAND, (tr, h2), 10,
        "tracers_polar",
    )
    u2, v2 = last_winds(polar, h1b, u1b, v1b, above, False, BAND, rows, cols, winds, "winds_polar")
    return (tr, h2, u2, v2)


def tiles_fit(mesh, tracers):
    count, levels, rows, cols = tracers.shape
    rows, cols = rows // mesh.shape["lat"], cols // mesh.shape["lon"]
    count, levels = count // mesh.shape["member"], levels // mesh.shape["lev"]
    last = (cols - 1) % LANE + 1
    return (
        mesh.shape["lat"] == 2
        and mesh.shape["lev"] == 2
        and levels == mesh.shape["lon"]
        and mesh.shape["lon"] % 2 == 0
        and rows % 8 == 0
        and rows >= 2 * BAND + 8
        and last + 4 <= LANE
        and last >= 2
        and cols > LANE
        and 2 * (count + 3) * levels <= LANE
        and count % 5 == 0
    )


def solution(mesh):
    placed = (
        P("member", "lev", "lat", "lon"),
        P(("member", "lev"), "lat", "lon"),
        P(("member", "lev"), "lat", "lon"),
        P(("member", "lev"), "lat", "lon"),
        P(),
    )
    outs = (
        P("member", "lev", "lat", "lon"),
        P(("member", "lev"), "lat", "lon"),
        P(("member", "lev"), "lat", "lon"),
        P(("member", "lev"), "lat", "lon"),
    )

    def program(*args):
        part = shards_tiled if tiles_fit(mesh, args[0]) else shards
        return jax.shard_map(part, mesh=mesh, in_specs=placed, out_specs=outs, check_vma=False)(*args)

    return program
```

```python
import functools
import math

import jax
import jax.numpy as jnp
import numpy as np
from jax import lax
from jax.experimental import pallas as pl
from jax.experimental.pallas import tpu as pltpu
from jax.sharding import PartitionSpec as P

NSUB = 2
POLAR = 60
KMAX = 191


COURANT_CAP = 0.15
GRADIENT_COEF = 0.1


def extended_2(block, sides, width):
    for axis, dim in sides:
        count = lax.axis_size(axis)
        forward = [(i, i + 1) for i in range(count - 1)]
        forward.append((count - 1, 0))
        backward = [(target, source) for source, target in forward]
        low = lax.ppermute(
            lax.slice_in_dim(block, block.shape[dim] - width, None, axis=dim), axis, forward
        )
        high = lax.ppermute(lax.slice_in_dim(block, 0, width, axis=dim), axis, backward)
        block = jnp.concatenate([low, block, high], axis=dim)
    return block


def shifted(block, axis, distance):
    devices = range(lax.axis_size(axis))
    route = [((i - distance) % len(devices), i) for i in devices]
    return lax.ppermute(block, axis, route)


def entering(value, axis, join, neutral):
    count, mine = (lax.axis_size(axis), lax.axis_index(axis))
    pieces = lax.all_gather(value, axis)
    running = jnp.full_like(value, 0) + jnp.asarray(neutral, value.dtype)

    def step(position, running):
        longer = join(running, pieces[position])
        return jnp.where(position < mine, longer, running)

    return lax.fori_loop(0, count - 1, step, running)


def advance_level(extended, pressure):
    tracer_count = extended.shape[0] - 3
    thick = extended[tracer_count]
    east_wind = extended[tracer_count + 1]
    north_wind = extended[tracer_count + 2]
    masses = jnp.concatenate([thick[None], extended[:tracer_count] * thick[None]], 0)
    east_courant = COURANT_CAP * jnp.tanh(0.5 * (east_wind[1:-1, :-1] + east_wind[1:-1, 1:]))
    east_flux = (
        jnp.maximum(east_courant, 0.0) * masses[:, 1:-1, :-1]
        + jnp.minimum(east_courant, 0.0) * masses[:, 1:-1, 1:]
    )
    south_courant = COURANT_CAP * jnp.tanh(0.5 * (north_wind[:-1, 1:-1] + north_wind[1:, 1:-1]))
    south_flux = (
        jnp.maximum(south_courant, 0.0) * masses[:, :-1, 1:-1]
        + jnp.minimum(south_courant, 0.0) * masses[:, 1:, 1:-1]
    )
    updated = (
        masses[:, 1:-1, 1:-1]
        - (east_flux[:, :, 1:] - east_flux[:, :, :-1])
        - (south_flux[:, 1:] - south_flux[:, :-1])
    )
    new_thick = updated[0]
    new_mixing = updated[1:] / new_thick[None]
    new_east = east_wind[1:-1, 1:-1] - GRADIENT_COEF * (pressure[1:-1, 2:] - pressure[1:-1, :-2])
    new_north = north_wind[1:-1, 1:-1] - GRADIENT_COEF * (pressure[2:, 1:-1] - pressure[:-2, 1:-1])
    return (new_mixing, new_thick, new_east, new_north)


def wave_basis(anchor, length, lon_total):
    cells = anchor + jnp.arange(length, dtype=jnp.int32)
    waves = jnp.arange(KMAX + 1, dtype=jnp.int32)
    phase = (cells[:, None] * waves[None, :] % lon_total).astype(jnp.float32) * (
        2.0 * math.pi / lon_total
    )
    return jnp.concatenate([jnp.cos(phase), jnp.sin(phase)], 1)


def wave_weights(limits, lon_total):
    waves = jnp.arange(KMAX + 1, dtype=jnp.int32)
    scaled = jnp.where(waves == 0, 1.0, 2.0).astype(jnp.float32) / lon_total
    kept = jnp.where(waves[None, :] <= limits[:, None], scaled[None, :], 0.0)
    return jnp.concatenate([kept, kept], 1)


def smooth_winds(zonal, meridional, cutoff, is_north, is_south):
    level_count, row_count, col_count = zonal.shape
    lon_count = lax.axis_size("lon")
    lon_total = col_count * lon_count
    north_rows = jnp.stack([zonal[:, :POLAR], meridional[:, :POLAR]], 0)
    south_rows = jnp.stack([zonal[:, row_count - POLAR :], meridional[:, row_count - POLAR :]], 0)
    selected = jnp.where(is_north, north_rows, south_rows).reshape(-1, col_count)
    limits = jnp.tile(jnp.where(is_north, cutoff[0], cutoff[1]), 2 * level_count)
    fragment = lax.all_gather(selected, "lon", axis=1, tiled=True)
    basis = wave_basis(jnp.int32(0), fragment.shape[1], lon_total)
    spectrum = jnp.dot(
        fragment, basis, precision=lax.Precision.HIGHEST, preferred_element_type=jnp.float32
    )
    own_basis = wave_basis(lax.axis_index("lon") * col_count, col_count, lon_total)
    filtered = jnp.dot(
        spectrum * wave_weights(limits, lon_total),
        own_basis.T,
        precision=lax.Precision.HIGHEST,
        preferred_element_type=jnp.float32,
    )
    filtered = filtered.reshape(2, level_count, POLAR, col_count)
    row_start = jnp.where(is_north, 0, row_count - POLAR).astype(jnp.int32)
    polar_band = jnp.logical_or(is_north, is_south)
    new_zonal = lax.dynamic_update_slice_in_dim(zonal, filtered[0], row_start, 1)
    new_merid = lax.dynamic_update_slice_in_dim(meridional, filtered[1], row_start, 1)
    return (jnp.where(polar_band, new_zonal, zonal), jnp.where(polar_band, new_merid, meridional))


def shards(tracers, thickness, zonal, meridional, cutoff):
    tracer_count = tracers.shape[0]
    lat_index = lax.axis_index("lat")
    is_north = lat_index == 0
    is_south = lat_index == lax.axis_size("lat") - 1
    lon_count = lax.axis_size("lon")
    flip_sign = jnp.concatenate(
        [jnp.ones((tracer_count + 1,), jnp.float32), -jnp.ones((2,), jnp.float32)]
    )[:, None, None]
    advance_all = jax.vmap(advance_level, in_axes=(1, 0), out_axes=(1, 0, 0, 0))
    for substep in range(NSUB):
        zonal, meridional = smooth_winds(zonal, meridional, cutoff, is_north, is_south)
        state = jnp.concatenate([tracers, thickness[None], zonal[None], meridional[None]], 0)
        extended = extended_2(state, (("lat", 2), ("lon", 3)), 1)
        edges = jnp.stack([state[:, :, 0], state[:, :, -1]], 2)
        opposite = shifted(edges, "lon", lon_count // 2)
        north_rim = jnp.where(is_north, opposite[:, :, 0] * flip_sign, extended[:, :, 0, 1:-1])
        south_rim = jnp.where(is_south, opposite[:, :, 1] * flip_sign, extended[:, :, -1, 1:-1])
        extended = extended.at[:, :, 0, 1:-1].set(north_rim)
        extended = extended.at[:, :, -1, 1:-1].set(south_rim)
        thick_ext = extended[tracer_count]
        column_above = entering(
            jnp.sum(thick_ext, 0),
            "lev",
            lambda earlier, later: earlier + later,
            jnp.zeros(thick_ext.shape[1:], jnp.float32),
        )
        pressure = jnp.cumsum(thick_ext, axis=0) - 0.5 * thick_ext + column_above[None]
        tracers, thickness, zonal, meridional = advance_all(extended, pressure)
    return (tracers, thickness, zonal, meridional)


LANE = 128
POLAR_AT, MIDDLE_AT = 2, 6
UNROLL = dict(step=8, bring=8, coef=8, one=8, two=8)
PAD = 16
BAND = 64


def cost(micros):
    return pl.CostEstimate(flops=0, bytes_accessed=int(micros * 3.3e6), transcendentals=0)


def params(mib=56):
    return pltpu.CompilerParams(vmem_limit_bytes=mib * 1024 * 1024)


def lanes():
    return lax.broadcasted_iota(jnp.int32, (8, LANE), 1)


def at_row(row):
    return pl.ds(row if isinstance(row, int) else pl.multiple_of(row, 8), 8)


def eight(index):
    return at_row(8 * index)


def from_east(tiles, lane):
    turned = [pltpu.roll(t, LANE - 1, 1) for t in tiles]
    n = len(tiles)
    return [jnp.where(lane < LANE - 1, turned[c], turned[(c + 1) % n]) for c in range(n)]


def from_west(tiles, lane):
    turned = [pltpu.roll(t, 1, 1) for t in tiles]
    n = len(tiles)
    return [jnp.where(lane > 0, turned[c], turned[(c - 1) % n]) for c in range(n)]


def courant(a, b):
    return COURANT_CAP * jnp.tanh(0.5 * (a + b))


def rim_lanes(east, west, plane, last, lane):
    to_east = lax.rem(last + LANE - 2 * plane, LANE)
    to_west = lax.rem(2 * LANE - 2 - 2 * plane, LANE)
    return jnp.where(lane < last + 2, pltpu.roll(east, to_east, 1), pltpu.roll(west, to_west, 1))


def inflows(h, u, v, h_n, h_s, v_n, v_s, lane):
    count = range(len(h))
    u_e, h_e = from_east(u, lane), from_east(h, lane)
    c_e = [courant(u[c], u_e[c]) for c in count]
    out_e = [jnp.maximum(c_e[c], 0.0) * h[c] for c in count]
    in_e = [jnp.maximum(-c_e[c], 0.0) * h_e[c] for c in count]
    in_w, out_w = from_west(out_e, lane), from_west(in_e, lane)
    c_s = [courant(v[c], v_s[c]) for c in count]
    c_n = [courant(v_n[c], v[c]) for c in count]
    in_s = [jnp.maximum(-c_s[c], 0.0) * h_s[c] for c in count]
    out_s = [jnp.maximum(c_s[c], 0.0) * h[c] for c in count]
    in_n = [jnp.maximum(c_n[c], 0.0) * h_n[c] for c in count]
    out_n = [jnp.maximum(-c_n[c], 0.0) * h[c] for c in count]
    new = [
        h[c] - (out_e[c] - in_e[c]) + (in_w[c] - out_w[c]) - (out_s[c] - in_s[c]) + (in_n[c] - out_n[c])
        for c in count
    ]
    return in_e, in_w, in_n, in_s, new


def sweep(first, end, body, depth):
    whole = (end - first) // depth

    def step(k, _):
        for j in range(depth):
            body(first + k * depth + j)
        return 0

    lax.fori_loop(0, whole, step, 0)
    for i in range(first + whole * depth, end):
        body(i)


def tiles_at(ref, base, count, lead=()):
    return [ref[lead + (c, base, slice(None))] for c in range(count)]


def inflows_at(h, u, v, row, count, lead, lane):
    mid = at_row(row)
    up, down = pl.ds(row - 1, 8), pl.ds(row + 1, 8)
    hl, vl = lead
    return inflows(
        tiles_at(h, mid, count, hl),
        tiles_at(u, mid, count, vl),
        tiles_at(v, mid, count, vl),
        tiles_at(h, up, count, hl),
        tiles_at(h, down, count, hl),
        tiles_at(v, up, count, vl),
        tiles_at(v, down, count, vl),
        lane,
    )


def band_kernel(n, s, *refs):
    ins, outs = refs[: 3 * n], refs[3 * n :]
    for north in (True, False):

        @pl.when(s[0] == int(north))
        def _():
            lo = 0 if north else BAND - POLAR
            for d in range(n):
                u, v, h = ins[3 * d : 3 * d + 3]
                outs[d][0:POLAR, :] = u[0, lo : lo + POLAR, :]
                outs[d][POLAR : 2 * POLAR, :] = v[0, lo : lo + POLAR, :]
                first = 0 if north else BAND - POLAR - 1
                outs[d][2 * POLAR : 3 * POLAR + 1, :] = h[0, first : first + POLAR + 1, :]
                outs[d][3 * POLAR + 1 :, :] = jnp.zeros((3, h.shape[2]), jnp.float32)


def band_rows(scalars, u, v, h, n):
    levels, _, cols = u.shape

    def spec(d):
        return pl.BlockSpec(
            (pl.Element(1), pl.Element(BAND), pl.Element(cols)),
            lambda i, s: (lax.rem(s[1] + d, n), s[POLAR_AT] * 8, 0),
        )

    rows = 3 * POLAR + 4
    return pl.pallas_call(
        functools.partial(band_kernel, n),
        grid_spec=pltpu.PrefetchScalarGridSpec(
            num_scalar_prefetch=1,
            grid=(1,),
            in_specs=[spec(d) for d in range(n) for _ in range(3)],
            out_specs=[pl.BlockSpec((rows, cols), lambda i, s: (0, 0))] * n,
        ),
        out_shape=[jax.ShapeDtypeStruct((rows, cols), jnp.float32)] * n,
        cost_estimate=cost(3),
        compiler_params=params(),
        name="band_rows",
    )(scalars, *([u, v, h] * n))


def spectrum_kernel(n, s, *refs):
    total = None
    for d in range(n):
        part = jnp.dot(
            refs[d][...],
            refs[n + d][0],
            precision=lax.Precision.HIGHEST,
            preferred_element_type=jnp.float32,
        )
        total = part if total is None else total + part
    refs[2 * n][...] = total


def spectra(scalars, pieces, basis):
    n = len(pieces)
    rows, cols = pieces[0].shape
    waves = basis.shape[2]

    def spec(d):
        return pl.BlockSpec((1, cols, waves), lambda i, s: (lax.rem(s[1] + n - d, n), 0, 0))

    return pl.pallas_call(
        functools.partial(spectrum_kernel, n),
        grid_spec=pltpu.PrefetchScalarGridSpec(
            num_scalar_prefetch=1,
            grid=(1,),
            in_specs=[pl.BlockSpec((rows, cols), lambda i, s: (0, 0))] * n + [spec(d) for d in range(n)],
            out_specs=pl.BlockSpec((rows, waves), lambda i, s: (0, 0)),
        ),
        out_shape=jax.ShapeDtypeStruct((rows, waves), jnp.float32),
        cost_estimate=cost(6),
        compiler_params=params(),
        name="spectra",
    )(scalars, *pieces, *([basis] * n))


def pack_kernel(fields, last, s, t_lo, t_hi, h_lo, h_hi, u_lo, u_hi, v_lo, v_hi, west, east):
    level = pl.program_id(0)
    lane = lanes()
    lows = [(t_lo, (f, 0)) for f in range(fields - 3)] + [(h_lo, (0,)), (u_lo, (0,)), (v_lo, (0,))]
    highs = [(t_hi, (f, 0)) for f in range(fields - 3)] + [(h_hi, (0,)), (u_hi, (0,)), (v_hi, (0,))]
    begin = 2 * fields * level
    mine = jnp.logical_and(lane >= begin, lane < begin + 2 * fields)

    def step(i):
        rows = eight(i)
        for f in range(fields):
            here = lane >= 2 * f
            ref, lead = lows[f]
            tile = ref[lead + (rows, slice(None))]
            got_w = jnp.where(here, pltpu.roll(tile, 2 * f, 1), got_w) if f else tile
            ref, lead = highs[f]
            tile = ref[lead + (rows, slice(None))]
            turned = pltpu.roll(tile, (2 * f - last + 2) % LANE, 1)
            got_e = jnp.where(here, turned, got_e) if f else turned
        west[rows, :] = jnp.where(mine, pltpu.roll(got_w, begin, 1), west[rows, :])
        east[rows, :] = jnp.where(mine, pltpu.roll(got_e, begin, 1), east[rows, :])

    sweep(0, west.shape[0] // 8, step, UNROLL["step"])


def pack_columns(scalars, tracers, h, u, v):
    count, levels, rows, cols = tracers.shape
    high = (cols - 1) // LANE
    t_spec = [pl.BlockSpec((count, 1, rows, LANE), lambda l, s, c=c: (0, l, 0, c)) for c in (0, high)]
    f_spec = [pl.BlockSpec((1, rows, LANE), lambda l, s, c=c: (l, 0, c)) for c in (0, high)]
    out = jax.ShapeDtypeStruct((rows, LANE), jnp.float32)
    return pl.pallas_call(
        functools.partial(pack_kernel, count + 3, cols - LANE * high),
        grid_spec=pltpu.PrefetchScalarGridSpec(
            num_scalar_prefetch=1,
            grid=(levels,),
            in_specs=t_spec + f_spec * 3,
            out_specs=[pl.BlockSpec((rows, LANE), lambda l, s: (0, 0))] * 2,
        ),
        out_shape=[out, out],
        cost_estimate=cost(10),
        compiler_params=params(),
        name="pack_columns",
    )(scalars, tracers, tracers, h, h, u, u, v, v)


def rows_kernel(fields, s, t_top, t_bot, h_top, h_bot, u_top, u_bot, v_top, v_bot,
                e_top, e_bot, w_top, w_bot, pole, facing, top, bot):
    level = pl.program_id(0)
    lane = lanes()
    cols = h_top.shape[2]
    tail = top.shape[1] - LANE
    last = cols - tail
    refs = [(t_top, t_bot, (f, 0)) for f in range(fields - 3)]
    refs += [(h_top, h_bot, (0,)), (u_top, u_bot, (0,)), (v_top, v_bot, (0,))]
    for f in range(fields):
        plane = fields * level + f
        a, b, lead = refs[f]
        top[:, 0:cols] = a[lead]
        bot[:, 0:cols] = b[lead]
        top[:, cols:] = rim_lanes(e_top[...], w_top[...], plane, last, lane)[:, last:]
        bot[:, cols:] = rim_lanes(e_bot[...], w_bot[...], plane, last, lane)[:, last:]
        flip = -1.0 if f == fields - 1 else 1.0

        @pl.when(s[0] == 1)
        def _():
            pole[0, f, 0:1, :] = flip * top[1:2, :]
            pole[0, f, 1:2, :] = flip * top[0:1, :]
            facing[0, f] = bot[6:8, :]

        @pl.when(s[0] == 0)
        def _():
            pole[0, f, 0:1, :] = flip * bot[7:8, :]
            pole[0, f, 1:2, :] = flip * bot[6:7, :]
            facing[0, f] = top[0:2, :]


def edge_rows(scalars, tracers, h, u, v, east, west):
    count, levels, rows, cols = tracers.shape
    fields = count + 3
    width = LANE * ((cols - 1) // LANE + 1)
    ends = (0, rows // 8 - 1)
    t_spec = [pl.BlockSpec((count, 1, 8, cols), lambda l, s, r=r: (0, l, r, 0)) for r in ends]
    f_spec = [pl.BlockSpec((1, 8, cols), lambda l, s, r=r: (l, r, 0)) for r in ends]
    c_spec = [pl.BlockSpec((8, LANE), lambda l, s, r=r: (r, 0)) for r in ends]
    out = jax.ShapeDtypeStruct((levels, fields, 2, width), jnp.float32)
    return pl.pallas_call(
        functools.partial(rows_kernel, fields),
        grid_spec=pltpu.PrefetchScalarGridSpec(
            num_scalar_prefetch=1,
            grid=(levels,),
            in_specs=t_spec + f_spec * 3 + c_spec * 2,
            out_specs=[pl.BlockSpec((1, fields, 2, width), lambda l, s: (l, 0, 0, 0))] * 2,
            scratch_shapes=[pltpu.VMEM((8, width), jnp.float32)] * 2,
        ),
        out_shape=[out, out],
        cost_estimate=cost(7),
        compiler_params=params(),
        name="edge_rows",
    )(scalars, tracers, tracers, h, h, u, u, v, v, east, east, west, west)


def bring_rows(plane, source, target, here, there, rim, count, last):
    (ref, lead), (out, at) = source, target
    for c in range(count - 1):
        out[at + (c, there, slice(None))] = ref[lead + (here, slice(c * LANE, (c + 1) * LANE))]
    out[at + (count - 1, there, slice(0, last))] = ref[lead + (here, slice(LANE * (count - 1), None))]
    out[at + (count - 1, there, slice(last, None))] = rim(plane)[:, last:]


def pressure_rows(level, above, cum, press, h, count, tall):
    def body(i):
        here = eight(i)
        for c in range(count):
            before = jnp.where(level == 0, above[c, here, :], cum[c, here, :])
            now = h[c, here, :]
            press[c, here, :] = before + 0.5 * now
            cum[c, here, :] = before + now

    sweep(0, tall // 8, body, 8)


def gradient(press, row, count, lane):
    p = tiles_at(press, at_row(row), count)
    p_e, p_w = from_east(p, lane), from_west(p, lane)
    p_n, p_s = tiles_at(press, pl.ds(row - 1, 8), count), tiles_at(press, pl.ds(row + 1, 8), count)
    zonal = [GRADIENT_COEF * (p_e[c] - p_w[c]) for c in range(count)]
    return zonal, [GRADIENT_COEF * (p_s[c] - p_n[c]) for c in range(count)]


def column_kernel(fields, s, h, east, west, facing, total):
    lane = lanes()
    levels, rows, cols = h.shape
    count = total.shape[0]
    last = cols - LANE * (count - 1)

    def body(i):
        here, there = eight(i), at_row(8 * i + PAD)
        e, w = east[here, :], west[here, :]
        for c in range(count - 1):
            total[c, there, :] = sum(h[l, here, c * LANE : (c + 1) * LANE] for l in range(levels))
        total[count - 1, there, 0:last] = sum(h[l, here, LANE * (count - 1) :] for l in range(levels))
        rim = sum(rim_lanes(e, w, fields * l + fields - 3, last, lane)[:, last:] for l in range(levels))
        total[count - 1, there, last:] = rim

    sweep(0, rows // 8, body, 5)
    for c in range(count):
        part = slice(c * LANE, (c + 1) * LANE)
        edge = sum(facing[l, fields - 3, :, part] for l in range(levels))
        total[c, PAD - 2 : PAD, :] = edge
        total[c, PAD + rows : PAD + rows + 2, :] = edge


def column_sum(scalars, h, east, west, facing):
    _, rows, cols = h.shape
    count, tall = (cols - 1) // LANE + 1, rows + 2 * PAD
    return pl.pallas_call(
        functools.partial(column_kernel, facing.shape[1]),
        grid_spec=pltpu.PrefetchScalarGridSpec(
            num_scalar_prefetch=1,
            grid=(1,),
            in_specs=[pl.BlockSpec(x.shape, lambda i, s, k=x.ndim: (0,) * k) for x in (h, east, west, facing)],
            out_specs=pl.BlockSpec((count, tall, LANE), lambda i, s: (0, 0, 0)),
        ),
        out_shape=jax.ShapeDtypeStruct((count, tall, LANE), jnp.float32),
        cost_estimate=cost(4),
        compiler_params=params(),
        name="column_sum",
    )(scalars, h, east, west, facing)


def filter_kernel(n, s, *refs):
    pieces = refs[:n]
    above, limits, basis, slope, column, h, u, v, east, west, pole = refs[n : n + 11]
    h0_out, u0_out, v0_out, u1_out, v1_out, h1_out, total = refs[n + 11 : n + 18]
    held, lhs, rhs, cum, press = refs[n + 18 :]
    levels, count, slab = u0_out.shape[:3]
    cols = h.shape[2]
    last = cols - LANE * (count - 1)
    fields = pole.shape[1]
    lane = lanes()

    for l in range(levels):

        def bring(i):
            here, there = eight(i), at_row(8 * (i + s[POLAR_AT + 2]))
            rim_at = eight(i + s[POLAR_AT + 1])
            e, w = east[rim_at, :], west[rim_at, :]
            for f, (ref, out) in enumerate(((h, h0_out), (u, u0_out), (v, v0_out))):
                bring_rows(
                    fields * l + fields - 3 + f, (ref, (l,)), (out, (l,)), here, there,
                    lambda p: rim_lanes(e, w, p, last, lane), count, last,
                )

        sweep(0, BAND // 8 + 1, bring, 9)
        for ends in (True, False):

            @pl.when(s[0] == int(not ends))
            def _():
                at = PAD + BAND if ends else PAD - 2
                for c in range(count):
                    h0_out[l, c, at : at + 2, :] = pole[l, fields - 3, :, c * LANE : (c + 1) * LANE]

        pressure_rows(jnp.int32(l), column, cum, press, h0_out.at[l], count, slab)

        def later(i):
            row = 8 * i
            zonal, merid = gradient(press, row, count, lane)
            for c in range(count):
                u1_out[l, c, at_row(row), :] = u0_out[l, c, at_row(row), :] - zonal[c]
                v1_out[l, c, at_row(row), :] = v0_out[l, c, at_row(row), :] - merid[c]

        sweep(1, slab // 8 - 1, later, 5)

    waves = basis.shape[1]
    for d in range(n):
        held[lax.rem(s[1] + n - d, n)] = pieces[d][...]
    half = waves // 2
    wave = lax.broadcasted_iota(jnp.int32, (POLAR, waves), 1)
    wave = jnp.where(wave < half, wave, wave - half)
    scale = jnp.where(wave == 0, 1.0, 2.0) / (n * cols)
    keep = jnp.where(wave <= limits[0:POLAR, 0:1], scale, 0.0)
    turn = jnp.where(lax.rem(wave[0:2], 2) == 0, 1.0, -1.0)
    one = turn[0:1]
    for north in (True, False):

        @pl.when(s[0] == int(north))
        def _():
            first = PAD if north else PAD + BAND - POLAR
            rim = PAD - 2 if north else PAD + BAND

            def level_step(l, cum):
                u = held[l, 0:POLAR, :] * keep
                v = held[l, POLAR : 2 * POLAR, :] * keep
                thick = held[l, 2 * POLAR : 3 * POLAR + 1, :]
                p = cum + 0.5 * thick
                if north:
                    before = jnp.concatenate([one * p[0:1], p[0 : POLAR - 1]], 0)
                    diff = (p[1:] - before) * keep
                    rhs[0:POLAR, :] = p[0:POLAR] * keep
                else:
                    after = jnp.concatenate([p[2:], one * p[POLAR:]], 0)
                    diff = (after - p[0:POLAR]) * keep
                    rhs[0:POLAR, :] = p[1:] * keep
                w = v - GRADIENT_COEF * diff
                lhs[0:POLAR, :] = u
                lhs[POLAR : 2 * POLAR, :] = v
                lhs[2 * POLAR : 3 * POLAR, :] = w
                for k, (x, sign) in enumerate(((u, 1.0), (v, -1.0), (w, -1.0))):
                    a, b = (x[1:2], x[0:1]) if north else (x[POLAR - 1 :], x[POLAR - 2 : POLAR - 1])
                    at = 3 * POLAR + 2 * k
                    lhs[at : at + 1, :] = sign * one * a
                    lhs[at + 1 : at + 2, :] = sign * one * b
                back = jnp.dot(
                    lhs[...], basis[0], precision=lax.Precision.HIGHEST, preferred_element_type=jnp.float32
                )
                grad = jnp.dot(
                    rhs[...], slope[0], precision=lax.Precision.HIGHEST, preferred_element_type=jnp.float32
                )
                zonal = back[0:POLAR]
                later = zonal - GRADIENT_COEF * grad[0:POLAR]
                for c in range(count):
                    part = slice(c * LANE, (c + 1) * LANE)
                    u0_out[l, c, first : first + POLAR, :] = zonal[:, part]
                    v0_out[l, c, first : first + POLAR, :] = back[POLAR : 2 * POLAR, part]
                    u1_out[l, c, first : first + POLAR, :] = later[:, part]
                    v1_out[l, c, first : first + POLAR, :] = back[2 * POLAR : 3 * POLAR, part]
                    u0_out[l, c, rim : rim + 2, :] = back[3 * POLAR : 3 * POLAR + 2, part]
                    v0_out[l, c, rim : rim + 2, :] = back[3 * POLAR + 2 : 3 * POLAR + 4, part]
                    v1_out[l, c, rim : rim + 2, :] = back[3 * POLAR + 4 : 3 * POLAR + 6, part]
                return cum + thick

            lax.fori_loop(0, levels, level_step, above[0 : POLAR + 1, :])

    def step(k):
        l, i = k // (slab // 8 - 2), lax.rem(k, slab // 8 - 2) + 1
        here = eight(i)
        new = inflows_at(h0_out, u0_out, v0_out, 8 * i, count, ((l,), (l,)), lane)[4]
        for c in range(count):
            h1_out[l, c, here, :] = new[c]
            total[c, here, :] = jnp.where(l == 0, new[c], total[c, here, :] + new[c])

    sweep(0, levels * (slab // 8 - 2), step, UNROLL["step"])


def filtered_band(scalars, pieces, above, limits, basis, slope, column, h, u, v, east, west, pole):
    n = len(pieces)
    rows, waves = pieces[0].shape
    width = basis.shape[2]
    levels, height, cols = h.shape
    count = column.shape[0]
    slab = BAND + 2 * PAD
    E = pl.Element
    raw = pl.BlockSpec((E(levels), E(BAND + 8), E(cols)), lambda i, s: (0, s[POLAR_AT + 1] * 8, 0))
    out = jax.ShapeDtypeStruct((levels, count, slab, LANE), jnp.float32)
    whole = pl.BlockSpec((levels, count, slab, LANE), lambda i, s: (0, 0, 0, 0))
    return pl.pallas_call(
        functools.partial(filter_kernel, n),
        grid_spec=pltpu.PrefetchScalarGridSpec(
            num_scalar_prefetch=1,
            grid=(1,),
            in_specs=[pl.BlockSpec((rows, waves), lambda i, s: (0, 0))] * n
            + [
                pl.BlockSpec(above.shape, lambda i, s: (0, 0)),
                pl.BlockSpec(limits.shape, lambda i, s: (0, 0)),
                pl.BlockSpec((1, waves, width), lambda i, s: (s[1], 0, 0)),
                pl.BlockSpec((1, waves, width), lambda i, s: (s[1], 0, 0)),
                pl.BlockSpec((E(count), E(slab), E(LANE)), lambda i, s: (0, s[POLAR_AT] * 8, 0)),
            ]
            + [raw] * 3
            + [pl.BlockSpec((height, LANE), lambda i, s: (0, 0))] * 2
            + [pl.BlockSpec(pole.shape, lambda i, s: (0, 0, 0, 0))],
            out_specs=[whole] * 6 + [pl.BlockSpec((count, slab, LANE), lambda i, s: (0, 0, 0))],
            scratch_shapes=[
                pltpu.VMEM((n, rows, waves), jnp.float32),
                pltpu.VMEM((3 * POLAR + 12, waves), jnp.float32),
                pltpu.VMEM((BAND, waves), jnp.float32),
            ]
            + [pltpu.VMEM((count, slab, LANE), jnp.float32)] * 2,
        ),
        out_shape=[out] * 6 + [jax.ShapeDtypeStruct((count, slab, LANE), jnp.float32)],
        cost_estimate=cost(12),
        compiler_params=params(),
        name="filtered_band",
    )(scalars, *pieces, above, limits, basis, slope, column, h, u, v, east, west, pole)


def slab_kernel(fields, group, rows, place, inner, s, *refs):
    if inner:
        tr, h, u, v, above, east, west, rim = refs[:8]
        tr_out, h_out, h1, u1, v1, total = refs[8:14]
        early, late, t0, t1, h0, u0, v0, cum, press = refs[14:]
        lead = ((), ())
        lead_one = (0,)
    else:
        tr, h0, u0, v0, u1, v1, east, west, rim = refs[:9]
        tr_out, h_out = refs[11:13]
        early, late, t0, t1, h1 = refs[13:]
        lead = ((0,), (0,))
        lead_one = ()
    level, part = pl.program_id(0), pl.program_id(1)
    lane = lanes()
    count = early.shape[1]
    cols = h_out.shape[2]
    last = cols - LANE * (count - 1)
    tiles = rows // 8

    def window(i):
        rim_at = eight(i + s[place + 1])
        e, w = east[rim_at, :], west[rim_at, :]
        return eight(i), at_row(8 * (i + s[place + 2])), lambda p: rim_lanes(e, w, p, last, lane)

    def rims(store):
        for ends in (True, False):

            @pl.when(s[place + 3] == int(ends))
            def _():
                at = PAD + rows if ends else PAD - 2
                for c in range(count):
                    store(c, slice(at, at + 2), slice(c * LANE, (c + 1) * LANE))

    def weights_from(target, here, flows, new):
        for c in range(count):
            inv = 1.0 / new[c]
            w = [x[c] * inv for x in flows]
            for k in range(4):
                target[k + 1, c, here, :] = w[k]
            target[0, c, here, :] = 1.0 - ((w[0] + w[1]) + (w[2] + w[3]))

    @pl.when(part == 0)
    def _():
        if inner:

            def bring(i):
                here, there, rim_of = window(i)
                for f, (ref, out) in enumerate(((h, h0), (u, u0), (v, v0))):
                    bring_rows(
                        fields * level + fields - 3 + f, (ref, (0,)), (out, ()), here, there, rim_of, count, last
                    )

            sweep(0, tiles + 1, bring, UNROLL["bring"])

            def store(c, at, part):
                for f, out in enumerate((h0, u0, v0)):
                    out[c, at, :] = rim[0, fields - 3 + f, :, part]

            rims(store)
            pressure_rows(level, above, cum, press, h0, count, rows + 2 * PAD)

        def one(i):
            row = 8 * i + PAD - 8
            there = at_row(row)
            *flows, new = inflows_at(h0, u0, v0, row, count, lead, lane)
            weights_from(early, eight(i), flows, new)
            for c in range(count):
                h1[lead_one + (c, there, slice(None))] = new[c]
            if inner:
                zonal, merid = gradient(press, row, count, lane)
                for c in range(count):
                    total[c, there, :] = jnp.where(level == 0, new[c], total[c, there, :] + new[c])
                    u1[0, c, there, :] = u0[c, there, :] - zonal[c]
                    v1[0, c, there, :] = v0[c, there, :] - merid[c]

        sweep(0, tiles + 2, one, UNROLL["coef"])

        def two(i):
            here = eight(i)
            *flows, new = inflows_at(h1, u1, v1, 8 * i + PAD, count, (lead_one, (0,)), lane)
            weights_from(late, here, flows, new)
            for c in range(count):
                wide = min(LANE, cols - c * LANE)
                h_out[0, here, c * LANE : c * LANE + wide] = new[c][:, 0:wide]

        sweep(0, tiles, two, UNROLL["coef"])

    def bring(i):
        here, there, rim_of = window(i)
        for j in range(group):
            bring_rows(
                fields * level + part * group + j, (tr, (j, 0)), (t0, (j,)), here, there, rim_of, count, last
            )

    sweep(0, tiles + 1, bring, UNROLL["bring"])

    def store(c, at, lanes_of):
        for j in range(group):
            t0[j, c, at, :] = rim[0, part * group + j, :, lanes_of]

    rims(store)

    def advance(source, j, row, weights):
        mid = tiles_at(source, at_row(row), count, (j,))
        up = tiles_at(source, pl.ds(row - 1, 8), count, (j,))
        down = tiles_at(source, pl.ds(row + 1, 8), count, (j,))
        right, left = from_east(mid, lane), from_west(mid, lane)
        return [
            weights[0][c] * mid[c]
            + weights[1][c] * right[c]
            + weights[2][c] * left[c]
            + weights[3][c] * up[c]
            + weights[4][c] * down[c]
            for c in range(count)
        ]

    def one(i):
        weights = [tiles_at(early, eight(i), count, (k,)) for k in range(5)]
        for j in range(group):
            new = advance(t0, j, 8 * i + PAD - 8, weights)
            for c in range(count):
                t1[j, c, at_row(8 * i + PAD - 8), :] = new[c]

    sweep(0, tiles + 2, one, UNROLL["one"])

    def two(i):
        here = eight(i)
        weights = [tiles_at(late, here, count, (k,)) for k in range(5)]
        for j in range(group):
            new = advance(t1, j, 8 * i + PAD, weights)
            for c in range(count):
                wide = min(LANE, cols - c * LANE)
                tr_out[j, 0, here, c * LANE : c * LANE + wide] = new[c][:, 0:wide]

    sweep(0, tiles, two, UNROLL["two"])


def tracer_slab(scalars, place, rows, group, tracers, fields, east, west, rim, base, micros, name):
    count, levels, height, cols = tracers.shape
    tiles = (cols - 1) // LANE + 1
    slab = rows + 2 * PAD
    inner = base is None
    E = pl.Element
    slabs = pl.BlockSpec((1, tiles, slab, LANE), lambda l, g, s: (l, 0, 0, 0))
    flat = pl.BlockSpec((tiles, slab, LANE), lambda l, g, s: (0, 0, 0))
    in_specs = [
        pl.BlockSpec(
            (E(group), E(1), E(rows + 8), E(cols)), lambda l, g, s: (g * group, l, s[place + 1] * 8, 0)
        )
    ]
    if inner:
        in_specs += [pl.BlockSpec((E(1), E(rows + 8), E(cols)), lambda l, g, s: (l, s[place + 1] * 8, 0))] * 3
        in_specs += [pl.BlockSpec((E(tiles), E(slab), E(LANE)), lambda l, g, s: (0, s[place] * 8, 0))]
    else:
        in_specs += [slabs] * 5
    in_specs += [pl.BlockSpec((height, LANE), lambda l, g, s: (0, 0))] * 2
    in_specs += [pl.BlockSpec((1,) + rim.shape[1:], lambda l, g, s: (l, 0, 0, 0))]
    operands = [tracers, *fields, east, west, rim]
    out_specs = [
        pl.BlockSpec((E(group), E(1), E(rows), E(cols)), lambda l, g, s: (g * group, l, s[place] * 8, 0)),
        pl.BlockSpec((E(1), E(rows), E(cols)), lambda l, g, s: (l, s[place] * 8, 0)),
    ]
    out_shape = [
        jax.ShapeDtypeStruct(tracers.shape, jnp.float32),
        jax.ShapeDtypeStruct((levels, height, cols), jnp.float32),
    ]
    scratch = [
        pltpu.VMEM((5, tiles, rows + 16, LANE), jnp.float32),
        pltpu.VMEM((5, tiles, rows, LANE), jnp.float32),
        pltpu.VMEM((group, tiles, slab, LANE), jnp.float32),
        pltpu.VMEM((group, tiles, slab, LANE), jnp.float32),
    ]
    plane = pltpu.VMEM((tiles, slab, LANE), jnp.float32)
    aliases = {}
    if inner:
        out_specs += [slabs] * 3 + [flat]
        out_shape += [jax.ShapeDtypeStruct((levels, tiles, slab, LANE), jnp.float32)] * 3
        out_shape += [jax.ShapeDtypeStruct((tiles, slab, LANE), jnp.float32)]
        scratch += [plane] * 5
    else:
        in_specs += [pl.BlockSpec(memory_space=pl.ANY)] * 2
        operands += list(base)
        aliases = {len(operands) - 1: 0, len(operands): 1}
        scratch += [plane]
    return pl.pallas_call(
        functools.partial(slab_kernel, rim.shape[1], group, rows, place, inner),
        grid_spec=pltpu.PrefetchScalarGridSpec(
            num_scalar_prefetch=1,
            grid=(levels, count // group),
            in_specs=in_specs,
            out_specs=out_specs,
            scratch_shapes=scratch,
        ),
        out_shape=out_shape,
        input_output_aliases=aliases,
        cost_estimate=cost(micros),
        compiler_params=params(),
        name=name,
    )(scalars, *operands)


def winds_kernel(rows, has_base, s, h, u, v, above, *refs):
    u_out, v_out, cum, press = refs[2:] if has_base else refs
    lane = lanes()
    count, slab = h.shape[1:3]
    cols = u_out.shape[2]
    pressure_rows(pl.program_id(0), above, cum, press, h.at[0], count, slab)

    def step(i):
        row = 8 * i + PAD
        zonal, merid = gradient(press, row, count, lane)
        for c in range(count):
            wide = min(LANE, cols - c * LANE)
            part = slice(c * LANE, c * LANE + wide)
            u_out[0, eight(i), part] = (u[0, c, at_row(row), :] - zonal[c])[:, 0:wide]
            v_out[0, eight(i), part] = (v[0, c, at_row(row), :] - merid[c])[:, 0:wide]

    sweep(0, rows // 8, step, UNROLL["step"])


def last_winds(scalars, place, rows, h, u, v, above, height, cols, base, micros, name):
    levels, tiles, slab = h.shape[:3]
    E = pl.Element
    spec = pl.BlockSpec((1, tiles, slab, LANE), lambda l, s: (l, 0, 0, 0))
    flat = pl.BlockSpec((tiles, slab, LANE), lambda l, s: (0, 0, 0))
    out_spec = pl.BlockSpec((E(1), E(rows), E(cols)), lambda l, s: (l, s[place] * 8, 0))
    out = jax.ShapeDtypeStruct((levels, height, cols), jnp.float32)
    in_specs, operands, aliases = [spec] * 3 + [flat], [h, u, v, above], {}
    if base is not None:
        in_specs += [pl.BlockSpec(memory_space=pl.ANY)] * 2
        operands += list(base)
        aliases = {5: 0, 6: 1}
    return pl.pallas_call(
        functools.partial(winds_kernel, rows, base is not None),
        grid_spec=pltpu.PrefetchScalarGridSpec(
            num_scalar_prefetch=1,
            grid=(levels,),
            in_specs=in_specs,
            out_specs=[out_spec] * 2,
            scratch_shapes=[pltpu.VMEM((tiles, slab, LANE), jnp.float32)] * 2,
        ),
        out_shape=[out, out],
        input_output_aliases=aliases,
        cost_estimate=cost(micros),
        compiler_params=params(),
        name=name,
    )(scalars, *operands)


def bases(n, cols):
    total = n * cols
    wave = np.arange(KMAX + 1)
    cell = np.arange(total).reshape(n, cols)
    angle = (cell[:, :, None] * wave % total) * (2.0 * math.pi / total)
    forward = np.concatenate([np.cos(angle), np.sin(angle)], 2)
    width = LANE * ((cols - 1) // LANE + 1)
    lane = np.arange(width)
    lane = np.where(lane < width - 2, lane, lane - width)
    cell = np.arange(n)[:, None] * cols + lane[None, :]
    angle = (cell[:, None, :] * wave[:, None] % total) * (2.0 * math.pi / total)
    inverse = np.concatenate([np.cos(angle), np.sin(angle)], 1)
    steep = 2.0 * np.sin(wave * (2.0 * math.pi / total))[:, None]
    slope = np.concatenate([-steep * np.sin(angle), steep * np.cos(angle)], 1)
    return [jnp.asarray(x.astype(np.float32)) for x in (forward, inverse, slope)]


def shards_tiled(tracers, thickness, zonal, meridional, cutoff):
    count, levels, rows, cols = tracers.shape
    n = lax.axis_size("lon")
    me = lax.axis_index("lon").astype(jnp.int32)
    is_north = lax.axis_index("lat") == 0
    inner = rows - BAND

    band_at = rows // 8 - BAND // 8
    scalars = jnp.where(
        is_north,
        jnp.array([1, 0, 0, 0, PAD // 8, 0, BAND // 8, BAND // 8 - 1, PAD // 8 - 1, 1], jnp.int32),
        jnp.array([0, 0, band_at, band_at - 1, PAD // 8 - 1, 1, 0, 0, PAD // 8, 0], jnp.int32),
    )
    scalars = scalars + jnp.where(jnp.arange(10) == 1, me, 0)
    forward, inverse, slope = bases(n, cols)
    limits = jnp.where(is_north, cutoff[0], cutoff[1])
    limits = jnp.broadcast_to(jnp.pad(limits, (0, BAND - POLAR))[:, None], (BAND, LANE))

    def along(value, d):
        return lax.ppermute(value, "lon", [(i, (i + d) % n) for i in range(n)])

    def to_lower(value):
        return lax.ppermute(value, "lev", [(0, 1)])

    sent = band_rows(scalars, zonal, meridional, thickness, n)
    scalars, sent = lax.optimization_barrier((scalars, sent))
    pieces = [sent[0]] + [along(sent[d], d) for d in range(1, n)]
    packed = pack_columns(scalars, tracers, thickness, zonal, meridional)
    scalars, packed = lax.optimization_barrier((scalars, packed))
    east, west = along(packed[0], n - 1), along(packed[1], 1)

    own = spectra(scalars, pieces, forward)
    scalars, own = lax.optimization_barrier((scalars, own))
    pieces = [own] + [along(own, d) for d in range(1, n)]

    pole, facing = edge_rows(scalars, tracers, thickness, zonal, meridional, east, west)
    facing = lax.ppermute(facing, "lat", [(0, 1), (1, 0)])
    pole = along(pole, n // 2)
    column = column_sum(scalars, thickness, east, west, facing)
    column = to_lower(column)
    tr, h2, h1, u1, v1, total = tracer_slab(
        scalars, MIDDLE_AT, inner, 5, tracers, (thickness, zonal, meridional, column), east, west, facing, None,
        50, "tracers_inner",
    )
    scalars, total, pieces = lax.optimization_barrier((scalars, total, pieces))
    total = to_lower(total)
    above_band = to_lower(sum(p[2 * POLAR :] for p in pieces))
    h0, u0, v0, u1b, v1b, h1b, band_total = filtered_band(
        scalars, pieces, above_band, limits, inverse, slope, column, thickness, zonal, meridional, east, west, pole
    )
    band_total = to_lower(band_total)
    winds = last_winds(scalars, MIDDLE_AT, inner, h1, u1, v1, total, rows, cols, None, 7, "winds_inner")
    tr, h2 = tracer_slab(
        scalars, POLAR_AT, BAND, 10, tracers, (h0, u0, v0, u1b, v1b), east, west, pole, (tr, h2), 13,
        "tracers_polar",
    )
    u2, v2 = last_winds(
        scalars, POLAR_AT, BAND, h1b, u1b, v1b, band_total, rows, cols, winds, 4, "winds_polar"
    )
    return (tr, h2, u2, v2)


def tiles_fit(mesh, tracers):
    count, levels, rows, cols = tracers.shape
    rows, cols = rows // mesh.shape["lat"], cols // mesh.shape["lon"]
    count, levels = count // mesh.shape["member"], levels // mesh.shape["lev"]
    last = (cols - 1) % LANE + 1
    return (
        mesh.shape["lat"] == 2
        and mesh.shape["lev"] == 2
        and levels == mesh.shape["lon"]
        and mesh.shape["lon"] % 2 == 0
        and rows % 8 == 0
        and rows >= 2 * BAND + 8
        and last + 4 <= LANE
        and last >= 2
        and cols > LANE
        and 2 * (count + 3) * levels <= LANE
        and count % 5 == 0
    )


def solution(mesh):
    placed = (
        P("member", "lev", "lat", "lon"),
        P(("member", "lev"), "lat", "lon"),
        P(("member", "lev"), "lat", "lon"),
        P(("member", "lev"), "lat", "lon"),
        P(),
    )
    outs = (
        P("member", "lev", "lat", "lon"),
        P(("member", "lev"), "lat", "lon"),
        P(("member", "lev"), "lat", "lon"),
        P(("member", "lev"), "lat", "lon"),
    )

    def program(*args):
        part = shards_tiled if tiles_fit(mesh, args[0]) else shards
        return jax.shard_map(part, mesh=mesh, in_specs=placed, out_specs=outs, check_vma=False)(*args)

    return program
```

```python
import functools
import math

import jax
import jax.numpy as jnp
import numpy as np
from jax import lax
from jax.experimental import pallas as pl
from jax.experimental.pallas import tpu as pltpu
from jax.sharding import PartitionSpec as P

NSUB = 2
POLAR = 60
KMAX = 191


COURANT_CAP = 0.15
GRADIENT_COEF = 0.1


def extended_2(block, sides, width):
    for axis, dim in sides:
        count = lax.axis_size(axis)
        forward = [(i, i + 1) for i in range(count - 1)]
        forward.append((count - 1, 0))
        backward = [(target, source) for source, target in forward]
        low = lax.ppermute(
            lax.slice_in_dim(block, block.shape[dim] - width, None, axis=dim), axis, forward
        )
        high = lax.ppermute(lax.slice_in_dim(block, 0, width, axis=dim), axis, backward)
        block = jnp.concatenate([low, block, high], axis=dim)
    return block


def shifted(block, axis, distance):
    devices = range(lax.axis_size(axis))
    route = [((i - distance) % len(devices), i) for i in devices]
    return lax.ppermute(block, axis, route)


def entering(value, axis, join, neutral):
    count, mine = (lax.axis_size(axis), lax.axis_index(axis))
    pieces = lax.all_gather(value, axis)
    running = jnp.full_like(value, 0) + jnp.asarray(neutral, value.dtype)

    def step(position, running):
        longer = join(running, pieces[position])
        return jnp.where(position < mine, longer, running)

    return lax.fori_loop(0, count - 1, step, running)


def advance_level(extended, pressure):
    tracer_count = extended.shape[0] - 3
    thick = extended[tracer_count]
    east_wind = extended[tracer_count + 1]
    north_wind = extended[tracer_count + 2]
    masses = jnp.concatenate([thick[None], extended[:tracer_count] * thick[None]], 0)
    east_courant = COURANT_CAP * jnp.tanh(0.5 * (east_wind[1:-1, :-1] + east_wind[1:-1, 1:]))
    east_flux = (
        jnp.maximum(east_courant, 0.0) * masses[:, 1:-1, :-1]
        + jnp.minimum(east_courant, 0.0) * masses[:, 1:-1, 1:]
    )
    south_courant = COURANT_CAP * jnp.tanh(0.5 * (north_wind[:-1, 1:-1] + north_wind[1:, 1:-1]))
    south_flux = (
        jnp.maximum(south_courant, 0.0) * masses[:, :-1, 1:-1]
        + jnp.minimum(south_courant, 0.0) * masses[:, 1:, 1:-1]
    )
    updated = (
        masses[:, 1:-1, 1:-1]
        - (east_flux[:, :, 1:] - east_flux[:, :, :-1])
        - (south_flux[:, 1:] - south_flux[:, :-1])
    )
    new_thick = updated[0]
    new_mixing = updated[1:] / new_thick[None]
    new_east = east_wind[1:-1, 1:-1] - GRADIENT_COEF * (pressure[1:-1, 2:] - pressure[1:-1, :-2])
    new_north = north_wind[1:-1, 1:-1] - GRADIENT_COEF * (pressure[2:, 1:-1] - pressure[:-2, 1:-1])
    return (new_mixing, new_thick, new_east, new_north)


def wave_basis(anchor, length, lon_total):
    cells = anchor + jnp.arange(length, dtype=jnp.int32)
    waves = jnp.arange(KMAX + 1, dtype=jnp.int32)
    phase = (cells[:, None] * waves[None, :] % lon_total).astype(jnp.float32) * (
        2.0 * math.pi / lon_total
    )
    return jnp.concatenate([jnp.cos(phase), jnp.sin(phase)], 1)


def wave_weights(limits, lon_total):
    waves = jnp.arange(KMAX + 1, dtype=jnp.int32)
    scaled = jnp.where(waves == 0, 1.0, 2.0).astype(jnp.float32) / lon_total
    kept = jnp.where(waves[None, :] <= limits[:, None], scaled[None, :], 0.0)
    return jnp.concatenate([kept, kept], 1)


def smooth_winds(zonal, meridional, cutoff, is_north, is_south):
    level_count, row_count, col_count = zonal.shape
    lon_count = lax.axis_size("lon")
    lon_total = col_count * lon_count
    north_rows = jnp.stack([zonal[:, :POLAR], meridional[:, :POLAR]], 0)
    south_rows = jnp.stack([zonal[:, row_count - POLAR :], meridional[:, row_count - POLAR :]], 0)
    selected = jnp.where(is_north, north_rows, south_rows).reshape(-1, col_count)
    limits = jnp.tile(jnp.where(is_north, cutoff[0], cutoff[1]), 2 * level_count)
    fragment = lax.all_gather(selected, "lon", axis=1, tiled=True)
    basis = wave_basis(jnp.int32(0), fragment.shape[1], lon_total)
    spectrum = jnp.dot(
        fragment, basis, precision=lax.Precision.HIGHEST, preferred_element_type=jnp.float32
    )
    own_basis = wave_basis(lax.axis_index("lon") * col_count, col_count, lon_total)
    filtered = jnp.dot(
        spectrum * wave_weights(limits, lon_total),
        own_basis.T,
        precision=lax.Precision.HIGHEST,
        preferred_element_type=jnp.float32,
    )
    filtered = filtered.reshape(2, level_count, POLAR, col_count)
    row_start = jnp.where(is_north, 0, row_count - POLAR).astype(jnp.int32)
    polar_band = jnp.logical_or(is_north, is_south)
    new_zonal = lax.dynamic_update_slice_in_dim(zonal, filtered[0], row_start, 1)
    new_merid = lax.dynamic_update_slice_in_dim(meridional, filtered[1], row_start, 1)
    return (jnp.where(polar_band, new_zonal, zonal), jnp.where(polar_band, new_merid, meridional))


def shards(tracers, thickness, zonal, meridional, cutoff):
    tracer_count = tracers.shape[0]
    lat_index = lax.axis_index("lat")
    is_north = lat_index == 0
    is_south = lat_index == lax.axis_size("lat") - 1
    lon_count = lax.axis_size("lon")
    flip_sign = jnp.concatenate(
        [jnp.ones((tracer_count + 1,), jnp.float32), -jnp.ones((2,), jnp.float32)]
    )[:, None, None]
    advance_all = jax.vmap(advance_level, in_axes=(1, 0), out_axes=(1, 0, 0, 0))
    for substep in range(NSUB):
        zonal, meridional = smooth_winds(zonal, meridional, cutoff, is_north, is_south)
        state = jnp.concatenate([tracers, thickness[None], zonal[None], meridional[None]], 0)
        extended = extended_2(state, (("lat", 2), ("lon", 3)), 1)
        edges = jnp.stack([state[:, :, 0], state[:, :, -1]], 2)
        opposite = shifted(edges, "lon", lon_count // 2)
        north_rim = jnp.where(is_north, opposite[:, :, 0] * flip_sign, extended[:, :, 0, 1:-1])
        south_rim = jnp.where(is_south, opposite[:, :, 1] * flip_sign, extended[:, :, -1, 1:-1])
        extended = extended.at[:, :, 0, 1:-1].set(north_rim)
        extended = extended.at[:, :, -1, 1:-1].set(south_rim)
        thick_ext = extended[tracer_count]
        column_above = entering(
            jnp.sum(thick_ext, 0),
            "lev",
            lambda earlier, later: earlier + later,
            jnp.zeros(thick_ext.shape[1:], jnp.float32),
        )
        pressure = jnp.cumsum(thick_ext, axis=0) - 0.5 * thick_ext + column_above[None]
        tracers, thickness, zonal, meridional = advance_all(extended, pressure)
    return (tracers, thickness, zonal, meridional)


LANE = 128
POLAR_AT, MIDDLE_AT = 2, 6
UNROLL = dict(step=8, bring=8, coef=8, one=8, two=8)
PAD = 16
BAND = 64


def cost(micros):
    return pl.CostEstimate(flops=0, bytes_accessed=int(micros * 3.3e6), transcendentals=0)


def params(mib=56):
    return pltpu.CompilerParams(vmem_limit_bytes=mib * 1024 * 1024)


def lanes():
    return lax.broadcasted_iota(jnp.int32, (8, LANE), 1)


def at_row(row):
    return pl.ds(row if isinstance(row, int) else pl.multiple_of(row, 8), 8)


def eight(index):
    return at_row(8 * index)


def from_east(tiles, lane):
    turned = [pltpu.roll(t, LANE - 1, 1) for t in tiles]
    n = len(tiles)
    return [jnp.where(lane < LANE - 1, turned[c], turned[(c + 1) % n]) for c in range(n)]


def from_west(tiles, lane):
    turned = [pltpu.roll(t, 1, 1) for t in tiles]
    n = len(tiles)
    return [jnp.where(lane > 0, turned[c], turned[(c - 1) % n]) for c in range(n)]


def courant(a, b):
    return COURANT_CAP * jnp.tanh(0.5 * (a + b))


def rim_lanes(east, west, plane, last, lane):
    to_east = lax.rem(last + LANE - 2 * plane, LANE)
    to_west = lax.rem(2 * LANE - 2 - 2 * plane, LANE)
    return jnp.where(lane < last + 2, pltpu.roll(east, to_east, 1), pltpu.roll(west, to_west, 1))


def inflows(h, u, v, h_n, h_s, v_n, v_s, lane):
    count = range(len(h))
    u_e, h_e = from_east(u, lane), from_east(h, lane)
    c_e = [courant(u[c], u_e[c]) for c in count]
    out_e = [jnp.maximum(c_e[c], 0.0) * h[c] for c in count]
    in_e = [jnp.maximum(-c_e[c], 0.0) * h_e[c] for c in count]
    in_w, out_w = from_west(out_e, lane), from_west(in_e, lane)
    c_s = [courant(v[c], v_s[c]) for c in count]
    c_n = [courant(v_n[c], v[c]) for c in count]
    in_s = [jnp.maximum(-c_s[c], 0.0) * h_s[c] for c in count]
    out_s = [jnp.maximum(c_s[c], 0.0) * h[c] for c in count]
    in_n = [jnp.maximum(c_n[c], 0.0) * h_n[c] for c in count]
    out_n = [jnp.maximum(-c_n[c], 0.0) * h[c] for c in count]
    new = [
        h[c] - (out_e[c] - in_e[c]) + (in_w[c] - out_w[c]) - (out_s[c] - in_s[c]) + (in_n[c] - out_n[c])
        for c in count
    ]
    return in_e, in_w, in_n, in_s, new


def halves(x):
    high = x.astype(jnp.bfloat16)
    return high, (x - high.astype(jnp.float32)).astype(jnp.bfloat16)


def dot3(a, b):
    (a_hi, a_lo), (b_hi, b_lo) = halves(a), halves(b)

    def one(x, y):
        return jnp.dot(x, y, preferred_element_type=jnp.float32)

    return one(a_hi, b_hi) + (one(a_hi, b_lo) + one(a_lo, b_hi))


def sweep(first, end, body, depth):
    whole = (end - first) // depth

    def step(k, _):
        for j in range(depth):
            body(first + k * depth + j)
        return 0

    lax.fori_loop(0, whole, step, 0)
    for i in range(first + whole * depth, end):
        body(i)


def tiles_at(ref, base, count, lead=()):
    return [ref[lead + (c, base, slice(None))] for c in range(count)]


def inflows_at(h, u, v, row, count, lead, lane):
    mid = at_row(row)
    up, down = pl.ds(row - 1, 8), pl.ds(row + 1, 8)
    hl, vl = lead
    return inflows(
        tiles_at(h, mid, count, hl),
        tiles_at(u, mid, count, vl),
        tiles_at(v, mid, count, vl),
        tiles_at(h, up, count, hl),
        tiles_at(h, down, count, hl),
        tiles_at(v, up, count, vl),
        tiles_at(v, down, count, vl),
        lane,
    )


def band_kernel(n, s, *refs):
    ins, outs = refs[: 3 * n], refs[3 * n :]
    for north in (True, False):

        @pl.when(s[0] == int(north))
        def _():
            lo = 0 if north else BAND - POLAR
            for d in range(n):
                u, v, h = ins[3 * d : 3 * d + 3]
                outs[d][0:POLAR, :] = u[0, lo : lo + POLAR, :]
                outs[d][POLAR : 2 * POLAR, :] = v[0, lo : lo + POLAR, :]
                first = 0 if north else BAND - POLAR - 1
                outs[d][2 * POLAR : 3 * POLAR + 1, :] = h[0, first : first + POLAR + 1, :]
                outs[d][3 * POLAR + 1 :, :] = jnp.zeros((3, h.shape[2]), jnp.float32)


def band_rows(scalars, u, v, h, n):
    levels, _, cols = u.shape

    def spec(d):
        return pl.BlockSpec(
            (pl.Element(1), pl.Element(BAND), pl.Element(cols)),
            lambda i, s: (lax.rem(s[1] + d, n), s[POLAR_AT] * 8, 0),
        )

    rows = 3 * POLAR + 4
    return pl.pallas_call(
        functools.partial(band_kernel, n),
        grid_spec=pltpu.PrefetchScalarGridSpec(
            num_scalar_prefetch=1,
            grid=(1,),
            in_specs=[spec(d) for d in range(n) for _ in range(3)],
            out_specs=[pl.BlockSpec((rows, cols), lambda i, s: (0, 0))] * n,
        ),
        out_shape=[jax.ShapeDtypeStruct((rows, cols), jnp.float32)] * n,
        cost_estimate=cost(3),
        compiler_params=params(),
        name="band_rows",
    )(scalars, *([u, v, h] * n))


def spectrum_kernel(n, s, *refs):
    total = None
    for d in range(n):
        part = dot3(refs[d][...], refs[n + d][0])
        total = part if total is None else total + part
    refs[2 * n][...] = total


def spectra(scalars, pieces, basis):
    n = len(pieces)
    rows, cols = pieces[0].shape
    waves = basis.shape[2]

    def spec(d):
        return pl.BlockSpec((1, cols, waves), lambda i, s: (lax.rem(s[1] + n - d, n), 0, 0))

    return pl.pallas_call(
        functools.partial(spectrum_kernel, n),
        grid_spec=pltpu.PrefetchScalarGridSpec(
            num_scalar_prefetch=1,
            grid=(1,),
            in_specs=[pl.BlockSpec((rows, cols), lambda i, s: (0, 0))] * n + [spec(d) for d in range(n)],
            out_specs=pl.BlockSpec((rows, waves), lambda i, s: (0, 0)),
        ),
        out_shape=jax.ShapeDtypeStruct((rows, waves), jnp.float32),
        cost_estimate=cost(6),
        compiler_params=params(),
        name="spectra",
    )(scalars, *pieces, *([basis] * n))


def pack_kernel(fields, last, s, t_lo, t_hi, h_lo, h_hi, u_lo, u_hi, v_lo, v_hi, west, east):
    lane = lanes()
    count, levels = t_lo.shape[:2]
    gap = last - 2

    def step(i):
        here = eight(i)
        got_w = got_e = None
        for l in range(levels):
            sources = [(t_lo, t_hi, (f, l)) for f in range(count)]
            sources += [(h_lo, h_hi, (l,)), (u_lo, u_hi, (l,)), (v_lo, v_hi, (l,))]
            got = None
            for f, (lo, hi, lead) in enumerate(sources):
                at = lead + (here, slice(None))
                both = jnp.where(lane < LANE // 2, lo[at], hi[at])
                turned = pltpu.roll(both, 2 * f, 1) if f else both
                mine = jnp.logical_or(jnp.logical_and(lane >= 2 * f, lane < LANE // 2), lane >= gap + 2 * f)
                got = jnp.where(mine, turned, got) if f else turned
            base = 2 * fields * l
            to_w = pltpu.roll(got, base, 1) if l else got
            to_e = pltpu.roll(got, (base - gap) % LANE, 1)
            got_w = jnp.where(lane >= base, to_w, got_w) if l else to_w
            got_e = jnp.where(lane >= base, to_e, got_e) if l else to_e
        west[here, :] = got_w
        east[here, :] = got_e

    sweep(0, west.shape[0] // 8, step, 3)


def pack_columns(scalars, tracers, h, u, v):
    count, levels, rows, cols = tracers.shape
    high = (cols - 1) // LANE
    part = rows // 5
    t_spec = [pl.BlockSpec((count, levels, part, LANE), lambda r, s, c=c: (0, 0, r, c)) for c in (0, high)]
    f_spec = [pl.BlockSpec((levels, part, LANE), lambda r, s, c=c: (0, r, c)) for c in (0, high)]
    out = jax.ShapeDtypeStruct((rows, LANE), jnp.float32)
    return pl.pallas_call(
        functools.partial(pack_kernel, count + 3, cols - LANE * high),
        grid_spec=pltpu.PrefetchScalarGridSpec(
            num_scalar_prefetch=1,
            grid=(5,),
            in_specs=t_spec + f_spec * 3,
            out_specs=[pl.BlockSpec((part, LANE), lambda r, s: (r, 0))] * 2,
        ),
        out_shape=[out, out],
        cost_estimate=cost(10),
        compiler_params=params(),
        name="pack_columns",
    )(scalars, tracers, tracers, h, h, u, u, v, v)


def rows_kernel(fields, s, t_top, t_bot, h_top, h_bot, u_top, u_bot, v_top, v_bot,
                e_top, e_bot, w_top, w_bot, pole, facing, top, bot):
    level = pl.program_id(0)
    lane = lanes()
    cols = h_top.shape[2]
    tail = top.shape[2] - LANE
    last = cols - tail
    refs = [(t_top, t_bot, (f, 0)) for f in range(fields - 3)]
    refs += [(h_top, h_bot, (0,)), (u_top, u_bot, (0,)), (v_top, v_bot, (0,))]
    for f in range(fields):
        plane = fields * level + f
        a, b, lead = refs[f]
        top[f, :, 0:cols] = a[lead]
        bot[f, :, 0:cols] = b[lead]
        top[f, :, cols:] = rim_lanes(e_top[...], w_top[...], plane, last, lane)[:, last:]
        bot[f, :, cols:] = rim_lanes(e_bot[...], w_bot[...], plane, last, lane)[:, last:]
    flips = [1.0] * (fields - 1) + [-1.0]

    @pl.when(s[0] == 1)
    def _():
        for f, flip in enumerate(flips):
            pole[0, f, 0:1, :] = flip * top[f, 1:2, :]
            pole[0, f, 1:2, :] = flip * top[f, 0:1, :]
            facing[0, f] = bot[f, 6:8, :]

    @pl.when(s[0] == 0)
    def _():
        for f, flip in enumerate(flips):
            pole[0, f, 0:1, :] = flip * bot[f, 7:8, :]
            pole[0, f, 1:2, :] = flip * bot[f, 6:7, :]
            facing[0, f] = top[f, 0:2, :]


def edge_rows(scalars, tracers, h, u, v, east, west):
    count, levels, rows, cols = tracers.shape
    fields = count + 3
    width = LANE * ((cols - 1) // LANE + 1)
    ends = (0, rows // 8 - 1)
    t_spec = [pl.BlockSpec((count, 1, 8, cols), lambda l, s, r=r: (0, l, r, 0)) for r in ends]
    f_spec = [pl.BlockSpec((1, 8, cols), lambda l, s, r=r: (l, r, 0)) for r in ends]
    c_spec = [pl.BlockSpec((8, LANE), lambda l, s, r=r: (r, 0)) for r in ends]
    out = jax.ShapeDtypeStruct((levels, fields, 2, width), jnp.float32)
    return pl.pallas_call(
        functools.partial(rows_kernel, fields),
        grid_spec=pltpu.PrefetchScalarGridSpec(
            num_scalar_prefetch=1,
            grid=(levels,),
            in_specs=t_spec + f_spec * 3 + c_spec * 2,
            out_specs=[pl.BlockSpec((1, fields, 2, width), lambda l, s: (l, 0, 0, 0))] * 2,
            scratch_shapes=[pltpu.VMEM((fields, 8, width), jnp.float32)] * 2,
        ),
        out_shape=[out, out],
        cost_estimate=cost(7),
        compiler_params=params(),
        name="edge_rows",
    )(scalars, tracers, tracers, h, h, u, u, v, v, east, east, west, west)


def bring_rows(plane, source, target, here, there, rim, count, last):
    (ref, lead), (out, at) = source, target
    for c in range(count - 1):
        out[at + (c, there, slice(None))] = ref[lead + (here, slice(c * LANE, (c + 1) * LANE))]
    out[at + (count - 1, there, slice(0, last))] = ref[lead + (here, slice(LANE * (count - 1), None))]
    out[at + (count - 1, there, slice(last, None))] = rim(plane)[:, last:]


def pressure_rows(level, above, cum, press, h, count, tall):
    def body(i):
        here = eight(i)
        for c in range(count):
            before = jnp.where(level == 0, above[c, here, :], cum[c, here, :])
            now = h[c, here, :]
            press[c, here, :] = before + 0.5 * now
            cum[c, here, :] = before + now

    sweep(0, tall // 8, body, 8)


def gradient(press, row, count, lane):
    p = tiles_at(press, at_row(row), count)
    p_e, p_w = from_east(p, lane), from_west(p, lane)
    p_n, p_s = tiles_at(press, pl.ds(row - 1, 8), count), tiles_at(press, pl.ds(row + 1, 8), count)
    zonal = [GRADIENT_COEF * (p_e[c] - p_w[c]) for c in range(count)]
    return zonal, [GRADIENT_COEF * (p_s[c] - p_n[c]) for c in range(count)]


def column_kernel(fields, s, h, east, west, facing, total):
    lane = lanes()
    levels, rows, cols = h.shape
    count = total.shape[0]
    last = cols - LANE * (count - 1)

    def body(i):
        here, there = eight(i), at_row(8 * i + PAD)
        e, w = east[here, :], west[here, :]
        for c in range(count - 1):
            total[c, there, :] = sum(h[l, here, c * LANE : (c + 1) * LANE] for l in range(levels))
        total[count - 1, there, 0:last] = sum(h[l, here, LANE * (count - 1) :] for l in range(levels))
        rim = sum(rim_lanes(e, w, fields * l + fields - 3, last, lane)[:, last:] for l in range(levels))
        total[count - 1, there, last:] = rim

    sweep(0, rows // 8, body, 5)
    for c in range(count):
        part = slice(c * LANE, (c + 1) * LANE)
        edge = sum(facing[l, fields - 3, :, part] for l in range(levels))
        total[c, PAD - 2 : PAD, :] = edge
        total[c, PAD + rows : PAD + rows + 2, :] = edge


def column_sum(scalars, h, east, west, facing):
    _, rows, cols = h.shape
    count, tall = (cols - 1) // LANE + 1, rows + 2 * PAD
    return pl.pallas_call(
        functools.partial(column_kernel, facing.shape[1]),
        grid_spec=pltpu.PrefetchScalarGridSpec(
            num_scalar_prefetch=1,
            grid=(1,),
            in_specs=[pl.BlockSpec(x.shape, lambda i, s, k=x.ndim: (0,) * k) for x in (h, east, west, facing)],
            out_specs=pl.BlockSpec((count, tall, LANE), lambda i, s: (0, 0, 0)),
        ),
        out_shape=jax.ShapeDtypeStruct((count, tall, LANE), jnp.float32),
        cost_estimate=cost(4),
        compiler_params=params(),
        name="column_sum",
    )(scalars, h, east, west, facing)


def filter_kernel(n, s, *refs):
    pieces = refs[:n]
    above, limits, basis, slope, column, h, u, v, east, west, pole = refs[n : n + 11]
    h0_out, u0_out, v0_out, u1_out, v1_out, h1_out, total = refs[n + 11 : n + 18]
    held, lhs, rhs, cum, press = refs[n + 18 :]
    levels, count, slab = u0_out.shape[:3]
    cols = h.shape[2]
    last = cols - LANE * (count - 1)
    fields = pole.shape[1]
    lane = lanes()

    for l in range(levels):

        def bring(i):
            here, there = eight(i), at_row(8 * (i + s[POLAR_AT + 2]))
            rim_at = eight(i + s[POLAR_AT + 1])
            e, w = east[rim_at, :], west[rim_at, :]
            for f, (ref, out) in enumerate(((h, h0_out), (u, u0_out), (v, v0_out))):
                bring_rows(
                    fields * l + fields - 3 + f, (ref, (l,)), (out, (l,)), here, there,
                    lambda p: rim_lanes(e, w, p, last, lane), count, last,
                )

        sweep(0, BAND // 8 + 1, bring, 9)
        for ends in (True, False):

            @pl.when(s[0] == int(not ends))
            def _():
                at = PAD + BAND if ends else PAD - 2
                for c in range(count):
                    h0_out[l, c, at : at + 2, :] = pole[l, fields - 3, :, c * LANE : (c + 1) * LANE]

        pressure_rows(jnp.int32(l), column, cum, press, h0_out.at[l], count, slab)

        def later(i):
            row = 8 * i
            zonal, merid = gradient(press, row, count, lane)
            for c in range(count):
                u1_out[l, c, at_row(row), :] = u0_out[l, c, at_row(row), :] - zonal[c]
                v1_out[l, c, at_row(row), :] = v0_out[l, c, at_row(row), :] - merid[c]

        sweep(1, slab // 8 - 1, later, 5)

    waves = basis.shape[1]
    for d in range(n):
        held[lax.rem(s[1] + n - d, n)] = pieces[d][...]
    half = waves // 2
    wave = lax.broadcasted_iota(jnp.int32, (POLAR, waves), 1)
    wave = jnp.where(wave < half, wave, wave - half)
    scale = jnp.where(wave == 0, 1.0, 2.0) / (n * cols)
    keep = jnp.where(wave <= limits[0:POLAR, 0:1], scale, 0.0)
    turn = jnp.where(lax.rem(wave[0:2], 2) == 0, 1.0, -1.0)
    one = turn[0:1]
    for north in (True, False):

        @pl.when(s[0] == int(north))
        def _():
            first = PAD if north else PAD + BAND - POLAR
            rim = PAD - 2 if north else PAD + BAND

            def level_step(l, cum):
                u = held[l, 0:POLAR, :] * keep
                v = held[l, POLAR : 2 * POLAR, :] * keep
                thick = held[l, 2 * POLAR : 3 * POLAR + 1, :]
                p = cum + 0.5 * thick
                if north:
                    before = jnp.concatenate([one * p[0:1], p[0 : POLAR - 1]], 0)
                    diff = (p[1:] - before) * keep
                    rhs[0:POLAR, :] = p[0:POLAR] * keep
                else:
                    after = jnp.concatenate([p[2:], one * p[POLAR:]], 0)
                    diff = (after - p[0:POLAR]) * keep
                    rhs[0:POLAR, :] = p[1:] * keep
                w = v - GRADIENT_COEF * diff
                lhs[0:POLAR, :] = u
                lhs[POLAR : 2 * POLAR, :] = v
                lhs[2 * POLAR : 3 * POLAR, :] = w
                for k, (x, sign) in enumerate(((u, 1.0), (v, -1.0), (w, -1.0))):
                    a, b = (x[1:2], x[0:1]) if north else (x[POLAR - 1 :], x[POLAR - 2 : POLAR - 1])
                    at = 3 * POLAR + 2 * k
                    lhs[at : at + 1, :] = sign * one * a
                    lhs[at + 1 : at + 2, :] = sign * one * b
                back = dot3(lhs[...], basis[0])
                grad = dot3(rhs[...], slope[0])
                zonal = back[0:POLAR]
                later = zonal - GRADIENT_COEF * grad[0:POLAR]
                for c in range(count):
                    part = slice(c * LANE, (c + 1) * LANE)
                    u0_out[l, c, first : first + POLAR, :] = zonal[:, part]
                    v0_out[l, c, first : first + POLAR, :] = back[POLAR : 2 * POLAR, part]
                    u1_out[l, c, first : first + POLAR, :] = later[:, part]
                    v1_out[l, c, first : first + POLAR, :] = back[2 * POLAR : 3 * POLAR, part]
                    u0_out[l, c, rim : rim + 2, :] = back[3 * POLAR : 3 * POLAR + 2, part]
                    v0_out[l, c, rim : rim + 2, :] = back[3 * POLAR + 2 : 3 * POLAR + 4, part]
                    v1_out[l, c, rim : rim + 2, :] = back[3 * POLAR + 4 : 3 * POLAR + 6, part]
                return cum + thick

            lax.fori_loop(0, levels, level_step, above[0 : POLAR + 1, :])

    def step(k):
        l, i = k // (slab // 8 - 2), lax.rem(k, slab // 8 - 2) + 1
        here = eight(i)
        new = inflows_at(h0_out, u0_out, v0_out, 8 * i, count, ((l,), (l,)), lane)[4]
        for c in range(count):
            h1_out[l, c, here, :] = new[c]
            total[c, here, :] = jnp.where(l == 0, new[c], total[c, here, :] + new[c])

    sweep(0, levels * (slab // 8 - 2), step, UNROLL["step"])


def filtered_band(scalars, pieces, above, limits, basis, slope, column, h, u, v, east, west, pole):
    n = len(pieces)
    rows, waves = pieces[0].shape
    width = basis.shape[2]
    levels, height, cols = h.shape
    count = column.shape[0]
    slab = BAND + 2 * PAD
    E = pl.Element
    raw = pl.BlockSpec((E(levels), E(BAND + 8), E(cols)), lambda i, s: (0, s[POLAR_AT + 1] * 8, 0))
    out = jax.ShapeDtypeStruct((levels, count, slab, LANE), jnp.float32)
    whole = pl.BlockSpec((levels, count, slab, LANE), lambda i, s: (0, 0, 0, 0))
    return pl.pallas_call(
        functools.partial(filter_kernel, n),
        grid_spec=pltpu.PrefetchScalarGridSpec(
            num_scalar_prefetch=1,
            grid=(1,),
            in_specs=[pl.BlockSpec((rows, waves), lambda i, s: (0, 0))] * n
            + [
                pl.BlockSpec(above.shape, lambda i, s: (0, 0)),
                pl.BlockSpec(limits.shape, lambda i, s: (0, 0)),
                pl.BlockSpec((1, waves, width), lambda i, s: (s[1], 0, 0)),
                pl.BlockSpec((1, waves, width), lambda i, s: (s[1], 0, 0)),
                pl.BlockSpec((E(count), E(slab), E(LANE)), lambda i, s: (0, s[POLAR_AT] * 8, 0)),
            ]
            + [raw] * 3
            + [pl.BlockSpec((height, LANE), lambda i, s: (0, 0))] * 2
            + [pl.BlockSpec(pole.shape, lambda i, s: (0, 0, 0, 0))],
            out_specs=[whole] * 6 + [pl.BlockSpec((count, slab, LANE), lambda i, s: (0, 0, 0))],
            scratch_shapes=[
                pltpu.VMEM((n, rows, waves), jnp.float32),
                pltpu.VMEM((3 * POLAR + 12, waves), jnp.float32),
                pltpu.VMEM((BAND, waves), jnp.float32),
            ]
            + [pltpu.VMEM((count, slab, LANE), jnp.float32)] * 2,
        ),
        out_shape=[out] * 6 + [jax.ShapeDtypeStruct((count, slab, LANE), jnp.float32)],
        cost_estimate=cost(12),
        compiler_params=params(),
        name="filtered_band",
    )(scalars, *pieces, above, limits, basis, slope, column, h, u, v, east, west, pole)


def slab_kernel(fields, group, rows, place, inner, s, *refs):
    if inner:
        tr, h, u, v, above, east, west, rim = refs[:8]
        tr_out, h_out, h1, u1, v1, total = refs[8:14]
        early, late, t0, t1, h0, u0, v0, cum, press = refs[14:]
        lead = ((), ())
        lead_one = (0,)
    else:
        tr, h0, u0, v0, u1, v1, east, west, rim = refs[:9]
        tr_out, h_out = refs[11:13]
        early, late, t0, t1, h1 = refs[13:]
        lead = ((0,), (0,))
        lead_one = ()
    level, part = pl.program_id(0), pl.program_id(1)
    lane = lanes()
    count = early.shape[1]
    cols = h_out.shape[2]
    last = cols - LANE * (count - 1)
    tiles = rows // 8

    def window(i):
        rim_at = eight(i + s[place + 1])
        e, w = east[rim_at, :], west[rim_at, :]
        return eight(i), at_row(8 * (i + s[place + 2])), lambda p: rim_lanes(e, w, p, last, lane)

    def rims(store):
        for ends in (True, False):

            @pl.when(s[place + 3] == int(ends))
            def _():
                at = PAD + rows if ends else PAD - 2
                for c in range(count):
                    store(c, slice(at, at + 2), slice(c * LANE, (c + 1) * LANE))

    def weights_from(target, here, flows, new):
        for c in range(count):
            inv = 1.0 / new[c]
            w = [x[c] * inv for x in flows]
            for k in range(4):
                target[k + 1, c, here, :] = w[k]
            target[0, c, here, :] = 1.0 - ((w[0] + w[1]) + (w[2] + w[3]))

    @pl.when(part == 0)
    def _():
        if inner:

            def bring(i):
                here, there, rim_of = window(i)
                for f, (ref, out) in enumerate(((h, h0), (u, u0), (v, v0))):
                    bring_rows(
                        fields * level + fields - 3 + f, (ref, (0,)), (out, ()), here, there, rim_of, count, last
                    )

            sweep(0, tiles + 1, bring, UNROLL["bring"])

            def store(c, at, part):
                for f, out in enumerate((h0, u0, v0)):
                    out[c, at, :] = rim[0, fields - 3 + f, :, part]

            rims(store)
            pressure_rows(level, above, cum, press, h0, count, rows + 2 * PAD)

        def one(i):
            row = 8 * i + PAD - 8
            there = at_row(row)
            *flows, new = inflows_at(h0, u0, v0, row, count, lead, lane)
            weights_from(early, eight(i), flows, new)
            for c in range(count):
                h1[lead_one + (c, there, slice(None))] = new[c]
            if inner:
                zonal, merid = gradient(press, row, count, lane)
                for c in range(count):
                    total[c, there, :] = jnp.where(level == 0, new[c], total[c, there, :] + new[c])
                    u1[0, c, there, :] = u0[c, there, :] - zonal[c]
                    v1[0, c, there, :] = v0[c, there, :] - merid[c]

        sweep(0, tiles + 2, one, UNROLL["coef"])

        def two(i):
            here = eight(i)
            *flows, new = inflows_at(h1, u1, v1, 8 * i + PAD, count, (lead_one, (0,)), lane)
            weights_from(late, here, flows, new)
            for c in range(count):
                wide = min(LANE, cols - c * LANE)
                h_out[0, here, c * LANE : c * LANE + wide] = new[c][:, 0:wide]

        sweep(0, tiles, two, UNROLL["coef"])

    def bring(i):
        here, there, rim_of = window(i)
        for j in range(group):
            bring_rows(
                fields * level + part * group + j, (tr, (j, 0)), (t0, (j,)), here, there, rim_of, count, last
            )

    sweep(0, tiles + 1, bring, UNROLL["bring"])

    def store(c, at, lanes_of):
        for j in range(group):
            t0[j, c, at, :] = rim[0, part * group + j, :, lanes_of]

    rims(store)

    def advance(source, j, row, weights):
        mid = tiles_at(source, at_row(row), count, (j,))
        up = tiles_at(source, pl.ds(row - 1, 8), count, (j,))
        down = tiles_at(source, pl.ds(row + 1, 8), count, (j,))
        right, left = from_east(mid, lane), from_west(mid, lane)
        return [
            weights[0][c] * mid[c]
            + weights[1][c] * right[c]
            + weights[2][c] * left[c]
            + weights[3][c] * up[c]
            + weights[4][c] * down[c]
            for c in range(count)
        ]

    def one(i):
        weights = [tiles_at(early, eight(i), count, (k,)) for k in range(5)]
        for j in range(group):
            new = advance(t0, j, 8 * i + PAD - 8, weights)
            for c in range(count):
                t1[j, c, at_row(8 * i + PAD - 8), :] = new[c]

    sweep(0, tiles + 2, one, UNROLL["one"])

    def two(i):
        here = eight(i)
        weights = [tiles_at(late, here, count, (k,)) for k in range(5)]
        for j in range(group):
            new = advance(t1, j, 8 * i + PAD, weights)
            for c in range(count):
                wide = min(LANE, cols - c * LANE)
                tr_out[j, 0, here, c * LANE : c * LANE + wide] = new[c][:, 0:wide]

    sweep(0, tiles, two, UNROLL["two"])


def tracer_slab(scalars, place, rows, group, tracers, fields, east, west, rim, base, micros, name):
    count, levels, height, cols = tracers.shape
    tiles = (cols - 1) // LANE + 1
    slab = rows + 2 * PAD
    inner = base is None
    E = pl.Element
    slabs = pl.BlockSpec((1, tiles, slab, LANE), lambda l, g, s: (l, 0, 0, 0))
    flat = pl.BlockSpec((tiles, slab, LANE), lambda l, g, s: (0, 0, 0))
    in_specs = [
        pl.BlockSpec(
            (E(group), E(1), E(rows + 8), E(cols)), lambda l, g, s: (g * group, l, s[place + 1] * 8, 0)
        )
    ]
    if inner:
        in_specs += [pl.BlockSpec((E(1), E(rows + 8), E(cols)), lambda l, g, s: (l, s[place + 1] * 8, 0))] * 3
        in_specs += [pl.BlockSpec((E(tiles), E(slab), E(LANE)), lambda l, g, s: (0, s[place] * 8, 0))]
    else:
        in_specs += [slabs] * 5
    in_specs += [pl.BlockSpec((height, LANE), lambda l, g, s: (0, 0))] * 2
    in_specs += [pl.BlockSpec((1,) + rim.shape[1:], lambda l, g, s: (l, 0, 0, 0))]
    operands = [tracers, *fields, east, west, rim]
    out_specs = [
        pl.BlockSpec((E(group), E(1), E(rows), E(cols)), lambda l, g, s: (g * group, l, s[place] * 8, 0)),
        pl.BlockSpec((E(1), E(rows), E(cols)), lambda l, g, s: (l, s[place] * 8, 0)),
    ]
    out_shape = [
        jax.ShapeDtypeStruct(tracers.shape, jnp.float32),
        jax.ShapeDtypeStruct((levels, height, cols), jnp.float32),
    ]
    scratch = [
        pltpu.VMEM((5, tiles, rows + 16, LANE), jnp.float32),
        pltpu.VMEM((5, tiles, rows, LANE), jnp.float32),
        pltpu.VMEM((group, tiles, slab, LANE), jnp.float32),
        pltpu.VMEM((group, tiles, slab, LANE), jnp.float32),
    ]
    plane = pltpu.VMEM((tiles, slab, LANE), jnp.float32)
    aliases = {}
    if inner:
        out_specs += [slabs] * 3 + [flat]
        out_shape += [jax.ShapeDtypeStruct((levels, tiles, slab, LANE), jnp.float32)] * 3
        out_shape += [jax.ShapeDtypeStruct((tiles, slab, LANE), jnp.float32)]
        scratch += [plane] * 5
    else:
        in_specs += [pl.BlockSpec(memory_space=pl.ANY)] * 2
        operands += list(base)
        aliases = {len(operands) - 1: 0, len(operands): 1}
        scratch += [plane]
    return pl.pallas_call(
        functools.partial(slab_kernel, rim.shape[1], group, rows, place, inner),
        grid_spec=pltpu.PrefetchScalarGridSpec(
            num_scalar_prefetch=1,
            grid=(levels, count // group),
            in_specs=in_specs,
            out_specs=out_specs,
            scratch_shapes=scratch,
        ),
        out_shape=out_shape,
        input_output_aliases=aliases,
        cost_estimate=cost(micros),
        compiler_params=params(),
        name=name,
    )(scalars, *operands)


def winds_kernel(s, *refs):
    u_out, v_out = refs[8:10]
    lane = lanes()
    cols = u_out.shape[2]
    for k, place in enumerate((MIDDLE_AT, POLAR_AT)):
        h, u, v, above = refs[4 * k : 4 * k + 4]
        cum, press = refs[10 + 2 * k : 12 + 2 * k]
        count, slab = h.shape[1:3]
        pressure_rows(pl.program_id(0), above, cum, press, h.at[0], count, slab)

        def step(i):
            row = 8 * i + PAD
            to = eight(i + s[place])
            zonal, merid = gradient(press, row, count, lane)
            for c in range(count):
                wide = min(LANE, cols - c * LANE)
                part = slice(c * LANE, c * LANE + wide)
                u_out[0, to, part] = (u[0, c, at_row(row), :] - zonal[c])[:, 0:wide]
                v_out[0, to, part] = (v[0, c, at_row(row), :] - merid[c])[:, 0:wide]

        sweep(0, slab // 8 - 4, step, UNROLL["step"])


def last_winds(scalars, slabs, rows, cols):
    levels, tiles = slabs[0][0].shape[:2]
    in_specs, scratch = [], []
    for h, _, _, _ in slabs:
        tall = h.shape[2]
        in_specs += [pl.BlockSpec((1, tiles, tall, LANE), lambda l, s: (l, 0, 0, 0))] * 3
        in_specs += [pl.BlockSpec((tiles, tall, LANE), lambda l, s: (0, 0, 0))]
        scratch += [pltpu.VMEM((tiles, tall, LANE), jnp.float32)] * 2
    out = jax.ShapeDtypeStruct((levels, rows, cols), jnp.float32)
    return pl.pallas_call(
        winds_kernel,
        grid_spec=pltpu.PrefetchScalarGridSpec(
            num_scalar_prefetch=1,
            grid=(levels,),
            in_specs=in_specs,
            out_specs=[pl.BlockSpec((1, rows, cols), lambda l, s: (l, 0, 0))] * 2,
            scratch_shapes=scratch,
        ),
        out_shape=[out, out],
        cost_estimate=cost(8),
        compiler_params=params(),
        name="last_winds",
    )(scalars, *slabs[0], *slabs[1])


def bases(n, cols):
    total = n * cols
    wave = np.arange(KMAX + 1)
    cell = np.arange(total).reshape(n, cols)
    angle = (cell[:, :, None] * wave % total) * (2.0 * math.pi / total)
    forward = np.concatenate([np.cos(angle), np.sin(angle)], 2)
    width = LANE * ((cols - 1) // LANE + 1)
    lane = np.arange(width)
    lane = np.where(lane < width - 2, lane, lane - width)
    cell = np.arange(n)[:, None] * cols + lane[None, :]
    angle = (cell[:, None, :] * wave[:, None] % total) * (2.0 * math.pi / total)
    inverse = np.concatenate([np.cos(angle), np.sin(angle)], 1)
    steep = 2.0 * np.sin(wave * (2.0 * math.pi / total))[:, None]
    slope = np.concatenate([-steep * np.sin(angle), steep * np.cos(angle)], 1)
    return [jnp.asarray(x.astype(np.float32)) for x in (forward, inverse, slope)]


def shards_tiled(tracers, thickness, zonal, meridional, cutoff):
    count, levels, rows, cols = tracers.shape
    n = lax.axis_size("lon")
    me = lax.axis_index("lon").astype(jnp.int32)
    is_north = lax.axis_index("lat") == 0
    inner = rows - BAND

    band_at = rows // 8 - BAND // 8
    scalars = jnp.where(
        is_north,
        jnp.array([1, 0, 0, 0, PAD // 8, 0, BAND // 8, BAND // 8 - 1, PAD // 8 - 1, 1], jnp.int32),
        jnp.array([0, 0, band_at, band_at - 1, PAD // 8 - 1, 1, 0, 0, PAD // 8, 0], jnp.int32),
    )
    scalars = scalars + jnp.where(jnp.arange(10) == 1, me, 0)
    forward, inverse, slope = bases(n, cols)
    limits = jnp.where(is_north, cutoff[0], cutoff[1])
    limits = jnp.broadcast_to(jnp.pad(limits, (0, BAND - POLAR))[:, None], (BAND, LANE))

    def along(value, d):
        return lax.ppermute(value, "lon", [(i, (i + d) % n) for i in range(n)])

    def to_lower(value):
        return lax.ppermute(value, "lev", [(0, 1)])

    sent = band_rows(scalars, zonal, meridional, thickness, n)
    scalars, sent = lax.optimization_barrier((scalars, sent))
    pieces = [sent[0]] + [along(sent[d], d) for d in range(1, n)]
    packed = pack_columns(scalars, tracers, thickness, zonal, meridional)
    scalars, packed = lax.optimization_barrier((scalars, packed))
    east, west = along(packed[0], n - 1), along(packed[1], 1)

    own = spectra(scalars, pieces, forward)
    scalars, own = lax.optimization_barrier((scalars, own))
    pieces = [own] + [along(own, d) for d in range(1, n)]

    pole, facing = edge_rows(scalars, tracers, thickness, zonal, meridional, east, west)
    facing = lax.ppermute(facing, "lat", [(0, 1), (1, 0)])
    pole = along(pole, n // 2)
    column = column_sum(scalars, thickness, east, west, facing)
    column = to_lower(column)
    tr, h2, h1, u1, v1, total = tracer_slab(
        scalars, MIDDLE_AT, inner, 5, tracers, (thickness, zonal, meridional, column), east, west, facing, None,
        50, "tracers_inner",
    )
    scalars, total, pieces = lax.optimization_barrier((scalars, total, pieces))
    total = to_lower(total)
    above_band = to_lower(sum(p[2 * POLAR :] for p in pieces))
    h0, u0, v0, u1b, v1b, h1b, band_total = filtered_band(
        scalars, pieces, above_band, limits, inverse, slope, column, thickness, zonal, meridional, east, west, pole
    )
    band_total = to_lower(band_total)
    tr, h2 = tracer_slab(
        scalars, POLAR_AT, BAND, 10, tracers, (h0, u0, v0, u1b, v1b), east, west, pole, (tr, h2), 13,
        "tracers_polar",
    )
    u2, v2 = last_winds(scalars, ((h1, u1, v1, total), (h1b, u1b, v1b, band_total)), rows, cols)
    return (tr, h2, u2, v2)


def tiles_fit(mesh, tracers):
    count, levels, rows, cols = tracers.shape
    rows, cols = rows // mesh.shape["lat"], cols // mesh.shape["lon"]
    count, levels = count // mesh.shape["member"], levels // mesh.shape["lev"]
    last = (cols - 1) % LANE + 1
    return (
        mesh.shape["lat"] == 2
        and mesh.shape["lev"] == 2
        and levels == mesh.shape["lon"]
        and mesh.shape["lon"] % 2 == 0
        and rows % 40 == 0
        and rows >= 2 * BAND + 8
        and last + 4 <= LANE
        and last - 2 >= LANE // 2
        and last + 2 * (count + 2) <= LANE
        and cols > LANE
        and 2 * (count + 3) * levels <= LANE
        and count % 5 == 0
    )


def solution(mesh):
    placed = (
        P("member", "lev", "lat", "lon"),
        P(("member", "lev"), "lat", "lon"),
        P(("member", "lev"), "lat", "lon"),
        P(("member", "lev"), "lat", "lon"),
        P(),
    )
    outs = (
        P("member", "lev", "lat", "lon"),
        P(("member", "lev"), "lat", "lon"),
        P(("member", "lev"), "lat", "lon"),
        P(("member", "lev"), "lat", "lon"),
    )

    def program(*args):
        part = shards_tiled if tiles_fit(mesh, args[0]) else shards
        return jax.shard_map(part, mesh=mesh, in_specs=placed, out_specs=outs, check_vma=False)(*args)

    return program
```

```python
import functools
import math

import jax
import jax.numpy as jnp
import numpy as np
from jax import lax
from jax.experimental import pallas as pl
from jax.experimental.pallas import tpu as pltpu
from jax.sharding import PartitionSpec as P

NSUB = 2
POLAR = 60
KMAX = 191


COURANT_CAP = 0.15
GRADIENT_COEF = 0.1


def extended_2(block, sides, width):
    for axis, dim in sides:
        count = lax.axis_size(axis)
        forward = [(i, i + 1) for i in range(count - 1)]
        forward.append((count - 1, 0))
        backward = [(target, source) for source, target in forward]
        low = lax.ppermute(
            lax.slice_in_dim(block, block.shape[dim] - width, None, axis=dim), axis, forward
        )
        high = lax.ppermute(lax.slice_in_dim(block, 0, width, axis=dim), axis, backward)
        block = jnp.concatenate([low, block, high], axis=dim)
    return block


def shifted(block, axis, distance):
    devices = range(lax.axis_size(axis))
    route = [((i - distance) % len(devices), i) for i in devices]
    return lax.ppermute(block, axis, route)


def entering(value, axis, join, neutral):
    count, mine = (lax.axis_size(axis), lax.axis_index(axis))
    pieces = lax.all_gather(value, axis)
    running = jnp.full_like(value, 0) + jnp.asarray(neutral, value.dtype)

    def step(position, running):
        longer = join(running, pieces[position])
        return jnp.where(position < mine, longer, running)

    return lax.fori_loop(0, count - 1, step, running)


def advance_level(extended, pressure):
    tracer_count = extended.shape[0] - 3
    thick = extended[tracer_count]
    east_wind = extended[tracer_count + 1]
    north_wind = extended[tracer_count + 2]
    masses = jnp.concatenate([thick[None], extended[:tracer_count] * thick[None]], 0)
    east_courant = COURANT_CAP * jnp.tanh(0.5 * (east_wind[1:-1, :-1] + east_wind[1:-1, 1:]))
    east_flux = (
        jnp.maximum(east_courant, 0.0) * masses[:, 1:-1, :-1]
        + jnp.minimum(east_courant, 0.0) * masses[:, 1:-1, 1:]
    )
    south_courant = COURANT_CAP * jnp.tanh(0.5 * (north_wind[:-1, 1:-1] + north_wind[1:, 1:-1]))
    south_flux = (
        jnp.maximum(south_courant, 0.0) * masses[:, :-1, 1:-1]
        + jnp.minimum(south_courant, 0.0) * masses[:, 1:, 1:-1]
    )
    updated = (
        masses[:, 1:-1, 1:-1]
        - (east_flux[:, :, 1:] - east_flux[:, :, :-1])
        - (south_flux[:, 1:] - south_flux[:, :-1])
    )
    new_thick = updated[0]
    new_mixing = updated[1:] / new_thick[None]
    new_east = east_wind[1:-1, 1:-1] - GRADIENT_COEF * (pressure[1:-1, 2:] - pressure[1:-1, :-2])
    new_north = north_wind[1:-1, 1:-1] - GRADIENT_COEF * (pressure[2:, 1:-1] - pressure[:-2, 1:-1])
    return (new_mixing, new_thick, new_east, new_north)


def wave_basis(anchor, length, lon_total):
    cells = anchor + jnp.arange(length, dtype=jnp.int32)
    waves = jnp.arange(KMAX + 1, dtype=jnp.int32)
    phase = (cells[:, None] * waves[None, :] % lon_total).astype(jnp.float32) * (
        2.0 * math.pi / lon_total
    )
    return jnp.concatenate([jnp.cos(phase), jnp.sin(phase)], 1)


def wave_weights(limits, lon_total):
    waves = jnp.arange(KMAX + 1, dtype=jnp.int32)
    scaled = jnp.where(waves == 0, 1.0, 2.0).astype(jnp.float32) / lon_total
    kept = jnp.where(waves[None, :] <= limits[:, None], scaled[None, :], 0.0)
    return jnp.concatenate([kept, kept], 1)


def smooth_winds(zonal, meridional, cutoff, is_north, is_south):
    level_count, row_count, col_count = zonal.shape
    lon_count = lax.axis_size("lon")
    lon_total = col_count * lon_count
    north_rows = jnp.stack([zonal[:, :POLAR], meridional[:, :POLAR]], 0)
    south_rows = jnp.stack([zonal[:, row_count - POLAR :], meridional[:, row_count - POLAR :]], 0)
    selected = jnp.where(is_north, north_rows, south_rows).reshape(-1, col_count)
    limits = jnp.tile(jnp.where(is_north, cutoff[0], cutoff[1]), 2 * level_count)
    fragment = lax.all_gather(selected, "lon", axis=1, tiled=True)
    basis = wave_basis(jnp.int32(0), fragment.shape[1], lon_total)
    spectrum = jnp.dot(
        fragment, basis, precision=lax.Precision.HIGHEST, preferred_element_type=jnp.float32
    )
    own_basis = wave_basis(lax.axis_index("lon") * col_count, col_count, lon_total)
    filtered = jnp.dot(
        spectrum * wave_weights(limits, lon_total),
        own_basis.T,
        precision=lax.Precision.HIGHEST,
        preferred_element_type=jnp.float32,
    )
    filtered = filtered.reshape(2, level_count, POLAR, col_count)
    row_start = jnp.where(is_north, 0, row_count - POLAR).astype(jnp.int32)
    polar_band = jnp.logical_or(is_north, is_south)
    new_zonal = lax.dynamic_update_slice_in_dim(zonal, filtered[0], row_start, 1)
    new_merid = lax.dynamic_update_slice_in_dim(meridional, filtered[1], row_start, 1)
    return (jnp.where(polar_band, new_zonal, zonal), jnp.where(polar_band, new_merid, meridional))


def shards(tracers, thickness, zonal, meridional, cutoff):
    tracer_count = tracers.shape[0]
    lat_index = lax.axis_index("lat")
    is_north = lat_index == 0
    is_south = lat_index == lax.axis_size("lat") - 1
    lon_count = lax.axis_size("lon")
    flip_sign = jnp.concatenate(
        [jnp.ones((tracer_count + 1,), jnp.float32), -jnp.ones((2,), jnp.float32)]
    )[:, None, None]
    advance_all = jax.vmap(advance_level, in_axes=(1, 0), out_axes=(1, 0, 0, 0))
    for substep in range(NSUB):
        zonal, meridional = smooth_winds(zonal, meridional, cutoff, is_north, is_south)
        state = jnp.concatenate([tracers, thickness[None], zonal[None], meridional[None]], 0)
        extended = extended_2(state, (("lat", 2), ("lon", 3)), 1)
        edges = jnp.stack([state[:, :, 0], state[:, :, -1]], 2)
        opposite = shifted(edges, "lon", lon_count // 2)
        north_rim = jnp.where(is_north, opposite[:, :, 0] * flip_sign, extended[:, :, 0, 1:-1])
        south_rim = jnp.where(is_south, opposite[:, :, 1] * flip_sign, extended[:, :, -1, 1:-1])
        extended = extended.at[:, :, 0, 1:-1].set(north_rim)
        extended = extended.at[:, :, -1, 1:-1].set(south_rim)
        thick_ext = extended[tracer_count]
        column_above = entering(
            jnp.sum(thick_ext, 0),
            "lev",
            lambda earlier, later: earlier + later,
            jnp.zeros(thick_ext.shape[1:], jnp.float32),
        )
        pressure = jnp.cumsum(thick_ext, axis=0) - 0.5 * thick_ext + column_above[None]
        tracers, thickness, zonal, meridional = advance_all(extended, pressure)
    return (tracers, thickness, zonal, meridional)


LANE = 128
POLAR_AT, MIDDLE_AT = 2, 6
UNROLL = dict(step=13, bring=13, coef=8, one=13, two=12)
PAD = 16
BAND = 64


def cost(micros):
    return pl.CostEstimate(flops=0, bytes_accessed=int(micros * 3.3e6), transcendentals=0)


def params(mib=56):
    return pltpu.CompilerParams(vmem_limit_bytes=mib * 1024 * 1024)


HELD = pl.BlockSpec(memory_space=pltpu.VMEM)


def lanes():
    return lax.broadcasted_iota(jnp.int32, (8, LANE), 1)


def at_row(row):
    return pl.ds(row if isinstance(row, int) else pl.multiple_of(row, 8), 8)


def eight(index):
    return at_row(8 * index)


def from_east(tiles, lane):
    turned = [pltpu.roll(t, LANE - 1, 1) for t in tiles]
    n = len(tiles)
    return [jnp.where(lane < LANE - 1, turned[c], turned[(c + 1) % n]) for c in range(n)]


def from_west(tiles, lane):
    turned = [pltpu.roll(t, 1, 1) for t in tiles]
    n = len(tiles)
    return [jnp.where(lane > 0, turned[c], turned[(c - 1) % n]) for c in range(n)]


def courant(a, b):
    return COURANT_CAP * jnp.tanh(0.5 * (a + b))


def rim_lanes(east, west, plane, last, lane):
    both = jnp.where(lane < 2 * plane + 2, east, west)
    return pltpu.roll(both, lax.rem(last + LANE - 2 * plane, LANE), 1)


def inflows(h, u, v, h_n, h_s, v_n, v_s, lane):
    count = range(len(h))
    u_e, h_e = from_east(u, lane), from_east(h, lane)
    c_e = [courant(u[c], u_e[c]) for c in count]
    out_e = [jnp.maximum(c_e[c], 0.0) * h[c] for c in count]
    in_e = [jnp.maximum(-c_e[c], 0.0) * h_e[c] for c in count]
    in_w, out_w = from_west(out_e, lane), from_west(in_e, lane)
    c_s = [courant(v[c], v_s[c]) for c in count]
    c_n = [courant(v_n[c], v[c]) for c in count]
    in_s = [jnp.maximum(-c_s[c], 0.0) * h_s[c] for c in count]
    out_s = [jnp.maximum(c_s[c], 0.0) * h[c] for c in count]
    in_n = [jnp.maximum(c_n[c], 0.0) * h_n[c] for c in count]
    out_n = [jnp.maximum(-c_n[c], 0.0) * h[c] for c in count]
    new = [
        h[c] - (out_e[c] - in_e[c]) + (in_w[c] - out_w[c]) - (out_s[c] - in_s[c]) + (in_n[c] - out_n[c])
        for c in count
    ]
    return in_e, in_w, in_n, in_s, new


def halves(x):
    high = x.astype(jnp.bfloat16)
    return high, (x - high.astype(jnp.float32)).astype(jnp.bfloat16)


def dot3(a, b):
    (a_hi, a_lo), (b_hi, b_lo) = halves(a), halves(b)

    def one(x, y):
        return jnp.dot(x, y, preferred_element_type=jnp.float32)

    return one(a_hi, b_hi) + (one(a_hi, b_lo) + one(a_lo, b_hi))


def sweep(first, end, body, depth):
    whole = (end - first) // depth

    def step(k, _):
        for j in range(depth):
            body(first + k * depth + j)
        return 0

    lax.fori_loop(0, whole, step, 0)
    for i in range(first + whole * depth, end):
        body(i)


def tiles_at(ref, base, count, lead=()):
    return [ref[lead + (c, base, slice(None))] for c in range(count)]


def inflows_at(h, u, v, row, count, lead, lane):
    mid = at_row(row)
    up, down = pl.ds(row - 1, 8), pl.ds(row + 1, 8)
    hl, vl = lead
    return inflows(
        tiles_at(h, mid, count, hl),
        tiles_at(u, mid, count, vl),
        tiles_at(v, mid, count, vl),
        tiles_at(h, up, count, hl),
        tiles_at(h, down, count, hl),
        tiles_at(v, up, count, vl),
        tiles_at(v, down, count, vl),
        lane,
    )


def band_kernel(n, s, *refs):
    ins, outs = refs[: 3 * n], refs[3 * n :]
    for north in (True, False):

        @pl.when(s[0] == int(north))
        def _():
            lo = 0 if north else BAND - POLAR
            for d in range(n):
                u, v, h = ins[3 * d : 3 * d + 3]
                outs[d][0:POLAR, :] = u[0, lo : lo + POLAR, :]
                outs[d][POLAR : 2 * POLAR, :] = v[0, lo : lo + POLAR, :]
                first = 0 if north else BAND - POLAR - 1
                outs[d][2 * POLAR : 3 * POLAR + 1, :] = h[0, first : first + POLAR + 1, :]
                outs[d][3 * POLAR + 1 :, :] = jnp.zeros((3, h.shape[2]), jnp.float32)


def band_rows(scalars, u, v, h, n):
    levels, _, cols = u.shape

    def spec(d):
        return pl.BlockSpec(
            (pl.Element(1), pl.Element(BAND), pl.Element(cols)),
            lambda i, s: (lax.rem(s[1] + d, n), s[POLAR_AT] * 8, 0),
        )

    rows = 3 * POLAR + 4
    return pl.pallas_call(
        functools.partial(band_kernel, n),
        grid_spec=pltpu.PrefetchScalarGridSpec(
            num_scalar_prefetch=1,
            grid=(1,),
            in_specs=[spec(d) for d in range(n) for _ in range(3)],
            out_specs=[pl.BlockSpec((rows, cols), lambda i, s: (0, 0))] * n,
        ),
        out_shape=[jax.ShapeDtypeStruct((rows, cols), jnp.float32)] * n,
        cost_estimate=cost(3),
        compiler_params=params(),
        name="band_rows",
    )(scalars, *([u, v, h] * n))


def spectrum_kernel(n, s, *refs):
    total = None
    for d in range(n):
        part = dot3(refs[d][...], refs[n + d][0])
        total = part if total is None else total + part
    refs[2 * n][...] = total


def spectra(scalars, pieces, basis):
    n = len(pieces)
    rows, cols = pieces[0].shape
    waves = basis.shape[2]

    def spec(d):
        return pl.BlockSpec((1, cols, waves), lambda i, s: (lax.rem(s[1] + n - d, n), 0, 0))

    return pl.pallas_call(
        functools.partial(spectrum_kernel, n),
        grid_spec=pltpu.PrefetchScalarGridSpec(
            num_scalar_prefetch=1,
            grid=(1,),
            in_specs=[HELD] * n + [spec(d) for d in range(n)],
            out_specs=pl.BlockSpec((rows, waves), lambda i, s: (0, 0)),
        ),
        out_shape=jax.ShapeDtypeStruct((rows, waves), jnp.float32),
        cost_estimate=cost(6),
        compiler_params=params(),
        name="spectra",
    )(scalars, *pieces, *([basis] * n))


def pack_kernel(fields, last, s, t_lo, t_hi, h_lo, h_hi, u_lo, u_hi, v_lo, v_hi, west, east):
    lane = lanes()
    count, levels = t_lo.shape[:2]
    gap = last - 2

    def step(i):
        here = eight(i)
        got_w = got_e = None
        for l in range(levels):
            sources = [(t_lo, t_hi, (f, l)) for f in range(count)]
            sources += [(h_lo, h_hi, (l,)), (u_lo, u_hi, (l,)), (v_lo, v_hi, (l,))]
            got = None
            for f, (lo, hi, lead) in enumerate(sources):
                at = lead + (here, slice(None))
                both = jnp.where(lane < LANE // 2, lo[at], hi[at])
                turned = pltpu.roll(both, 2 * f, 1) if f else both
                mine = jnp.logical_or(jnp.logical_and(lane >= 2 * f, lane < LANE // 2), lane >= gap + 2 * f)
                got = jnp.where(mine, turned, got) if f else turned
            base = 2 * fields * l
            to_w = pltpu.roll(got, base, 1) if l else got
            to_e = pltpu.roll(got, (base - gap + LANE - 2 - last) % LANE, 1)
            got_w = jnp.where(lane >= base, to_w, got_w) if l else to_w
            got_e = jnp.where(lane >= base + LANE - 2 - last, to_e, got_e) if l else to_e
        west[here, :] = got_w
        east[here, :] = got_e

    sweep(0, west.shape[0] // 8, step, 3)


def pack_columns(scalars, tracers, h, u, v):
    count, levels, rows, cols = tracers.shape
    high = (cols - 1) // LANE
    part = rows // 5
    t_spec = [pl.BlockSpec((count, levels, part, LANE), lambda r, s, c=c: (0, 0, r, c)) for c in (0, high)]
    f_spec = [pl.BlockSpec((levels, part, LANE), lambda r, s, c=c: (0, r, c)) for c in (0, high)]
    out = jax.ShapeDtypeStruct((rows, LANE), jnp.float32)
    return pl.pallas_call(
        functools.partial(pack_kernel, count + 3, cols - LANE * high),
        grid_spec=pltpu.PrefetchScalarGridSpec(
            num_scalar_prefetch=1,
            grid=(5,),
            in_specs=t_spec + f_spec * 3,
            out_specs=[pl.BlockSpec((part, LANE), lambda r, s: (r, 0))] * 2,
        ),
        out_shape=[out, out],
        cost_estimate=cost(10),
        compiler_params=params(),
        name="pack_columns",
    )(scalars, tracers, tracers, h, h, u, u, v, v)


def rows_kernel(fields, s, t_top, t_bot, h_top, h_bot, u_top, u_bot, v_top, v_bot,
                east, west, pole, facing, top, bot):
    level = pl.program_id(0)
    lane = lanes()
    cols = h_top.shape[2]
    tail = top.shape[2] - LANE
    last = cols - tail
    height = east.shape[0]
    e_top, e_bot = east[0:8, :], east[height - 8 :, :]
    w_top, w_bot = west[0:8, :], west[height - 8 :, :]
    refs = [(t_top, t_bot, (f, 0)) for f in range(fields - 3)]
    refs += [(h_top, h_bot, (0,)), (u_top, u_bot, (0,)), (v_top, v_bot, (0,))]
    for f in range(fields):
        plane = fields * level + f
        a, b, lead = refs[f]
        top[f, :, 0:cols] = a[lead]
        bot[f, :, 0:cols] = b[lead]
        top[f, :, cols:] = rim_lanes(e_top, w_top, plane, last, lane)[:, last:]
        bot[f, :, cols:] = rim_lanes(e_bot, w_bot, plane, last, lane)[:, last:]
    flips = [1.0] * (fields - 1) + [-1.0]

    @pl.when(s[0] == 1)
    def _():
        for f, flip in enumerate(flips):
            pole[0, f, 0:1, :] = flip * top[f, 1:2, :]
            pole[0, f, 1:2, :] = flip * top[f, 0:1, :]
            facing[0, f] = bot[f, 6:8, :]

    @pl.when(s[0] == 0)
    def _():
        for f, flip in enumerate(flips):
            pole[0, f, 0:1, :] = flip * bot[f, 7:8, :]
            pole[0, f, 1:2, :] = flip * bot[f, 6:7, :]
            facing[0, f] = top[f, 0:2, :]


def edge_rows(scalars, tracers, h, u, v, east, west):
    count, levels, rows, cols = tracers.shape
    fields = count + 3
    width = LANE * ((cols - 1) // LANE + 1)
    ends = (0, rows // 8 - 1)
    t_spec = [pl.BlockSpec((count, 1, 8, cols), lambda l, s, r=r: (0, l, r, 0)) for r in ends]
    f_spec = [pl.BlockSpec((1, 8, cols), lambda l, s, r=r: (l, r, 0)) for r in ends]
    out = jax.ShapeDtypeStruct((levels, fields, 2, width), jnp.float32)
    return pl.pallas_call(
        functools.partial(rows_kernel, fields),
        grid_spec=pltpu.PrefetchScalarGridSpec(
            num_scalar_prefetch=1,
            grid=(levels,),
            in_specs=t_spec + f_spec * 3 + [HELD] * 2,
            out_specs=[pl.BlockSpec((1, fields, 2, width), lambda l, s: (l, 0, 0, 0))] * 2,
            scratch_shapes=[pltpu.VMEM((fields, 8, width), jnp.float32)] * 2,
        ),
        out_shape=[out, out],
        cost_estimate=cost(4),
        compiler_params=params(),
        name="edge_rows",
    )(scalars, tracers, tracers, h, h, u, u, v, v, east, west)


def bring_rows(plane, source, target, here, there, rim, count, last):
    (ref, lead), (out, at) = source, target
    for c in range(count - 1):
        out[at + (c, there, slice(None))] = ref[lead + (here, slice(c * LANE, (c + 1) * LANE))]
    out[at + (count - 1, there, slice(0, last))] = ref[lead + (here, slice(LANE * (count - 1), None))]
    out[at + (count - 1, there, slice(last, None))] = rim(plane)[:, last:]


def pressure_rows(level, above, cum, press, h, count, tall):
    def body(i):
        here = eight(i)
        for c in range(count):
            before = jnp.where(level == 0, above[c, here, :], cum[c, here, :])
            now = h[c, here, :]
            press[c, here, :] = before + 0.5 * now
            cum[c, here, :] = before + now

    sweep(0, tall // 8, body, 8)


def gradient(press, row, count, lane):
    p = tiles_at(press, at_row(row), count)
    p_e, p_w = from_east(p, lane), from_west(p, lane)
    p_n, p_s = tiles_at(press, pl.ds(row - 1, 8), count), tiles_at(press, pl.ds(row + 1, 8), count)
    zonal = [GRADIENT_COEF * (p_e[c] - p_w[c]) for c in range(count)]
    return zonal, [GRADIENT_COEF * (p_s[c] - p_n[c]) for c in range(count)]


def column_kernel(h, total):
    levels, rows, cols = h.shape
    count = total.shape[0]

    def body(i):
        here, there = eight(i), at_row(8 * i + PAD)
        for c in range(count):
            wide = min(LANE, cols - c * LANE)
            part = slice(c * LANE, c * LANE + wide)
            total[c, there, 0:wide] = sum(h[l, here, part] for l in range(levels))

    sweep(0, rows // 8, body, 9)


def column_sum(h):
    _, rows, cols = h.shape
    shape = ((cols - 1) // LANE + 1, rows + 2 * PAD, LANE)
    return pl.pallas_call(
        column_kernel,
        out_shape=jax.ShapeDtypeStruct(shape, jnp.float32),
        in_specs=[pl.BlockSpec(memory_space=pltpu.VMEM)],
        out_specs=pl.BlockSpec(memory_space=pltpu.VMEM),
        cost_estimate=cost(3),
        compiler_params=params(),
        name="column_sum",
    )(h)


def rims_kernel(fields, cols, s, own, east, west, facing, total):
    lane = lanes()
    levels, rows = facing.shape[0], east.shape[0]
    count = total.shape[0]
    last = cols - LANE * (count - 1)
    total[0 : count - 1] = own[0 : count - 1]

    def body(i):
        here, there = eight(i), at_row(8 * i + PAD)
        e, w = east[here, :], west[here, :]
        rim = sum(rim_lanes(e, w, fields * l + fields - 3, last, lane) for l in range(levels))
        total[count - 1, there, :] = jnp.where(lane < last, own[count - 1, there, :], rim)

    sweep(0, rows // 8, body, 9)
    for c in range(count):
        part = slice(c * LANE, (c + 1) * LANE)
        edge = sum(facing[l, fields - 3, :, part] for l in range(levels))
        total[c, PAD - 2 : PAD, :] = edge
        total[c, PAD + rows : PAD + rows + 2, :] = edge


def column_rims(scalars, own, cols, east, west, facing):
    return pl.pallas_call(
        functools.partial(rims_kernel, facing.shape[1], cols),
        grid_spec=pltpu.PrefetchScalarGridSpec(
            num_scalar_prefetch=1,
            grid=(1,),
            in_specs=[HELD] * 4,
            out_specs=pl.BlockSpec(own.shape, lambda i, s: (0, 0, 0)),
        ),
        out_shape=jax.ShapeDtypeStruct(own.shape, jnp.float32),
        cost_estimate=cost(2),
        compiler_params=params(),
        name="column_rims",
    )(scalars, own, east, west, facing)


def filter_kernel(n, s, *refs):
    pieces = refs[:n]
    above, limits, basis, slope, column, h, u, v, east, west, pole = refs[n : n + 11]
    h0_out, u0_out, v0_out, u1_out, v1_out, h1_out, total = refs[n + 11 : n + 18]
    held, lhs, rhs, cum, press = refs[n + 18 :]
    levels, count, slab = u0_out.shape[:3]
    cols = h.shape[2]
    last = cols - LANE * (count - 1)
    fields = pole.shape[1]
    lane = lanes()

    for l in range(levels):

        def bring(i):
            here, there = eight(i), at_row(8 * (i + s[POLAR_AT + 2]))
            rim_at = eight(i + s[POLAR_AT + 1])
            e, w = east[rim_at, :], west[rim_at, :]
            for f, (ref, out) in enumerate(((h, h0_out), (u, u0_out), (v, v0_out))):
                bring_rows(
                    fields * l + fields - 3 + f, (ref, (l,)), (out, (l,)), here, there,
                    lambda p: rim_lanes(e, w, p, last, lane), count, last,
                )

        sweep(0, BAND // 8 + 1, bring, 9)
        for ends in (True, False):

            @pl.when(s[0] == int(not ends))
            def _():
                at = PAD + BAND if ends else PAD - 2
                for c in range(count):
                    h0_out[l, c, at : at + 2, :] = pole[l, fields - 3, :, c * LANE : (c + 1) * LANE]

        pressure_rows(jnp.int32(l), column, cum, press, h0_out.at[l], count, slab)

        def later(i):
            row = 8 * i
            zonal, merid = gradient(press, row, count, lane)
            for c in range(count):
                u1_out[l, c, at_row(row), :] = u0_out[l, c, at_row(row), :] - zonal[c]
                v1_out[l, c, at_row(row), :] = v0_out[l, c, at_row(row), :] - merid[c]

        sweep(1, slab // 8 - 1, later, 5)

    waves = basis.shape[1]
    for d in range(n):
        held[lax.rem(s[1] + n - d, n)] = pieces[d][...]
    half = waves // 2
    wave = lax.broadcasted_iota(jnp.int32, (POLAR, waves), 1)
    wave = jnp.where(wave < half, wave, wave - half)
    scale = jnp.where(wave == 0, 1.0, 2.0) / (n * cols)
    keep = jnp.where(wave <= limits[0:POLAR, 0:1], scale, 0.0)
    turn = jnp.where(lax.rem(wave[0:2], 2) == 0, 1.0, -1.0)
    one = turn[0:1]
    for north in (True, False):

        @pl.when(s[0] == int(north))
        def _():
            first = PAD if north else PAD + BAND - POLAR
            rim = PAD - 2 if north else PAD + BAND

            def level_step(l, cum):
                u = held[l, 0:POLAR, :] * keep
                v = held[l, POLAR : 2 * POLAR, :] * keep
                thick = held[l, 2 * POLAR : 3 * POLAR + 1, :]
                p = cum + 0.5 * thick
                if north:
                    before = jnp.concatenate([one * p[0:1], p[0 : POLAR - 1]], 0)
                    diff = (p[1:] - before) * keep
                    rhs[0:POLAR, :] = p[0:POLAR] * keep
                else:
                    after = jnp.concatenate([p[2:], one * p[POLAR:]], 0)
                    diff = (after - p[0:POLAR]) * keep
                    rhs[0:POLAR, :] = p[1:] * keep
                w = v - GRADIENT_COEF * diff
                lhs[0:POLAR, :] = u
                lhs[POLAR : 2 * POLAR, :] = v
                lhs[2 * POLAR : 3 * POLAR, :] = w
                for k, (x, sign) in enumerate(((u, 1.0), (v, -1.0), (w, -1.0))):
                    a, b = (x[1:2], x[0:1]) if north else (x[POLAR - 1 :], x[POLAR - 2 : POLAR - 1])
                    at = 3 * POLAR + 2 * k
                    lhs[at : at + 1, :] = sign * one * a
                    lhs[at + 1 : at + 2, :] = sign * one * b
                back = dot3(lhs[...], basis[0])
                grad = dot3(rhs[...], slope[0])
                zonal = back[0:POLAR]
                later = zonal - GRADIENT_COEF * grad[0:POLAR]
                for c in range(count):
                    part = slice(c * LANE, (c + 1) * LANE)
                    u0_out[l, c, first : first + POLAR, :] = zonal[:, part]
                    v0_out[l, c, first : first + POLAR, :] = back[POLAR : 2 * POLAR, part]
                    u1_out[l, c, first : first + POLAR, :] = later[:, part]
                    v1_out[l, c, first : first + POLAR, :] = back[2 * POLAR : 3 * POLAR, part]
                    u0_out[l, c, rim : rim + 2, :] = back[3 * POLAR : 3 * POLAR + 2, part]
                    v0_out[l, c, rim : rim + 2, :] = back[3 * POLAR + 2 : 3 * POLAR + 4, part]
                    v1_out[l, c, rim : rim + 2, :] = back[3 * POLAR + 4 : 3 * POLAR + 6, part]
                return cum + thick

            lax.fori_loop(0, levels, level_step, above[0 : POLAR + 1, :])

    def step(k):
        l, i = k // (slab // 8 - 2), lax.rem(k, slab // 8 - 2) + 1
        here = eight(i)
        new = inflows_at(h0_out, u0_out, v0_out, 8 * i, count, ((l,), (l,)), lane)[4]
        for c in range(count):
            h1_out[l, c, here, :] = new[c]
            total[c, here, :] = jnp.where(l == 0, new[c], total[c, here, :] + new[c])

    sweep(0, levels * (slab // 8 - 2), step, UNROLL["step"])


def filtered_band(scalars, pieces, above, limits, basis, slope, column, h, u, v, east, west, pole):
    n = len(pieces)
    rows, waves = pieces[0].shape
    width = basis.shape[2]
    levels, height, cols = h.shape
    count = column.shape[0]
    slab = BAND + 2 * PAD
    E = pl.Element
    raw = pl.BlockSpec((E(levels), E(BAND + 8), E(cols)), lambda i, s: (0, s[POLAR_AT + 1] * 8, 0))
    out = jax.ShapeDtypeStruct((levels, count, slab, LANE), jnp.float32)
    whole = pl.BlockSpec((levels, count, slab, LANE), lambda i, s: (0, 0, 0, 0))
    return pl.pallas_call(
        functools.partial(filter_kernel, n),
        grid_spec=pltpu.PrefetchScalarGridSpec(
            num_scalar_prefetch=1,
            grid=(1,),
            in_specs=[HELD] * (n + 2)
            + [
                pl.BlockSpec((1, waves, width), lambda i, s: (s[1], 0, 0)),
                pl.BlockSpec((1, waves, width), lambda i, s: (s[1], 0, 0)),
                pl.BlockSpec((E(count), E(slab), E(LANE)), lambda i, s: (0, s[POLAR_AT] * 8, 0)),
            ]
            + [raw] * 3
            + [HELD] * 3,
            out_specs=[whole] * 6 + [pl.BlockSpec((count, slab, LANE), lambda i, s: (0, 0, 0))],
            scratch_shapes=[
                pltpu.VMEM((n, rows, waves), jnp.float32),
                pltpu.VMEM((3 * POLAR + 12, waves), jnp.float32),
                pltpu.VMEM((BAND, waves), jnp.float32),
            ]
            + [pltpu.VMEM((count, slab, LANE), jnp.float32)] * 2,
        ),
        out_shape=[out] * 6 + [jax.ShapeDtypeStruct((count, slab, LANE), jnp.float32)],
        cost_estimate=cost(12),
        compiler_params=params(),
        name="filtered_band",
    )(scalars, *pieces, above, limits, basis, slope, column, h, u, v, east, west, pole)


def slab_kernel(fields, group, rows, place, inner, s, *refs):
    if inner:
        tr, h, u, v, above, east, west, rim = refs[:8]
        tr_out, h_out, h1, u1, v1, total = refs[8:14]
        early, late, t0, t1, h0, u0, v0, cum, press = refs[14:]
        lead = ((), ())
        lead_one = (0,)
    else:
        tr, h0, u0, v0, u1, v1, east, west, rim = refs[:9]
        tr_out, h_out = refs[11:13]
        early, late, t0, t1, h1 = refs[13:]
        lead = ((0,), (0,))
        lead_one = ()
    level, part = pl.program_id(0), pl.program_id(1)
    lane = lanes()
    count = early.shape[1]
    cols = h_out.shape[2]
    last = cols - LANE * (count - 1)
    tiles = rows // 8

    def window(i):
        rim_at = eight(i + s[place + 1])
        e, w = east[rim_at, :], west[rim_at, :]
        return eight(i), at_row(8 * (i + s[place + 2])), lambda p: rim_lanes(e, w, p, last, lane)

    def rims(store):
        for ends in (True, False):

            @pl.when(s[place + 3] == int(ends))
            def _():
                at = PAD + rows if ends else PAD - 2
                for c in range(count):
                    store(c, slice(at, at + 2), slice(c * LANE, (c + 1) * LANE))

    def weights_from(target, here, flows, new):
        for c in range(count):
            inv = 1.0 / new[c]
            w = [x[c] * inv for x in flows]
            for k in range(4):
                target[k + 1, c, here, :] = w[k]
            target[0, c, here, :] = 1.0 - ((w[0] + w[1]) + (w[2] + w[3]))

    @pl.when(part == 0)
    def _():
        if inner:

            def bring(i):
                here, there, rim_of = window(i)
                for f, (ref, out) in enumerate(((h, h0), (u, u0), (v, v0))):
                    bring_rows(
                        fields * level + fields - 3 + f, (ref, (0,)), (out, ()), here, there, rim_of, count, last
                    )

            sweep(0, tiles + 1, bring, UNROLL["bring"])

            def store(c, at, part):
                for f, out in enumerate((h0, u0, v0)):
                    out[c, at, :] = rim[level, fields - 3 + f, :, part]

            rims(store)
            pressure_rows(level, above, cum, press, h0, count, rows + 2 * PAD)

        def one(i):
            row = 8 * i + PAD - 8
            there = at_row(row)
            *flows, new = inflows_at(h0, u0, v0, row, count, lead, lane)
            weights_from(early, eight(i), flows, new)
            for c in range(count):
                h1[lead_one + (c, there, slice(None))] = new[c]
            if inner:
                zonal, merid = gradient(press, row, count, lane)
                for c in range(count):
                    total[c, there, :] = jnp.where(level == 0, new[c], total[c, there, :] + new[c])
                    u1[0, c, there, :] = u0[c, there, :] - zonal[c]
                    v1[0, c, there, :] = v0[c, there, :] - merid[c]

        sweep(0, tiles + 2, one, UNROLL["coef"])

        def two(i):
            here = eight(i)
            *flows, new = inflows_at(h1, u1, v1, 8 * i + PAD, count, (lead_one, (0,)), lane)
            weights_from(late, here, flows, new)
            for c in range(count):
                wide = min(LANE, cols - c * LANE)
                h_out[0, here, c * LANE : c * LANE + wide] = new[c][:, 0:wide]

        sweep(0, tiles, two, UNROLL["coef"])

    def bring(i):
        here, there, rim_of = window(i)
        for j in range(group):
            bring_rows(
                fields * level + part * group + j, (tr, (j, 0)), (t0, (j,)), here, there, rim_of, count, last
            )

    sweep(0, tiles + 1, bring, UNROLL["bring"])

    def store(c, at, lanes_of):
        for j in range(group):
            t0[j, c, at, :] = rim[level, part * group + j, :, lanes_of]

    rims(store)

    def advance(source, j, row, weights):
        mid = tiles_at(source, at_row(row), count, (j,))
        up = tiles_at(source, pl.ds(row - 1, 8), count, (j,))
        down = tiles_at(source, pl.ds(row + 1, 8), count, (j,))
        right, left = from_east(mid, lane), from_west(mid, lane)
        return [
            weights[0][c] * mid[c]
            + weights[1][c] * right[c]
            + weights[2][c] * left[c]
            + weights[3][c] * up[c]
            + weights[4][c] * down[c]
            for c in range(count)
        ]

    def one(i):
        weights = [tiles_at(early, eight(i), count, (k,)) for k in range(5)]
        for j in range(group):
            new = advance(t0, j, 8 * i + PAD - 8, weights)
            for c in range(count):
                t1[j, c, at_row(8 * i + PAD - 8), :] = new[c]

    sweep(0, tiles + 2, one, UNROLL["one"])

    def two(i):
        here = eight(i)
        weights = [tiles_at(late, here, count, (k,)) for k in range(5)]
        for j in range(group):
            new = advance(t1, j, 8 * i + PAD, weights)
            for c in range(count):
                wide = min(LANE, cols - c * LANE)
                tr_out[j, 0, here, c * LANE : c * LANE + wide] = new[c][:, 0:wide]

    sweep(0, tiles, two, UNROLL["two"])


def tracer_slab(scalars, place, rows, group, tracers, fields, east, west, rim, base, micros, name):
    count, levels, height, cols = tracers.shape
    tiles = (cols - 1) // LANE + 1
    slab = rows + 2 * PAD
    inner = base is None
    E = pl.Element
    slabs = pl.BlockSpec((1, tiles, slab, LANE), lambda l, g, s: (l, 0, 0, 0))
    flat = pl.BlockSpec((tiles, slab, LANE), lambda l, g, s: (0, 0, 0))
    in_specs = [
        pl.BlockSpec(
            (E(group), E(1), E(rows + 8), E(cols)), lambda l, g, s: (g * group, l, s[place + 1] * 8, 0)
        )
    ]
    if inner:
        in_specs += [pl.BlockSpec((E(1), E(rows + 8), E(cols)), lambda l, g, s: (l, s[place + 1] * 8, 0))] * 3
        in_specs += [pl.BlockSpec((E(tiles), E(slab), E(LANE)), lambda l, g, s: (0, s[place] * 8, 0))]
    else:
        in_specs += [slabs] * 5
    in_specs += [HELD] * 3
    operands = [tracers, *fields, east, west, rim]
    out_specs = [
        pl.BlockSpec((E(group), E(1), E(rows), E(cols)), lambda l, g, s: (g * group, l, s[place] * 8, 0)),
        pl.BlockSpec((E(1), E(rows), E(cols)), lambda l, g, s: (l, s[place] * 8, 0)),
    ]
    out_shape = [
        jax.ShapeDtypeStruct(tracers.shape, jnp.float32),
        jax.ShapeDtypeStruct((levels, height, cols), jnp.float32),
    ]
    scratch = [
        pltpu.VMEM((5, tiles, rows + 16, LANE), jnp.float32),
        pltpu.VMEM((5, tiles, rows, LANE), jnp.float32),
        pltpu.VMEM((group, tiles, slab, LANE), jnp.float32),
        pltpu.VMEM((group, tiles, slab, LANE), jnp.float32),
    ]
    plane = pltpu.VMEM((tiles, slab, LANE), jnp.float32)
    aliases = {}
    if inner:
        out_specs += [slabs] * 3 + [flat]
        out_shape += [jax.ShapeDtypeStruct((levels, tiles, slab, LANE), jnp.float32)] * 3
        out_shape += [jax.ShapeDtypeStruct((tiles, slab, LANE), jnp.float32)]
        scratch += [plane] * 5
    else:
        in_specs += [pl.BlockSpec(memory_space=pl.ANY)] * 2
        operands += list(base)
        aliases = {len(operands) - 1: 0, len(operands): 1}
        scratch += [plane]
    return pl.pallas_call(
        functools.partial(slab_kernel, rim.shape[1], group, rows, place, inner),
        grid_spec=pltpu.PrefetchScalarGridSpec(
            num_scalar_prefetch=1,
            grid=(levels, count // group),
            in_specs=in_specs,
            out_specs=out_specs,
            scratch_shapes=scratch,
        ),
        out_shape=out_shape,
        input_output_aliases=aliases,
        cost_estimate=cost(micros),
        compiler_params=params(),
        name=name,
    )(scalars, *operands)


def winds_kernel(s, *refs):
    u_out, v_out = refs[8:10]
    lane = lanes()
    cols = u_out.shape[2]
    for k, place in enumerate((MIDDLE_AT, POLAR_AT)):
        h, u, v, above = refs[4 * k : 4 * k + 4]
        cum, press = refs[10 + 2 * k : 12 + 2 * k]
        count, slab = h.shape[1:3]
        pressure_rows(pl.program_id(0), above, cum, press, h.at[0], count, slab)

        def step(i):
            row = 8 * i + PAD
            to = eight(i + s[place])
            zonal, merid = gradient(press, row, count, lane)
            for c in range(count):
                wide = min(LANE, cols - c * LANE)
                part = slice(c * LANE, c * LANE + wide)
                u_out[0, to, part] = (u[0, c, at_row(row), :] - zonal[c])[:, 0:wide]
                v_out[0, to, part] = (v[0, c, at_row(row), :] - merid[c])[:, 0:wide]

        sweep(0, slab // 8 - 4, step, UNROLL["step"])


def last_winds(scalars, slabs, rows, cols):
    levels, tiles = slabs[0][0].shape[:2]
    in_specs, scratch = [], []
    for h, _, _, _ in slabs:
        tall = h.shape[2]
        in_specs += [pl.BlockSpec((1, tiles, tall, LANE), lambda l, s: (l, 0, 0, 0))] * 3
        in_specs += [HELD]
        scratch += [pltpu.VMEM((tiles, tall, LANE), jnp.float32)] * 2
    out = jax.ShapeDtypeStruct((levels, rows, cols), jnp.float32)
    return pl.pallas_call(
        winds_kernel,
        grid_spec=pltpu.PrefetchScalarGridSpec(
            num_scalar_prefetch=1,
            grid=(levels,),
            in_specs=in_specs,
            out_specs=[pl.BlockSpec((1, rows, cols), lambda l, s: (l, 0, 0))] * 2,
            scratch_shapes=scratch,
        ),
        out_shape=[out, out],
        cost_estimate=cost(8),
        compiler_params=params(),
        name="last_winds",
    )(scalars, *slabs[0], *slabs[1])


def bases(n, cols):
    total = n * cols
    wave = np.arange(KMAX + 1)
    cell = np.arange(total).reshape(n, cols)
    angle = (cell[:, :, None] * wave % total) * (2.0 * math.pi / total)
    forward = np.concatenate([np.cos(angle), np.sin(angle)], 2)
    width = LANE * ((cols - 1) // LANE + 1)
    lane = np.arange(width)
    lane = np.where(lane < width - 2, lane, lane - width)
    cell = np.arange(n)[:, None] * cols + lane[None, :]
    angle = (cell[:, None, :] * wave[:, None] % total) * (2.0 * math.pi / total)
    inverse = np.concatenate([np.cos(angle), np.sin(angle)], 1)
    steep = 2.0 * np.sin(wave * (2.0 * math.pi / total))[:, None]
    slope = np.concatenate([-steep * np.sin(angle), steep * np.cos(angle)], 1)
    return [jnp.asarray(x.astype(np.float32)) for x in (forward, inverse, slope)]


def shards_tiled(tracers, thickness, zonal, meridional, cutoff):
    count, levels, rows, cols = tracers.shape
    n = lax.axis_size("lon")
    me = lax.axis_index("lon").astype(jnp.int32)
    is_north = lax.axis_index("lat") == 0
    inner = rows - BAND

    band_at = rows // 8 - BAND // 8
    scalars = jnp.where(
        is_north,
        jnp.array([1, 0, 0, 0, PAD // 8, 0, BAND // 8, BAND // 8 - 1, PAD // 8 - 1, 1], jnp.int32),
        jnp.array([0, 0, band_at, band_at - 1, PAD // 8 - 1, 1, 0, 0, PAD // 8, 0], jnp.int32),
    )
    scalars = scalars + jnp.where(jnp.arange(10) == 1, me, 0)
    forward, inverse, slope = bases(n, cols)
    limits = jnp.where(is_north, cutoff[0], cutoff[1])
    limits = jnp.broadcast_to(jnp.pad(limits, (0, BAND - POLAR))[:, None], (BAND, LANE))

    def along(value, d):
        return lax.ppermute(value, "lon", [(i, (i + d) % n) for i in range(n)])

    def to_lower(value):
        return lax.ppermute(value, "lev", [(0, 1)])

    fields = (thickness, zonal, meridional)
    sent = band_rows(scalars, zonal, meridional, thickness, n)
    scalars, sent = lax.optimization_barrier((scalars, sent))
    pieces = [sent[0]] + [along(sent[d], d) for d in range(1, n)]

    packed = pack_columns(scalars, tracers, *fields)
    scalars, packed, deep = lax.optimization_barrier((scalars, packed, thickness))
    east, west = along(packed[0], n - 1), along(packed[1], 1)
    column = column_sum(deep)
    scalars, column = lax.optimization_barrier((scalars, column))

    own = spectra(scalars, pieces, forward)
    scalars, own = lax.optimization_barrier((scalars, own))
    pieces = [own] + [along(own, d) for d in range(1, n)]

    pole, facing = edge_rows(scalars, tracers, *fields, east, west)
    facing = lax.ppermute(facing, "lat", [(0, 1), (1, 0)])
    pole = along(pole, n // 2)
    column = to_lower(column_rims(scalars, column, cols, east, west, facing))
    tr, h2, h1, u1, v1, total = tracer_slab(
        scalars, MIDDLE_AT, inner, 5, tracers, (*fields, column), east, west, facing, None, 50, "tracers_inner"
    )
    scalars, total, pieces = lax.optimization_barrier((scalars, total, pieces))
    total = to_lower(total)
    above_band = to_lower(sum(p[2 * POLAR :] for p in pieces))
    h0, u0, v0, u1b, v1b, h1b, band_total = filtered_band(
        scalars, pieces, above_band, limits, inverse, slope, column, thickness, zonal, meridional, east, west, pole
    )
    band_total = to_lower(band_total)
    tr, h2 = tracer_slab(
        scalars, POLAR_AT, BAND, 10, tracers, (h0, u0, v0, u1b, v1b), east, west, pole, (tr, h2), 13,
        "tracers_polar",
    )
    u2, v2 = last_winds(scalars, ((h1, u1, v1, total), (h1b, u1b, v1b, band_total)), rows, cols)
    return (tr, h2, u2, v2)


def tiles_fit(mesh, tracers):
    count, levels, rows, cols = tracers.shape
    rows, cols = rows // mesh.shape["lat"], cols // mesh.shape["lon"]
    count, levels = count // mesh.shape["member"], levels // mesh.shape["lev"]
    last = (cols - 1) % LANE + 1
    return (
        mesh.shape["lat"] == 2
        and mesh.shape["lev"] == 2
        and levels == mesh.shape["lon"]
        and mesh.shape["lon"] % 2 == 0
        and rows % 40 == 0
        and rows >= 2 * BAND + 8
        and last + 4 <= LANE
        and last - 2 >= LANE // 2
        and last + 2 * (count + 2) <= LANE
        and cols > LANE
        and 2 * (count + 3) * levels <= last + 2
        and count % 5 == 0
    )


def solution(mesh):
    placed = (
        P("member", "lev", "lat", "lon"),
        P(("member", "lev"), "lat", "lon"),
        P(("member", "lev"), "lat", "lon"),
        P(("member", "lev"), "lat", "lon"),
        P(),
    )
    outs = (
        P("member", "lev", "lat", "lon"),
        P(("member", "lev"), "lat", "lon"),
        P(("member", "lev"), "lat", "lon"),
        P(("member", "lev"), "lat", "lon"),
    )

    def program(*args):
        part = shards_tiled if tiles_fit(mesh, args[0]) else shards
        return jax.shard_map(part, mesh=mesh, in_specs=placed, out_specs=outs, check_vma=False)(*args)

    return program
```

```python
import functools
import math

import jax
import jax.numpy as jnp
import numpy as np
from jax import lax
from jax.experimental import pallas as pl
from jax.experimental.pallas import tpu as pltpu
from jax.sharding import PartitionSpec as P

NSUB = 2
POLAR = 60
KMAX = 191


COURANT_CAP = 0.15
GRADIENT_COEF = 0.1


def extended_2(block, sides, width):
    for axis, dim in sides:
        count = lax.axis_size(axis)
        forward = [(i, i + 1) for i in range(count - 1)]
        forward.append((count - 1, 0))
        backward = [(target, source) for source, target in forward]
        low = lax.ppermute(
            lax.slice_in_dim(block, block.shape[dim] - width, None, axis=dim), axis, forward
        )
        high = lax.ppermute(lax.slice_in_dim(block, 0, width, axis=dim), axis, backward)
        block = jnp.concatenate([low, block, high], axis=dim)
    return block


def shifted(block, axis, distance):
    devices = range(lax.axis_size(axis))
    route = [((i - distance) % len(devices), i) for i in devices]
    return lax.ppermute(block, axis, route)


def entering(value, axis, join, neutral):
    count, mine = (lax.axis_size(axis), lax.axis_index(axis))
    pieces = lax.all_gather(value, axis)
    running = jnp.full_like(value, 0) + jnp.asarray(neutral, value.dtype)

    def step(position, running):
        longer = join(running, pieces[position])
        return jnp.where(position < mine, longer, running)

    return lax.fori_loop(0, count - 1, step, running)


def advance_level(extended, pressure):
    tracer_count = extended.shape[0] - 3
    thick = extended[tracer_count]
    east_wind = extended[tracer_count + 1]
    north_wind = extended[tracer_count + 2]
    masses = jnp.concatenate([thick[None], extended[:tracer_count] * thick[None]], 0)
    east_courant = COURANT_CAP * jnp.tanh(0.5 * (east_wind[1:-1, :-1] + east_wind[1:-1, 1:]))
    east_flux = (
        jnp.maximum(east_courant, 0.0) * masses[:, 1:-1, :-1]
        + jnp.minimum(east_courant, 0.0) * masses[:, 1:-1, 1:]
    )
    south_courant = COURANT_CAP * jnp.tanh(0.5 * (north_wind[:-1, 1:-1] + north_wind[1:, 1:-1]))
    south_flux = (
        jnp.maximum(south_courant, 0.0) * masses[:, :-1, 1:-1]
        + jnp.minimum(south_courant, 0.0) * masses[:, 1:, 1:-1]
    )
    updated = (
        masses[:, 1:-1, 1:-1]
        - (east_flux[:, :, 1:] - east_flux[:, :, :-1])
        - (south_flux[:, 1:] - south_flux[:, :-1])
    )
    new_thick = updated[0]
    new_mixing = updated[1:] / new_thick[None]
    new_east = east_wind[1:-1, 1:-1] - GRADIENT_COEF * (pressure[1:-1, 2:] - pressure[1:-1, :-2])
    new_north = north_wind[1:-1, 1:-1] - GRADIENT_COEF * (pressure[2:, 1:-1] - pressure[:-2, 1:-1])
    return (new_mixing, new_thick, new_east, new_north)


def wave_basis(anchor, length, lon_total):
    cells = anchor + jnp.arange(length, dtype=jnp.int32)
    waves = jnp.arange(KMAX + 1, dtype=jnp.int32)
    phase = (cells[:, None] * waves[None, :] % lon_total).astype(jnp.float32) * (
        2.0 * math.pi / lon_total
    )
    return jnp.concatenate([jnp.cos(phase), jnp.sin(phase)], 1)


def wave_weights(limits, lon_total):
    waves = jnp.arange(KMAX + 1, dtype=jnp.int32)
    scaled = jnp.where(waves == 0, 1.0, 2.0).astype(jnp.float32) / lon_total
    kept = jnp.where(waves[None, :] <= limits[:, None], scaled[None, :], 0.0)
    return jnp.concatenate([kept, kept], 1)


def smooth_winds(zonal, meridional, cutoff, is_north, is_south):
    level_count, row_count, col_count = zonal.shape
    lon_count = lax.axis_size("lon")
    lon_total = col_count * lon_count
    north_rows = jnp.stack([zonal[:, :POLAR], meridional[:, :POLAR]], 0)
    south_rows = jnp.stack([zonal[:, row_count - POLAR :], meridional[:, row_count - POLAR :]], 0)
    selected = jnp.where(is_north, north_rows, south_rows).reshape(-1, col_count)
    limits = jnp.tile(jnp.where(is_north, cutoff[0], cutoff[1]), 2 * level_count)
    fragment = lax.all_gather(selected, "lon", axis=1, tiled=True)
    basis = wave_basis(jnp.int32(0), fragment.shape[1], lon_total)
    spectrum = jnp.dot(
        fragment, basis, precision=lax.Precision.HIGHEST, preferred_element_type=jnp.float32
    )
    own_basis = wave_basis(lax.axis_index("lon") * col_count, col_count, lon_total)
    filtered = jnp.dot(
        spectrum * wave_weights(limits, lon_total),
        own_basis.T,
        precision=lax.Precision.HIGHEST,
        preferred_element_type=jnp.float32,
    )
    filtered = filtered.reshape(2, level_count, POLAR, col_count)
    row_start = jnp.where(is_north, 0, row_count - POLAR).astype(jnp.int32)
    polar_band = jnp.logical_or(is_north, is_south)
    new_zonal = lax.dynamic_update_slice_in_dim(zonal, filtered[0], row_start, 1)
    new_merid = lax.dynamic_update_slice_in_dim(meridional, filtered[1], row_start, 1)
    return (jnp.where(polar_band, new_zonal, zonal), jnp.where(polar_band, new_merid, meridional))


def shards(tracers, thickness, zonal, meridional, cutoff):
    tracer_count = tracers.shape[0]
    lat_index = lax.axis_index("lat")
    is_north = lat_index == 0
    is_south = lat_index == lax.axis_size("lat") - 1
    lon_count = lax.axis_size("lon")
    flip_sign = jnp.concatenate(
        [jnp.ones((tracer_count + 1,), jnp.float32), -jnp.ones((2,), jnp.float32)]
    )[:, None, None]
    advance_all = jax.vmap(advance_level, in_axes=(1, 0), out_axes=(1, 0, 0, 0))
    for substep in range(NSUB):
        zonal, meridional = smooth_winds(zonal, meridional, cutoff, is_north, is_south)
        state = jnp.concatenate([tracers, thickness[None], zonal[None], meridional[None]], 0)
        extended = extended_2(state, (("lat", 2), ("lon", 3)), 1)
        edges = jnp.stack([state[:, :, 0], state[:, :, -1]], 2)
        opposite = shifted(edges, "lon", lon_count // 2)
        north_rim = jnp.where(is_north, opposite[:, :, 0] * flip_sign, extended[:, :, 0, 1:-1])
        south_rim = jnp.where(is_south, opposite[:, :, 1] * flip_sign, extended[:, :, -1, 1:-1])
        extended = extended.at[:, :, 0, 1:-1].set(north_rim)
        extended = extended.at[:, :, -1, 1:-1].set(south_rim)
        thick_ext = extended[tracer_count]
        column_above = entering(
            jnp.sum(thick_ext, 0),
            "lev",
            lambda earlier, later: earlier + later,
            jnp.zeros(thick_ext.shape[1:], jnp.float32),
        )
        pressure = jnp.cumsum(thick_ext, axis=0) - 0.5 * thick_ext + column_above[None]
        tracers, thickness, zonal, meridional = advance_all(extended, pressure)
    return (tracers, thickness, zonal, meridional)


LANE = 128
POLAR_AT, MIDDLE_AT = 2, 6
UNROLL = dict(step=13, bring=13, coef=8, one=13, two=12)
PAD = 16
BAND = 64


def cost(micros):
    return pl.CostEstimate(flops=0, bytes_accessed=int(micros * 3.3e6), transcendentals=0)


def params(mib=56):
    return pltpu.CompilerParams(vmem_limit_bytes=mib * 1024 * 1024)


HELD = pl.BlockSpec(memory_space=pltpu.VMEM)


def lanes():
    return lax.broadcasted_iota(jnp.int32, (8, LANE), 1)


def at_row(row):
    return pl.ds(row if isinstance(row, int) else pl.multiple_of(row, 8), 8)


def eight(index):
    return at_row(8 * index)


def from_east(tiles, lane):
    turned = [pltpu.roll(t, LANE - 1, 1) for t in tiles]
    n = len(tiles)
    return [jnp.where(lane < LANE - 1, turned[c], turned[(c + 1) % n]) for c in range(n)]


def from_west(tiles, lane):
    turned = [pltpu.roll(t, 1, 1) for t in tiles]
    n = len(tiles)
    return [jnp.where(lane > 0, turned[c], turned[(c - 1) % n]) for c in range(n)]


def courant(a, b):
    return COURANT_CAP * jnp.tanh(0.5 * (a + b))


def rim_lanes(east, west, plane, last, lane):
    both = jnp.where(lane < 2 * plane + 2, east, west)
    return pltpu.roll(both, lax.rem(last + LANE - 2 * plane, LANE), 1)


def inflows(h, u, v, h_n, h_s, v_n, v_s, lane):
    count = range(len(h))
    u_e, h_e = from_east(u, lane), from_east(h, lane)
    c_e = [courant(u[c], u_e[c]) for c in count]
    out_e = [jnp.maximum(c_e[c], 0.0) * h[c] for c in count]
    in_e = [jnp.maximum(-c_e[c], 0.0) * h_e[c] for c in count]
    in_w, out_w = from_west(out_e, lane), from_west(in_e, lane)
    c_s = [courant(v[c], v_s[c]) for c in count]
    c_n = [courant(v_n[c], v[c]) for c in count]
    in_s = [jnp.maximum(-c_s[c], 0.0) * h_s[c] for c in count]
    out_s = [jnp.maximum(c_s[c], 0.0) * h[c] for c in count]
    in_n = [jnp.maximum(c_n[c], 0.0) * h_n[c] for c in count]
    out_n = [jnp.maximum(-c_n[c], 0.0) * h[c] for c in count]
    new = [
        h[c] - (out_e[c] - in_e[c]) + (in_w[c] - out_w[c]) - (out_s[c] - in_s[c]) + (in_n[c] - out_n[c])
        for c in count
    ]
    return in_e, in_w, in_n, in_s, new


def halves(x):
    high = x.astype(jnp.bfloat16)
    return high, (x - high.astype(jnp.float32)).astype(jnp.bfloat16)


def dot3(a, b):
    (a_hi, a_lo), (b_hi, b_lo) = halves(a), halves(b)

    def one(x, y):
        return jnp.dot(x, y, preferred_element_type=jnp.float32)

    return one(a_hi, b_hi) + (one(a_hi, b_lo) + one(a_lo, b_hi))


def sweep(first, end, body, depth):
    whole = (end - first) // depth

    def step(k, _):
        for j in range(depth):
            body(first + k * depth + j)
        return 0

    lax.fori_loop(0, whole, step, 0)
    for i in range(first + whole * depth, end):
        body(i)


def tiles_at(ref, base, count, lead=()):
    return [ref[lead + (c, base, slice(None))] for c in range(count)]


def inflows_at(h, u, v, row, count, lead, lane):
    mid = at_row(row)
    up, down = pl.ds(row - 1, 8), pl.ds(row + 1, 8)
    hl, vl = lead
    return inflows(
        tiles_at(h, mid, count, hl),
        tiles_at(u, mid, count, vl),
        tiles_at(v, mid, count, vl),
        tiles_at(h, up, count, hl),
        tiles_at(h, down, count, hl),
        tiles_at(v, up, count, vl),
        tiles_at(v, down, count, vl),
        lane,
    )


def band_kernel(n, s, *refs):
    ins, outs = refs[: 3 * n], refs[3 * n :]
    for north in (True, False):

        @pl.when(s[0] == int(north))
        def _():
            lo = 0 if north else BAND - POLAR
            for d in range(n):
                u, v, h = ins[3 * d : 3 * d + 3]
                outs[d][0:POLAR, :] = u[0, lo : lo + POLAR, :]
                outs[d][POLAR : 2 * POLAR, :] = v[0, lo : lo + POLAR, :]
                first = 0 if north else BAND - POLAR - 1
                outs[d][2 * POLAR : 3 * POLAR + 1, :] = h[0, first : first + POLAR + 1, :]
                outs[d][3 * POLAR + 1 :, :] = jnp.zeros((3, h.shape[2]), jnp.float32)


def band_rows(scalars, u, v, h, n):
    levels, _, cols = u.shape

    def spec(d):
        return pl.BlockSpec(
            (pl.Element(1), pl.Element(BAND), pl.Element(cols)),
            lambda i, s: (lax.rem(s[1] + d, n), s[POLAR_AT] * 8, 0),
        )

    rows = 3 * POLAR + 4
    return pl.pallas_call(
        functools.partial(band_kernel, n),
        grid_spec=pltpu.PrefetchScalarGridSpec(
            num_scalar_prefetch=1,
            grid=(1,),
            in_specs=[spec(d) for d in range(n) for _ in range(3)],
            out_specs=[pl.BlockSpec((rows, cols), lambda i, s: (0, 0))] * n,
        ),
        out_shape=[jax.ShapeDtypeStruct((rows, cols), jnp.float32)] * n,
        cost_estimate=cost(3),
        compiler_params=params(),
        name="band_rows",
    )(scalars, *([u, v, h] * n))


def spectrum_kernel(n, s, *refs):
    total = None
    for d in range(n):
        part = dot3(refs[d][...], refs[n + d][0])
        total = part if total is None else total + part
    refs[2 * n][...] = total


def spectra(scalars, pieces, basis):
    n = len(pieces)
    rows, cols = pieces[0].shape
    waves = basis.shape[2]

    def spec(d):
        return pl.BlockSpec((1, cols, waves), lambda i, s: (lax.rem(s[1] + n - d, n), 0, 0))

    return pl.pallas_call(
        functools.partial(spectrum_kernel, n),
        grid_spec=pltpu.PrefetchScalarGridSpec(
            num_scalar_prefetch=1,
            grid=(1,),
            in_specs=[HELD] * n + [spec(d) for d in range(n)],
            out_specs=pl.BlockSpec((rows, waves), lambda i, s: (0, 0)),
        ),
        out_shape=jax.ShapeDtypeStruct((rows, waves), jnp.float32),
        cost_estimate=cost(6),
        compiler_params=params(),
        name="spectra",
    )(scalars, *pieces, *([basis] * n))


def pack_kernel(fields, last, s, t_lo, t_hi, h_lo, h_hi, u_lo, u_hi, v_lo, v_hi, west, east):
    lane = lanes()
    count, levels = t_lo.shape[:2]
    gap = last - 2

    def step(i):
        here = eight(i)
        got_w = got_e = None
        for l in range(levels):
            sources = [(t_lo, t_hi, (f, l)) for f in range(count)]
            sources += [(h_lo, h_hi, (l,)), (u_lo, u_hi, (l,)), (v_lo, v_hi, (l,))]
            got = None
            for f, (lo, hi, lead) in enumerate(sources):
                at = lead + (here, slice(None))
                both = jnp.where(lane < LANE // 2, lo[at], hi[at])
                turned = pltpu.roll(both, 2 * f, 1) if f else both
                mine = jnp.logical_or(jnp.logical_and(lane >= 2 * f, lane < LANE // 2), lane >= gap + 2 * f)
                got = jnp.where(mine, turned, got) if f else turned
            base = 2 * fields * l
            to_w = pltpu.roll(got, base, 1) if l else got
            to_e = pltpu.roll(got, (base - gap + LANE - 2 - last) % LANE, 1)
            got_w = jnp.where(lane >= base, to_w, got_w) if l else to_w
            got_e = jnp.where(lane >= base + LANE - 2 - last, to_e, got_e) if l else to_e
        west[here, :] = got_w
        east[here, :] = got_e

    sweep(0, west.shape[0] // 8, step, 3)


def pack_columns(scalars, tracers, h, u, v):
    count, levels, rows, cols = tracers.shape
    high = (cols - 1) // LANE
    part = rows // 5
    t_spec = [pl.BlockSpec((count, levels, part, LANE), lambda r, s, c=c: (0, 0, r, c)) for c in (0, high)]
    f_spec = [pl.BlockSpec((levels, part, LANE), lambda r, s, c=c: (0, r, c)) for c in (0, high)]
    out = jax.ShapeDtypeStruct((rows, LANE), jnp.float32)
    return pl.pallas_call(
        functools.partial(pack_kernel, count + 3, cols - LANE * high),
        grid_spec=pltpu.PrefetchScalarGridSpec(
            num_scalar_prefetch=1,
            grid=(5,),
            in_specs=t_spec + f_spec * 3,
            out_specs=[pl.BlockSpec((part, LANE), lambda r, s: (r, 0))] * 2,
        ),
        out_shape=[out, out],
        cost_estimate=cost(10),
        compiler_params=params(),
        name="pack_columns",
    )(scalars, tracers, tracers, h, h, u, u, v, v)


def rows_kernel(fields, s, t_top, t_bot, h_top, h_bot, u_top, u_bot, v_top, v_bot,
                east, west, pole, facing, top, bot):
    level = pl.program_id(0)
    lane = lanes()
    cols = h_top.shape[2]
    tail = top.shape[2] - LANE
    last = cols - tail
    height = east.shape[0]
    e_top, e_bot = east[0:8, :], east[height - 8 :, :]
    w_top, w_bot = west[0:8, :], west[height - 8 :, :]
    refs = [(t_top, t_bot, (f, 0)) for f in range(fields - 3)]
    refs += [(h_top, h_bot, (0,)), (u_top, u_bot, (0,)), (v_top, v_bot, (0,))]
    for f in range(fields):
        plane = fields * level + f
        a, b, lead = refs[f]
        top[f, :, 0:cols] = a[lead]
        bot[f, :, 0:cols] = b[lead]
        top[f, :, cols:] = rim_lanes(e_top, w_top, plane, last, lane)[:, last:]
        bot[f, :, cols:] = rim_lanes(e_bot, w_bot, plane, last, lane)[:, last:]
    flips = [1.0] * (fields - 1) + [-1.0]

    @pl.when(s[0] == 1)
    def _():
        for f, flip in enumerate(flips):
            pole[0, f, 0:1, :] = flip * top[f, 1:2, :]
            pole[0, f, 1:2, :] = flip * top[f, 0:1, :]
            facing[0, f] = bot[f, 6:8, :]

    @pl.when(s[0] == 0)
    def _():
        for f, flip in enumerate(flips):
            pole[0, f, 0:1, :] = flip * bot[f, 7:8, :]
            pole[0, f, 1:2, :] = flip * bot[f, 6:7, :]
            facing[0, f] = top[f, 0:2, :]


def edge_rows(scalars, tracers, h, u, v, east, west):
    count, levels, rows, cols = tracers.shape
    fields = count + 3
    width = LANE * ((cols - 1) // LANE + 1)
    ends = (0, rows // 8 - 1)
    t_spec = [pl.BlockSpec((count, 1, 8, cols), lambda l, s, r=r: (0, l, r, 0)) for r in ends]
    f_spec = [pl.BlockSpec((1, 8, cols), lambda l, s, r=r: (l, r, 0)) for r in ends]
    out = jax.ShapeDtypeStruct((levels, fields, 2, width), jnp.float32)
    return pl.pallas_call(
        functools.partial(rows_kernel, fields),
        grid_spec=pltpu.PrefetchScalarGridSpec(
            num_scalar_prefetch=1,
            grid=(levels,),
            in_specs=t_spec + f_spec * 3 + [HELD] * 2,
            out_specs=[pl.BlockSpec((1, fields, 2, width), lambda l, s: (l, 0, 0, 0))] * 2,
            scratch_shapes=[pltpu.VMEM((fields, 8, width), jnp.float32)] * 2,
        ),
        out_shape=[out, out],
        cost_estimate=cost(4),
        compiler_params=params(),
        name="edge_rows",
    )(scalars, tracers, tracers, h, h, u, u, v, v, east, west)


def bring_rows(plane, source, target, here, there, rim, count, last):
    (ref, lead), (out, at) = source, target
    for c in range(count - 1):
        out[at + (c, there, slice(None))] = ref[lead + (here, slice(c * LANE, (c + 1) * LANE))]
    out[at + (count - 1, there, slice(0, last))] = ref[lead + (here, slice(LANE * (count - 1), None))]
    out[at + (count - 1, there, slice(last, None))] = rim(plane)[:, last:]


def pressure_rows(level, above, cum, press, h, count, tall):
    def body(i):
        here = eight(i)
        for c in range(count):
            before = jnp.where(level == 0, above[c, here, :], cum[c, here, :])
            now = h[c, here, :]
            press[c, here, :] = before + 0.5 * now
            cum[c, here, :] = before + now

    sweep(0, tall // 8, body, 8)


def gradient(press, row, count, lane):
    p = tiles_at(press, at_row(row), count)
    p_e, p_w = from_east(p, lane), from_west(p, lane)
    p_n, p_s = tiles_at(press, pl.ds(row - 1, 8), count), tiles_at(press, pl.ds(row + 1, 8), count)
    zonal = [GRADIENT_COEF * (p_e[c] - p_w[c]) for c in range(count)]
    return zonal, [GRADIENT_COEF * (p_s[c] - p_n[c]) for c in range(count)]


def column_kernel(h, total):
    levels, rows, cols = h.shape
    count = total.shape[0]

    def body(i):
        here, there = eight(i), at_row(8 * i + PAD)
        for c in range(count):
            wide = min(LANE, cols - c * LANE)
            part = slice(c * LANE, c * LANE + wide)
            total[c, there, 0:wide] = sum(h[l, here, part] for l in range(levels))

    sweep(0, rows // 8, body, 9)


def column_sum(h):
    _, rows, cols = h.shape
    shape = ((cols - 1) // LANE + 1, rows + 2 * PAD, LANE)
    return pl.pallas_call(
        column_kernel,
        out_shape=jax.ShapeDtypeStruct(shape, jnp.float32),
        in_specs=[pl.BlockSpec(memory_space=pltpu.VMEM)],
        out_specs=pl.BlockSpec(memory_space=pltpu.VMEM),
        cost_estimate=cost(3),
        compiler_params=params(),
        name="column_sum",
    )(h)


def rims_kernel(fields, cols, s, own, east, west, facing, total):
    lane = lanes()
    levels, rows = facing.shape[0], east.shape[0]
    count = total.shape[0]
    last = cols - LANE * (count - 1)
    total[0 : count - 1] = own[0 : count - 1]

    def body(i):
        here, there = eight(i), at_row(8 * i + PAD)
        e, w = east[here, :], west[here, :]
        rim = sum(rim_lanes(e, w, fields * l + fields - 3, last, lane) for l in range(levels))
        total[count - 1, there, :] = jnp.where(lane < last, own[count - 1, there, :], rim)

    sweep(0, rows // 8, body, 9)
    for c in range(count):
        part = slice(c * LANE, (c + 1) * LANE)
        edge = sum(facing[l, fields - 3, :, part] for l in range(levels))
        total[c, PAD - 2 : PAD, :] = edge
        total[c, PAD + rows : PAD + rows + 2, :] = edge


def column_rims(scalars, own, cols, east, west, facing):
    return pl.pallas_call(
        functools.partial(rims_kernel, facing.shape[1], cols),
        grid_spec=pltpu.PrefetchScalarGridSpec(
            num_scalar_prefetch=1,
            grid=(1,),
            in_specs=[HELD] * 4,
            out_specs=pl.BlockSpec(own.shape, lambda i, s: (0, 0, 0)),
        ),
        out_shape=jax.ShapeDtypeStruct(own.shape, jnp.float32),
        cost_estimate=cost(2),
        compiler_params=params(),
        name="column_rims",
    )(scalars, own, east, west, facing)


def filter_kernel(n, s, *refs):
    pieces = refs[:n]
    limits, basis, slope, column, h, u, v, east, west, pole = refs[n : n + 10]
    h0_out, u0_out, v0_out, u1_out, v1_out, h1_out, total = refs[n + 10 : n + 17]
    held, lhs, rhs, cum, press = refs[n + 17 :]
    levels, count, slab = u0_out.shape[:3]
    cols = h.shape[2]
    last = cols - LANE * (count - 1)
    fields = pole.shape[1]
    lane = lanes()

    for l in range(levels):

        def bring(i):
            here, there = eight(i), at_row(8 * (i + s[POLAR_AT + 2]))
            rim_at = eight(i + s[POLAR_AT + 1])
            e, w = east[rim_at, :], west[rim_at, :]
            for f, (ref, out) in enumerate(((h, h0_out), (u, u0_out), (v, v0_out))):
                bring_rows(
                    fields * l + fields - 3 + f, (ref, (l,)), (out, (l,)), here, there,
                    lambda p: rim_lanes(e, w, p, last, lane), count, last,
                )

        sweep(0, BAND // 8 + 1, bring, 9)
        for ends in (True, False):

            @pl.when(s[0] == int(not ends))
            def _():
                at = PAD + BAND if ends else PAD - 2
                for c in range(count):
                    h0_out[l, c, at : at + 2, :] = pole[l, fields - 3, :, c * LANE : (c + 1) * LANE]

        pressure_rows(jnp.int32(l), column, cum, press, h0_out.at[l], count, slab)

        def later(i):
            row = 8 * i
            zonal, merid = gradient(press, row, count, lane)
            for c in range(count):
                u1_out[l, c, at_row(row), :] = u0_out[l, c, at_row(row), :] - zonal[c]
                v1_out[l, c, at_row(row), :] = v0_out[l, c, at_row(row), :] - merid[c]

        sweep(1, slab // 8 - 1, later, 5)

    waves = basis.shape[1]
    for d in range(n):
        held[lax.rem(s[1] + n - d, n)] = pieces[d][...]
    half = waves // 2
    wave = lax.broadcasted_iota(jnp.int32, (POLAR, waves), 1)
    wave = jnp.where(wave < half, wave, wave - half)
    scale = jnp.where(wave == 0, 1.0, 2.0) / (n * cols)
    keep = jnp.where(wave <= limits[0:POLAR, 0:1], scale, 0.0)
    turn = jnp.where(lax.rem(wave[0:2], 2) == 0, 1.0, -1.0)
    one = turn[0:1]
    for north in (True, False):

        @pl.when(s[0] == int(north))
        def _():
            after = 3 * POLAR + 4
            first = PAD if north else PAD + BAND - POLAR
            rim = PAD - 2 if north else PAD + BAND

            def level_step(l, cum):
                u = held[l, 0:POLAR, :] * keep
                v = held[l, POLAR : 2 * POLAR, :] * keep
                thick = held[l, 2 * POLAR : 3 * POLAR + 1, :]
                p = cum + 0.5 * thick
                if north:
                    before = jnp.concatenate([one * p[0:1], p[0 : POLAR - 1]], 0)
                    diff = (p[1:] - before) * keep
                    rhs[0:POLAR, :] = p[0:POLAR] * keep
                else:
                    after = jnp.concatenate([p[2:], one * p[POLAR:]], 0)
                    diff = (after - p[0:POLAR]) * keep
                    rhs[0:POLAR, :] = p[1:] * keep
                w = v - GRADIENT_COEF * diff
                lhs[0:POLAR, :] = u
                lhs[POLAR : 2 * POLAR, :] = v
                lhs[2 * POLAR : 3 * POLAR, :] = w
                for k, (x, sign) in enumerate(((u, 1.0), (v, -1.0), (w, -1.0))):
                    a, b = (x[1:2], x[0:1]) if north else (x[POLAR - 1 :], x[POLAR - 2 : POLAR - 1])
                    at = 3 * POLAR + 2 * k
                    lhs[at : at + 1, :] = sign * one * a
                    lhs[at + 1 : at + 2, :] = sign * one * b
                back = dot3(lhs[...], basis[0])
                grad = dot3(rhs[...], slope[0])
                zonal = back[0:POLAR]
                later = zonal - GRADIENT_COEF * grad[0:POLAR]
                for c in range(count):
                    part = slice(c * LANE, (c + 1) * LANE)
                    u0_out[l, c, first : first + POLAR, :] = zonal[:, part]
                    v0_out[l, c, first : first + POLAR, :] = back[POLAR : 2 * POLAR, part]
                    u1_out[l, c, first : first + POLAR, :] = later[:, part]
                    v1_out[l, c, first : first + POLAR, :] = back[2 * POLAR : 3 * POLAR, part]
                    u0_out[l, c, rim : rim + 2, :] = back[3 * POLAR : 3 * POLAR + 2, part]
                    v0_out[l, c, rim : rim + 2, :] = back[3 * POLAR + 2 : 3 * POLAR + 4, part]
                    v1_out[l, c, rim : rim + 2, :] = back[3 * POLAR + 4 : 3 * POLAR + 6, part]
                return cum + thick

            upper = sum(pieces[d][after : after + POLAR + 1, :] for d in range(n))
            lax.fori_loop(0, levels, level_step, upper)

    def step(k):
        l, i = k // (slab // 8 - 2), lax.rem(k, slab // 8 - 2) + 1
        here = eight(i)
        new = inflows_at(h0_out, u0_out, v0_out, 8 * i, count, ((l,), (l,)), lane)[4]
        for c in range(count):
            h1_out[l, c, here, :] = new[c]
            total[c, here, :] = jnp.where(l == 0, new[c], total[c, here, :] + new[c])

    sweep(0, levels * (slab // 8 - 2), step, UNROLL["step"])


def filtered_band(scalars, pieces, limits, basis, slope, column, h, u, v, east, west, pole):
    n = len(pieces)
    rows, waves = pieces[0].shape
    width = basis.shape[2]
    levels, height, cols = h.shape
    count = column.shape[0]
    slab = BAND + 2 * PAD
    E = pl.Element
    raw = pl.BlockSpec((E(levels), E(BAND + 8), E(cols)), lambda i, s: (0, s[POLAR_AT + 1] * 8, 0))
    out = jax.ShapeDtypeStruct((levels, count, slab, LANE), jnp.float32)
    whole = pl.BlockSpec((levels, count, slab, LANE), lambda i, s: (0, 0, 0, 0))
    return pl.pallas_call(
        functools.partial(filter_kernel, n),
        grid_spec=pltpu.PrefetchScalarGridSpec(
            num_scalar_prefetch=1,
            grid=(1,),
            in_specs=[HELD] * (n + 1)
            + [
                pl.BlockSpec((1, waves, width), lambda i, s: (s[1], 0, 0)),
                pl.BlockSpec((1, waves, width), lambda i, s: (s[1], 0, 0)),
                pl.BlockSpec((E(count), E(slab), E(LANE)), lambda i, s: (0, s[POLAR_AT] * 8, 0)),
            ]
            + [raw] * 3
            + [HELD] * 3,
            out_specs=[whole] * 6 + [pl.BlockSpec((count, slab, LANE), lambda i, s: (0, 0, 0))],
            scratch_shapes=[
                pltpu.VMEM((n, rows, waves), jnp.float32),
                pltpu.VMEM((3 * POLAR + 12, waves), jnp.float32),
                pltpu.VMEM((BAND, waves), jnp.float32),
            ]
            + [pltpu.VMEM((count, slab, LANE), jnp.float32)] * 2,
        ),
        out_shape=[out] * 6 + [jax.ShapeDtypeStruct((count, slab, LANE), jnp.float32)],
        cost_estimate=cost(12),
        compiler_params=params(),
        name="filtered_band",
    )(scalars, *pieces, limits, basis, slope, column, h, u, v, east, west, pole)


def slab_kernel(fields, group, rows, place, inner, s, *refs):
    if inner:
        tr, h, u, v, above, east, west, rim = refs[:8]
        tr_out, h_out, h1, u1, v1, total = refs[8:14]
        early, late, t0, t1, h0, u0, v0, cum, press = refs[14:]
        lead = ((), ())
        lead_one = (0,)
    else:
        tr, h0, u0, v0, u1, v1, east, west, rim = refs[:9]
        tr_out, h_out = refs[11:13]
        early, late, t0, t1, h1 = refs[13:]
        lead = ((0,), (0,))
        lead_one = ()
    level, part = pl.program_id(0), pl.program_id(1)
    lane = lanes()
    count = early.shape[1]
    cols = h_out.shape[2]
    last = cols - LANE * (count - 1)
    tiles = rows // 8

    def window(i):
        rim_at = eight(i + s[place + 1])
        e, w = east[rim_at, :], west[rim_at, :]
        return eight(i), at_row(8 * (i + s[place + 2])), lambda p: rim_lanes(e, w, p, last, lane)

    def rims(store):
        for ends in (True, False):

            @pl.when(s[place + 3] == int(ends))
            def _():
                at = PAD + rows if ends else PAD - 2
                for c in range(count):
                    store(c, slice(at, at + 2), slice(c * LANE, (c + 1) * LANE))

    def weights_from(target, here, flows, new):
        for c in range(count):
            inv = 1.0 / new[c]
            w = [x[c] * inv for x in flows]
            for k in range(4):
                target[k + 1, c, here, :] = w[k]
            target[0, c, here, :] = 1.0 - ((w[0] + w[1]) + (w[2] + w[3]))

    @pl.when(part == 0)
    def _():
        if inner:

            def bring(i):
                here, there, rim_of = window(i)
                for f, (ref, out) in enumerate(((h, h0), (u, u0), (v, v0))):
                    bring_rows(
                        fields * level + fields - 3 + f, (ref, (0,)), (out, ()), here, there, rim_of, count, last
                    )

            sweep(0, tiles + 1, bring, UNROLL["bring"])

            def store(c, at, part):
                for f, out in enumerate((h0, u0, v0)):
                    out[c, at, :] = rim[level, fields - 3 + f, :, part]

            rims(store)
            pressure_rows(level, above, cum, press, h0, count, rows + 2 * PAD)

        def one(i):
            row = 8 * i + PAD - 8
            there = at_row(row)
            *flows, new = inflows_at(h0, u0, v0, row, count, lead, lane)
            weights_from(early, eight(i), flows, new)
            for c in range(count):
                h1[lead_one + (c, there, slice(None))] = new[c]
            if inner:
                zonal, merid = gradient(press, row, count, lane)
                for c in range(count):
                    total[c, there, :] = jnp.where(level == 0, new[c], total[c, there, :] + new[c])
                    u1[0, c, there, :] = u0[c, there, :] - zonal[c]
                    v1[0, c, there, :] = v0[c, there, :] - merid[c]

        sweep(0, tiles + 2, one, UNROLL["coef"])

        def two(i):
            here = eight(i)
            *flows, new = inflows_at(h1, u1, v1, 8 * i + PAD, count, (lead_one, (0,)), lane)
            weights_from(late, here, flows, new)
            for c in range(count):
                wide = min(LANE, cols - c * LANE)
                h_out[0, here, c * LANE : c * LANE + wide] = new[c][:, 0:wide]

        sweep(0, tiles, two, UNROLL["coef"])

    def bring(i):
        here, there, rim_of = window(i)
        for j in range(group):
            bring_rows(
                fields * level + part * group + j, (tr, (j, 0)), (t0, (j,)), here, there, rim_of, count, last
            )

    sweep(0, tiles + 1, bring, UNROLL["bring"])

    def store(c, at, lanes_of):
        for j in range(group):
            t0[j, c, at, :] = rim[level, part * group + j, :, lanes_of]

    rims(store)

    def advance(source, j, row, weights):
        mid = tiles_at(source, at_row(row), count, (j,))
        up = tiles_at(source, pl.ds(row - 1, 8), count, (j,))
        down = tiles_at(source, pl.ds(row + 1, 8), count, (j,))
        right, left = from_east(mid, lane), from_west(mid, lane)
        return [
            weights[0][c] * mid[c]
            + weights[1][c] * right[c]
            + weights[2][c] * left[c]
            + weights[3][c] * up[c]
            + weights[4][c] * down[c]
            for c in range(count)
        ]

    def one(i):
        weights = [tiles_at(early, eight(i), count, (k,)) for k in range(5)]
        for j in range(group):
            new = advance(t0, j, 8 * i + PAD - 8, weights)
            for c in range(count):
                t1[j, c, at_row(8 * i + PAD - 8), :] = new[c]

    sweep(0, tiles + 2, one, UNROLL["one"])

    def two(i):
        here = eight(i)
        weights = [tiles_at(late, here, count, (k,)) for k in range(5)]
        for j in range(group):
            new = advance(t1, j, 8 * i + PAD, weights)
            for c in range(count):
                wide = min(LANE, cols - c * LANE)
                tr_out[j, 0, here, c * LANE : c * LANE + wide] = new[c][:, 0:wide]

    sweep(0, tiles, two, UNROLL["two"])


def tracer_slab(scalars, place, rows, group, tracers, fields, east, west, rim, base, micros, name):
    count, levels, height, cols = tracers.shape
    tiles = (cols - 1) // LANE + 1
    slab = rows + 2 * PAD
    inner = base is None
    E = pl.Element
    slabs = pl.BlockSpec((1, tiles, slab, LANE), lambda l, g, s: (l, 0, 0, 0))
    flat = pl.BlockSpec((tiles, slab, LANE), lambda l, g, s: (0, 0, 0))
    in_specs = [
        pl.BlockSpec(
            (E(group), E(1), E(rows + 8), E(cols)), lambda l, g, s: (g * group, l, s[place + 1] * 8, 0)
        )
    ]
    if inner:
        in_specs += [pl.BlockSpec((E(1), E(rows + 8), E(cols)), lambda l, g, s: (l, s[place + 1] * 8, 0))] * 3
        in_specs += [pl.BlockSpec((E(tiles), E(slab), E(LANE)), lambda l, g, s: (0, s[place] * 8, 0))]
    else:
        in_specs += [slabs] * 5
    in_specs += [HELD] * 3
    operands = [tracers, *fields, east, west, rim]
    out_specs = [
        pl.BlockSpec((E(group), E(1), E(rows), E(cols)), lambda l, g, s: (g * group, l, s[place] * 8, 0)),
        pl.BlockSpec((E(1), E(rows), E(cols)), lambda l, g, s: (l, s[place] * 8, 0)),
    ]
    out_shape = [
        jax.ShapeDtypeStruct(tracers.shape, jnp.float32),
        jax.ShapeDtypeStruct((levels, height, cols), jnp.float32),
    ]
    scratch = [
        pltpu.VMEM((5, tiles, rows + 16, LANE), jnp.float32),
        pltpu.VMEM((5, tiles, rows, LANE), jnp.float32),
        pltpu.VMEM((group, tiles, slab, LANE), jnp.float32),
        pltpu.VMEM((group, tiles, slab, LANE), jnp.float32),
    ]
    plane = pltpu.VMEM((tiles, slab, LANE), jnp.float32)
    aliases = {}
    if inner:
        out_specs += [slabs] * 3 + [flat]
        out_shape += [jax.ShapeDtypeStruct((levels, tiles, slab, LANE), jnp.float32)] * 3
        out_shape += [jax.ShapeDtypeStruct((tiles, slab, LANE), jnp.float32)]
        scratch += [plane] * 5
    else:
        in_specs += [pl.BlockSpec(memory_space=pl.ANY)] * 2
        operands += list(base)
        aliases = {len(operands) - 1: 0, len(operands): 1}
        scratch += [plane]
    return pl.pallas_call(
        functools.partial(slab_kernel, rim.shape[1], group, rows, place, inner),
        grid_spec=pltpu.PrefetchScalarGridSpec(
            num_scalar_prefetch=1,
            grid=(levels, count // group),
            in_specs=in_specs,
            out_specs=out_specs,
            scratch_shapes=scratch,
        ),
        out_shape=out_shape,
        input_output_aliases=aliases,
        cost_estimate=cost(micros),
        compiler_params=params(),
        name=name,
    )(scalars, *operands)


def winds_kernel(s, *refs):
    u_out, v_out = refs[8:10]
    lane = lanes()
    cols = u_out.shape[2]
    for k, place in enumerate((MIDDLE_AT, POLAR_AT)):
        h, u, v, above = refs[4 * k : 4 * k + 4]
        cum, press = refs[10 + 2 * k : 12 + 2 * k]
        count, slab = h.shape[1:3]
        pressure_rows(pl.program_id(0), above, cum, press, h.at[0], count, slab)

        def step(i):
            row = 8 * i + PAD
            to = eight(i + s[place])
            zonal, merid = gradient(press, row, count, lane)
            for c in range(count):
                wide = min(LANE, cols - c * LANE)
                part = slice(c * LANE, c * LANE + wide)
                u_out[0, to, part] = (u[0, c, at_row(row), :] - zonal[c])[:, 0:wide]
                v_out[0, to, part] = (v[0, c, at_row(row), :] - merid[c])[:, 0:wide]

        sweep(0, slab // 8 - 4, step, UNROLL["step"])


def last_winds(scalars, slabs, rows, cols):
    levels, tiles = slabs[0][0].shape[:2]
    in_specs, scratch = [], []
    for h, _, _, _ in slabs:
        tall = h.shape[2]
        in_specs += [pl.BlockSpec((1, tiles, tall, LANE), lambda l, s: (l, 0, 0, 0))] * 3
        in_specs += [HELD]
        scratch += [pltpu.VMEM((tiles, tall, LANE), jnp.float32)] * 2
    out = jax.ShapeDtypeStruct((levels, rows, cols), jnp.float32)
    return pl.pallas_call(
        winds_kernel,
        grid_spec=pltpu.PrefetchScalarGridSpec(
            num_scalar_prefetch=1,
            grid=(levels,),
            in_specs=in_specs,
            out_specs=[pl.BlockSpec((1, rows, cols), lambda l, s: (l, 0, 0))] * 2,
            scratch_shapes=scratch,
        ),
        out_shape=[out, out],
        cost_estimate=cost(8),
        compiler_params=params(),
        name="last_winds",
    )(scalars, *slabs[0], *slabs[1])


def bases(n, cols):
    total = n * cols
    wave = np.arange(KMAX + 1)
    cell = np.arange(total).reshape(n, cols)
    angle = (cell[:, :, None] * wave % total) * (2.0 * math.pi / total)
    forward = np.concatenate([np.cos(angle), np.sin(angle)], 2)
    width = LANE * ((cols - 1) // LANE + 1)
    lane = np.arange(width)
    lane = np.where(lane < width - 2, lane, lane - width)
    cell = np.arange(n)[:, None] * cols + lane[None, :]
    angle = (cell[:, None, :] * wave[:, None] % total) * (2.0 * math.pi / total)
    inverse = np.concatenate([np.cos(angle), np.sin(angle)], 1)
    steep = 2.0 * np.sin(wave * (2.0 * math.pi / total))[:, None]
    slope = np.concatenate([-steep * np.sin(angle), steep * np.cos(angle)], 1)
    return [jnp.asarray(x.astype(np.float32)) for x in (forward, inverse, slope)]


def shards_tiled(tracers, thickness, zonal, meridional, cutoff):
    count, levels, rows, cols = tracers.shape
    n = lax.axis_size("lon")
    me = lax.axis_index("lon").astype(jnp.int32)
    is_north = lax.axis_index("lat") == 0
    inner = rows - BAND

    band_at = rows // 8 - BAND // 8
    scalars = jnp.where(
        is_north,
        jnp.array([1, 0, 0, 0, PAD // 8, 0, BAND // 8, BAND // 8 - 1, PAD // 8 - 1, 1], jnp.int32),
        jnp.array([0, 0, band_at, band_at - 1, PAD // 8 - 1, 1, 0, 0, PAD // 8, 0], jnp.int32),
    )
    scalars = scalars + jnp.where(jnp.arange(10) == 1, me, 0)
    forward, inverse, slope = bases(n, cols)
    limits = jnp.where(is_north, cutoff[0], cutoff[1])
    limits = jnp.broadcast_to(jnp.pad(limits, (0, BAND - POLAR))[:, None], (BAND, LANE))

    def along(value, d):
        return lax.ppermute(value, "lon", [(i, (i + d) % n) for i in range(n)])

    def to_lower(value):
        return lax.ppermute(value, "lev", [(0, 1)])

    fields = (thickness, zonal, meridional)
    sent = band_rows(scalars, zonal, meridional, thickness, n)
    scalars, sent = lax.optimization_barrier((scalars, sent))
    pieces = [sent[0]] + [along(sent[d], d) for d in range(1, n)]

    packed = pack_columns(scalars, tracers, *fields)
    scalars, packed, deep = lax.optimization_barrier((scalars, packed, thickness))
    east, west = along(packed[0], n - 1), along(packed[1], 1)
    column = column_sum(deep)
    scalars, column, pieces = lax.optimization_barrier((scalars, column, pieces))

    pole, facing = edge_rows(scalars, tracers, *fields, east, west)
    scalars, pole, facing = lax.optimization_barrier((scalars, pole, facing))
    facing = lax.ppermute(facing, "lat", [(0, 1), (1, 0)])
    pole = along(pole, n // 2)

    own = spectra(scalars, pieces, forward)
    scalars, own = lax.optimization_barrier((scalars, own))
    upper = to_lower(own[2 * POLAR :])
    column = column_rims(scalars, column, cols, east, west, facing)
    scalars, column, upper = lax.optimization_barrier((scalars, column, upper))
    column = to_lower(column)
    own = jnp.concatenate([own, upper], 0)
    pieces = [own] + [along(own, d) for d in range(1, n)]
    tr, h2, h1, u1, v1, total = tracer_slab(
        scalars, MIDDLE_AT, inner, 10, tracers, (*fields, column), east, west, facing, None, 50, "tracers_inner"
    )
    scalars, total, pieces, pole = lax.optimization_barrier((scalars, total, pieces, pole))
    total = to_lower(total)
    h0, u0, v0, u1b, v1b, h1b, band_total = filtered_band(
        scalars, pieces, limits, inverse, slope, column, thickness, zonal, meridional, east, west, pole
    )
    band_total = to_lower(band_total)
    tr, h2 = tracer_slab(
        scalars, POLAR_AT, BAND, 10, tracers, (h0, u0, v0, u1b, v1b), east, west, pole, (tr, h2), 13,
        "tracers_polar",
    )
    u2, v2 = last_winds(scalars, ((h1, u1, v1, total), (h1b, u1b, v1b, band_total)), rows, cols)
    return (tr, h2, u2, v2)


def tiles_fit(mesh, tracers):
    count, levels, rows, cols = tracers.shape
    rows, cols = rows // mesh.shape["lat"], cols // mesh.shape["lon"]
    count, levels = count // mesh.shape["member"], levels // mesh.shape["lev"]
    last = (cols - 1) % LANE + 1
    return (
        mesh.shape["lat"] == 2
        and mesh.shape["lev"] == 2
        and levels == mesh.shape["lon"]
        and mesh.shape["lon"] % 2 == 0
        and rows % 40 == 0
        and rows >= 2 * BAND + 8
        and last + 4 <= LANE
        and last - 2 >= LANE // 2
        and last + 2 * (count + 2) <= LANE
        and cols > LANE
        and 2 * (count + 3) * levels <= last + 2
        and count % 10 == 0
    )


def solution(mesh):
    placed = (
        P("member", "lev", "lat", "lon"),
        P(("member", "lev"), "lat", "lon"),
        P(("member", "lev"), "lat", "lon"),
        P(("member", "lev"), "lat", "lon"),
        P(),
    )
    outs = (
        P("member", "lev", "lat", "lon"),
        P(("member", "lev"), "lat", "lon"),
        P(("member", "lev"), "lat", "lon"),
        P(("member", "lev"), "lat", "lon"),
    )

    def program(*args):
        part = shards_tiled if tiles_fit(mesh, args[0]) else shards
        return jax.shard_map(part, mesh=mesh, in_specs=placed, out_specs=outs, check_vma=False)(*args)

    return program
```

```python
import functools
import math

import jax
import jax.numpy as jnp
import numpy as np
from jax import lax
from jax.experimental import pallas as pl
from jax.experimental.pallas import tpu as pltpu
from jax.sharding import PartitionSpec as P

NSUB = 2
POLAR = 60
KMAX = 191


COURANT_CAP = 0.15
GRADIENT_COEF = 0.1


def extended_2(block, sides, width):
    for axis, dim in sides:
        count = lax.axis_size(axis)
        forward = [(i, i + 1) for i in range(count - 1)]
        forward.append((count - 1, 0))
        backward = [(target, source) for source, target in forward]
        low = lax.ppermute(
            lax.slice_in_dim(block, block.shape[dim] - width, None, axis=dim), axis, forward
        )
        high = lax.ppermute(lax.slice_in_dim(block, 0, width, axis=dim), axis, backward)
        block = jnp.concatenate([low, block, high], axis=dim)
    return block


def shifted(block, axis, distance):
    devices = range(lax.axis_size(axis))
    route = [((i - distance) % len(devices), i) for i in devices]
    return lax.ppermute(block, axis, route)


def entering(value, axis, join, neutral):
    count, mine = (lax.axis_size(axis), lax.axis_index(axis))
    pieces = lax.all_gather(value, axis)
    running = jnp.full_like(value, 0) + jnp.asarray(neutral, value.dtype)

    def step(position, running):
        longer = join(running, pieces[position])
        return jnp.where(position < mine, longer, running)

    return lax.fori_loop(0, count - 1, step, running)


def advance_level(extended, pressure):
    tracer_count = extended.shape[0] - 3
    thick = extended[tracer_count]
    east_wind = extended[tracer_count + 1]
    north_wind = extended[tracer_count + 2]
    masses = jnp.concatenate([thick[None], extended[:tracer_count] * thick[None]], 0)
    east_courant = COURANT_CAP * jnp.tanh(0.5 * (east_wind[1:-1, :-1] + east_wind[1:-1, 1:]))
    east_flux = (
        jnp.maximum(east_courant, 0.0) * masses[:, 1:-1, :-1]
        + jnp.minimum(east_courant, 0.0) * masses[:, 1:-1, 1:]
    )
    south_courant = COURANT_CAP * jnp.tanh(0.5 * (north_wind[:-1, 1:-1] + north_wind[1:, 1:-1]))
    south_flux = (
        jnp.maximum(south_courant, 0.0) * masses[:, :-1, 1:-1]
        + jnp.minimum(south_courant, 0.0) * masses[:, 1:, 1:-1]
    )
    updated = (
        masses[:, 1:-1, 1:-1]
        - (east_flux[:, :, 1:] - east_flux[:, :, :-1])
        - (south_flux[:, 1:] - south_flux[:, :-1])
    )
    new_thick = updated[0]
    new_mixing = updated[1:] / new_thick[None]
    new_east = east_wind[1:-1, 1:-1] - GRADIENT_COEF * (pressure[1:-1, 2:] - pressure[1:-1, :-2])
    new_north = north_wind[1:-1, 1:-1] - GRADIENT_COEF * (pressure[2:, 1:-1] - pressure[:-2, 1:-1])
    return (new_mixing, new_thick, new_east, new_north)


def wave_basis(anchor, length, lon_total):
    cells = anchor + jnp.arange(length, dtype=jnp.int32)
    waves = jnp.arange(KMAX + 1, dtype=jnp.int32)
    phase = (cells[:, None] * waves[None, :] % lon_total).astype(jnp.float32) * (
        2.0 * math.pi / lon_total
    )
    return jnp.concatenate([jnp.cos(phase), jnp.sin(phase)], 1)


def wave_weights(limits, lon_total):
    waves = jnp.arange(KMAX + 1, dtype=jnp.int32)
    scaled = jnp.where(waves == 0, 1.0, 2.0).astype(jnp.float32) / lon_total
    kept = jnp.where(waves[None, :] <= limits[:, None], scaled[None, :], 0.0)
    return jnp.concatenate([kept, kept], 1)


def smooth_winds(zonal, meridional, cutoff, is_north, is_south):
    level_count, row_count, col_count = zonal.shape
    lon_count = lax.axis_size("lon")
    lon_total = col_count * lon_count
    north_rows = jnp.stack([zonal[:, :POLAR], meridional[:, :POLAR]], 0)
    south_rows = jnp.stack([zonal[:, row_count - POLAR :], meridional[:, row_count - POLAR :]], 0)
    selected = jnp.where(is_north, north_rows, south_rows).reshape(-1, col_count)
    limits = jnp.tile(jnp.where(is_north, cutoff[0], cutoff[1]), 2 * level_count)
    fragment = lax.all_gather(selected, "lon", axis=1, tiled=True)
    basis = wave_basis(jnp.int32(0), fragment.shape[1], lon_total)
    spectrum = jnp.dot(
        fragment, basis, precision=lax.Precision.HIGHEST, preferred_element_type=jnp.float32
    )
    own_basis = wave_basis(lax.axis_index("lon") * col_count, col_count, lon_total)
    filtered = jnp.dot(
        spectrum * wave_weights(limits, lon_total),
        own_basis.T,
        precision=lax.Precision.HIGHEST,
        preferred_element_type=jnp.float32,
    )
    filtered = filtered.reshape(2, level_count, POLAR, col_count)
    row_start = jnp.where(is_north, 0, row_count - POLAR).astype(jnp.int32)
    polar_band = jnp.logical_or(is_north, is_south)
    new_zonal = lax.dynamic_update_slice_in_dim(zonal, filtered[0], row_start, 1)
    new_merid = lax.dynamic_update_slice_in_dim(meridional, filtered[1], row_start, 1)
    return (jnp.where(polar_band, new_zonal, zonal), jnp.where(polar_band, new_merid, meridional))


def shards(tracers, thickness, zonal, meridional, cutoff):
    tracer_count = tracers.shape[0]
    lat_index = lax.axis_index("lat")
    is_north = lat_index == 0
    is_south = lat_index == lax.axis_size("lat") - 1
    lon_count = lax.axis_size("lon")
    flip_sign = jnp.concatenate(
        [jnp.ones((tracer_count + 1,), jnp.float32), -jnp.ones((2,), jnp.float32)]
    )[:, None, None]
    advance_all = jax.vmap(advance_level, in_axes=(1, 0), out_axes=(1, 0, 0, 0))
    for substep in range(NSUB):
        zonal, meridional = smooth_winds(zonal, meridional, cutoff, is_north, is_south)
        state = jnp.concatenate([tracers, thickness[None], zonal[None], meridional[None]], 0)
        extended = extended_2(state, (("lat", 2), ("lon", 3)), 1)
        edges = jnp.stack([state[:, :, 0], state[:, :, -1]], 2)
        opposite = shifted(edges, "lon", lon_count // 2)
        north_rim = jnp.where(is_north, opposite[:, :, 0] * flip_sign, extended[:, :, 0, 1:-1])
        south_rim = jnp.where(is_south, opposite[:, :, 1] * flip_sign, extended[:, :, -1, 1:-1])
        extended = extended.at[:, :, 0, 1:-1].set(north_rim)
        extended = extended.at[:, :, -1, 1:-1].set(south_rim)
        thick_ext = extended[tracer_count]
        column_above = entering(
            jnp.sum(thick_ext, 0),
            "lev",
            lambda earlier, later: earlier + later,
            jnp.zeros(thick_ext.shape[1:], jnp.float32),
        )
        pressure = jnp.cumsum(thick_ext, axis=0) - 0.5 * thick_ext + column_above[None]
        tracers, thickness, zonal, meridional = advance_all(extended, pressure)
    return (tracers, thickness, zonal, meridional)


LANE = 128
POLAR_AT, MIDDLE_AT = 2, 6
UNROLL = dict(step=13, bring=13, coef=8, one=13, two=12)
PAD = 16
BAND = 64


def cost(micros):
    return pl.CostEstimate(flops=0, bytes_accessed=int(micros * 3.3e6), transcendentals=0)


def params(mib=56):
    return pltpu.CompilerParams(vmem_limit_bytes=mib * 1024 * 1024)


HELD = pl.BlockSpec(memory_space=pltpu.VMEM)


def lanes():
    return lax.broadcasted_iota(jnp.int32, (8, LANE), 1)


def at_row(row):
    return pl.ds(row if isinstance(row, int) else pl.multiple_of(row, 8), 8)


def eight(index):
    return at_row(8 * index)


def from_east(tiles, lane):
    turned = [pltpu.roll(t, LANE - 1, 1) for t in tiles]
    n = len(tiles)
    return [jnp.where(lane < LANE - 1, turned[c], turned[(c + 1) % n]) for c in range(n)]


def from_west(tiles, lane):
    turned = [pltpu.roll(t, 1, 1) for t in tiles]
    n = len(tiles)
    return [jnp.where(lane > 0, turned[c], turned[(c - 1) % n]) for c in range(n)]


def courant(a, b):
    return COURANT_CAP * jnp.tanh(0.5 * (a + b))


def rim_lanes(east, west, plane, last, lane):
    both = jnp.where(lane < 2 * plane + 2, east, west)
    return pltpu.roll(both, lax.rem(last + LANE - 2 * plane, LANE), 1)


def inflows(h, u, v, h_n, h_s, v_n, v_s, lane):
    count = range(len(h))
    u_e, h_e = from_east(u, lane), from_east(h, lane)
    c_e = [courant(u[c], u_e[c]) for c in count]
    out_e = [jnp.maximum(c_e[c], 0.0) * h[c] for c in count]
    in_e = [jnp.maximum(-c_e[c], 0.0) * h_e[c] for c in count]
    in_w, out_w = from_west(out_e, lane), from_west(in_e, lane)
    c_s = [courant(v[c], v_s[c]) for c in count]
    c_n = [courant(v_n[c], v[c]) for c in count]
    in_s = [jnp.maximum(-c_s[c], 0.0) * h_s[c] for c in count]
    out_s = [jnp.maximum(c_s[c], 0.0) * h[c] for c in count]
    in_n = [jnp.maximum(c_n[c], 0.0) * h_n[c] for c in count]
    out_n = [jnp.maximum(-c_n[c], 0.0) * h[c] for c in count]
    new = [
        h[c] - (out_e[c] - in_e[c]) + (in_w[c] - out_w[c]) - (out_s[c] - in_s[c]) + (in_n[c] - out_n[c])
        for c in count
    ]
    return in_e, in_w, in_n, in_s, new


def halves(x):
    high = x.astype(jnp.bfloat16)
    return high, (x - high.astype(jnp.float32)).astype(jnp.bfloat16)


def dot3(a, b):
    (a_hi, a_lo), (b_hi, b_lo) = halves(a), halves(b)

    def one(x, y):
        return jnp.dot(x, y, preferred_element_type=jnp.float32)

    return one(a_hi, b_hi) + (one(a_hi, b_lo) + one(a_lo, b_hi))


def sweep(first, end, body, depth):
    whole = (end - first) // depth

    def step(k, _):
        for j in range(depth):
            body(first + k * depth + j)
        return 0

    lax.fori_loop(0, whole, step, 0)
    for i in range(first + whole * depth, end):
        body(i)


def tiles_at(ref, base, count, lead=()):
    return [ref[lead + (c, base, slice(None))] for c in range(count)]


def inflows_at(h, u, v, row, count, lead, lane):
    mid = at_row(row)
    up, down = pl.ds(row - 1, 8), pl.ds(row + 1, 8)
    hl, vl = lead
    return inflows(
        tiles_at(h, mid, count, hl),
        tiles_at(u, mid, count, vl),
        tiles_at(v, mid, count, vl),
        tiles_at(h, up, count, hl),
        tiles_at(h, down, count, hl),
        tiles_at(v, up, count, vl),
        tiles_at(v, down, count, vl),
        lane,
    )


def band_kernel(n, s, *refs):
    ins, outs = refs[: 3 * n], refs[3 * n :]
    for north in (True, False):

        @pl.when(s[0] == int(north))
        def _():
            lo = 0 if north else BAND - POLAR
            for d in range(n):
                u, v, h = ins[3 * d : 3 * d + 3]
                outs[d][0:POLAR, :] = u[0, lo : lo + POLAR, :]
                outs[d][POLAR : 2 * POLAR, :] = v[0, lo : lo + POLAR, :]
                first = 0 if north else BAND - POLAR - 1
                outs[d][2 * POLAR : 3 * POLAR + 1, :] = h[0, first : first + POLAR + 1, :]
                outs[d][3 * POLAR + 1 :, :] = jnp.zeros((3, h.shape[2]), jnp.float32)


def band_rows(scalars, u, v, h, n):
    levels, _, cols = u.shape

    def spec(d):
        return pl.BlockSpec(
            (pl.Element(1), pl.Element(BAND), pl.Element(cols)),
            lambda i, s: (lax.rem(s[1] + d, n), s[POLAR_AT] * 8, 0),
        )

    rows = 3 * POLAR + 4
    return pl.pallas_call(
        functools.partial(band_kernel, n),
        grid_spec=pltpu.PrefetchScalarGridSpec(
            num_scalar_prefetch=1,
            grid=(1,),
            in_specs=[spec(d) for d in range(n) for _ in range(3)],
            out_specs=[pl.BlockSpec((rows, cols), lambda i, s: (0, 0))] * n,
        ),
        out_shape=[jax.ShapeDtypeStruct((rows, cols), jnp.float32)] * n,
        cost_estimate=cost(3),
        compiler_params=params(),
        name="band_rows",
    )(scalars, *([u, v, h] * n))


def spectrum_kernel(n, s, *refs):
    total = None
    for d in range(n):
        part = dot3(refs[d][...], refs[n + d][0])
        total = part if total is None else total + part
    refs[2 * n][...] = total
    refs[2 * n + 1][...] = total[2 * POLAR :]


def spectra(scalars, pieces, basis):
    n = len(pieces)
    rows, cols = pieces[0].shape
    waves = basis.shape[2]

    def spec(d):
        return pl.BlockSpec((1, cols, waves), lambda i, s: (lax.rem(s[1] + n - d, n), 0, 0))

    return pl.pallas_call(
        functools.partial(spectrum_kernel, n),
        grid_spec=pltpu.PrefetchScalarGridSpec(
            num_scalar_prefetch=1,
            grid=(1,),
            in_specs=[HELD] * n + [spec(d) for d in range(n)],
            out_specs=[pl.BlockSpec((k, waves), lambda i, s: (0, 0)) for k in (rows, rows - 2 * POLAR)],
        ),
        out_shape=[jax.ShapeDtypeStruct((k, waves), jnp.float32) for k in (rows, rows - 2 * POLAR)],
        cost_estimate=cost(6),
        compiler_params=params(),
        name="spectra",
    )(scalars, *pieces, *([basis] * n))


def pack_kernel(fields, last, s, t_lo, t_hi, h_lo, h_hi, u_lo, u_hi, v_lo, v_hi, west, east):
    lane = lanes()
    count, levels = t_lo.shape[:2]
    gap = last - 2

    def step(i):
        here = eight(i)
        got_w = got_e = None
        for l in range(levels):
            sources = [(t_lo, t_hi, (f, l)) for f in range(count)]
            sources += [(h_lo, h_hi, (l,)), (u_lo, u_hi, (l,)), (v_lo, v_hi, (l,))]
            got = None
            for f, (lo, hi, lead) in enumerate(sources):
                at = lead + (here, slice(None))
                both = jnp.where(lane < LANE // 2, lo[at], hi[at])
                turned = pltpu.roll(both, 2 * f, 1) if f else both
                mine = jnp.logical_or(jnp.logical_and(lane >= 2 * f, lane < LANE // 2), lane >= gap + 2 * f)
                got = jnp.where(mine, turned, got) if f else turned
            base = 2 * fields * l
            to_w = pltpu.roll(got, base, 1) if l else got
            to_e = pltpu.roll(got, (base - gap + LANE - 2 - last) % LANE, 1)
            got_w = jnp.where(lane >= base, to_w, got_w) if l else to_w
            got_e = jnp.where(lane >= base + LANE - 2 - last, to_e, got_e) if l else to_e
        west[here, :] = got_w
        east[here, :] = got_e

    sweep(0, west.shape[0] // 8, step, 3)


def pack_columns(scalars, tracers, h, u, v):
    count, levels, rows, cols = tracers.shape
    high = (cols - 1) // LANE
    part = rows // 5
    t_spec = [pl.BlockSpec((count, levels, part, LANE), lambda r, s, c=c: (0, 0, r, c)) for c in (0, high)]
    f_spec = [pl.BlockSpec((levels, part, LANE), lambda r, s, c=c: (0, r, c)) for c in (0, high)]
    out = jax.ShapeDtypeStruct((rows, LANE), jnp.float32)
    return pl.pallas_call(
        functools.partial(pack_kernel, count + 3, cols - LANE * high),
        grid_spec=pltpu.PrefetchScalarGridSpec(
            num_scalar_prefetch=1,
            grid=(5,),
            in_specs=t_spec + f_spec * 3,
            out_specs=[pl.BlockSpec((part, LANE), lambda r, s: (r, 0))] * 2,
        ),
        out_shape=[out, out],
        cost_estimate=cost(10),
        compiler_params=params(),
        name="pack_columns",
    )(scalars, tracers, tracers, h, h, u, u, v, v)


def rows_kernel(fields, s, t_top, t_bot, h_top, h_bot, u_top, u_bot, v_top, v_bot,
                east, west, pole, facing, top, bot):
    level = pl.program_id(0)
    lane = lanes()
    cols = h_top.shape[2]
    tail = top.shape[2] - LANE
    last = cols - tail
    height = east.shape[0]
    e_top, e_bot = east[0:8, :], east[height - 8 :, :]
    w_top, w_bot = west[0:8, :], west[height - 8 :, :]
    refs = [(t_top, t_bot, (f, 0)) for f in range(fields - 3)]
    refs += [(h_top, h_bot, (0,)), (u_top, u_bot, (0,)), (v_top, v_bot, (0,))]
    for f in range(fields):
        plane = fields * level + f
        a, b, lead = refs[f]
        top[f, :, 0:cols] = a[lead]
        bot[f, :, 0:cols] = b[lead]
        top[f, :, cols:] = rim_lanes(e_top, w_top, plane, last, lane)[:, last:]
        bot[f, :, cols:] = rim_lanes(e_bot, w_bot, plane, last, lane)[:, last:]
    flips = [1.0] * (fields - 1) + [-1.0]

    @pl.when(s[0] == 1)
    def _():
        for f, flip in enumerate(flips):
            pole[0, f, 0:1, :] = flip * top[f, 1:2, :]
            pole[0, f, 1:2, :] = flip * top[f, 0:1, :]
            facing[0, f] = bot[f, 6:8, :]

    @pl.when(s[0] == 0)
    def _():
        for f, flip in enumerate(flips):
            pole[0, f, 0:1, :] = flip * bot[f, 7:8, :]
            pole[0, f, 1:2, :] = flip * bot[f, 6:7, :]
            facing[0, f] = top[f, 0:2, :]


def edge_rows(scalars, tracers, h, u, v, east, west):
    count, levels, rows, cols = tracers.shape
    fields = count + 3
    width = LANE * ((cols - 1) // LANE + 1)
    ends = (0, rows // 8 - 1)
    t_spec = [pl.BlockSpec((count, 1, 8, cols), lambda l, s, r=r: (0, l, r, 0)) for r in ends]
    f_spec = [pl.BlockSpec((1, 8, cols), lambda l, s, r=r: (l, r, 0)) for r in ends]
    out = jax.ShapeDtypeStruct((levels, fields, 2, width), jnp.float32)
    return pl.pallas_call(
        functools.partial(rows_kernel, fields),
        grid_spec=pltpu.PrefetchScalarGridSpec(
            num_scalar_prefetch=1,
            grid=(levels,),
            in_specs=t_spec + f_spec * 3 + [HELD] * 2,
            out_specs=[pl.BlockSpec((1, fields, 2, width), lambda l, s: (l, 0, 0, 0))] * 2,
            scratch_shapes=[pltpu.VMEM((fields, 8, width), jnp.float32)] * 2,
        ),
        out_shape=[out, out],
        cost_estimate=cost(4),
        compiler_params=params(),
        name="edge_rows",
    )(scalars, tracers, tracers, h, h, u, u, v, v, east, west)


def bring_rows(plane, source, target, here, there, rim, count, last):
    (ref, lead), (out, at) = source, target
    for c in range(count - 1):
        out[at + (c, there, slice(None))] = ref[lead + (here, slice(c * LANE, (c + 1) * LANE))]
    out[at + (count - 1, there, slice(0, last))] = ref[lead + (here, slice(LANE * (count - 1), None))]
    out[at + (count - 1, there, slice(last, None))] = rim(plane)[:, last:]


def pressure_rows(level, above, cum, press, h, count, tall):
    def body(i):
        here = eight(i)
        for c in range(count):
            before = jnp.where(level == 0, above[c, here, :], cum[c, here, :])
            now = h[c, here, :]
            press[c, here, :] = before + 0.5 * now
            cum[c, here, :] = before + now

    sweep(0, tall // 8, body, 8)


def gradient(press, row, count, lane):
    p = tiles_at(press, at_row(row), count)
    p_e, p_w = from_east(p, lane), from_west(p, lane)
    p_n, p_s = tiles_at(press, pl.ds(row - 1, 8), count), tiles_at(press, pl.ds(row + 1, 8), count)
    zonal = [GRADIENT_COEF * (p_e[c] - p_w[c]) for c in range(count)]
    return zonal, [GRADIENT_COEF * (p_s[c] - p_n[c]) for c in range(count)]


def column_kernel(h, total):
    levels, rows, cols = h.shape
    count = total.shape[0]

    def body(i):
        here, there = eight(i), at_row(8 * i + PAD)
        for c in range(count):
            wide = min(LANE, cols - c * LANE)
            part = slice(c * LANE, c * LANE + wide)
            total[c, there, 0:wide] = sum(h[l, here, part] for l in range(levels))

    sweep(0, rows // 8, body, 9)


def column_sum(h):
    _, rows, cols = h.shape
    shape = ((cols - 1) // LANE + 1, rows + 2 * PAD, LANE)
    return pl.pallas_call(
        column_kernel,
        out_shape=jax.ShapeDtypeStruct(shape, jnp.float32),
        in_specs=[pl.BlockSpec(memory_space=pltpu.VMEM)],
        out_specs=pl.BlockSpec(memory_space=pltpu.VMEM),
        cost_estimate=cost(3),
        compiler_params=params(),
        name="column_sum",
    )(h)


def rims_kernel(fields, cols, s, own, east, west, facing, total):
    lane = lanes()
    levels, rows = facing.shape[0], east.shape[0]
    count = total.shape[0]
    last = cols - LANE * (count - 1)
    total[0 : count - 1] = own[0 : count - 1]

    def body(i):
        here, there = eight(i), at_row(8 * i + PAD)
        e, w = east[here, :], west[here, :]
        rim = sum(rim_lanes(e, w, fields * l + fields - 3, last, lane) for l in range(levels))
        total[count - 1, there, :] = jnp.where(lane < last, own[count - 1, there, :], rim)

    sweep(0, rows // 8, body, 9)
    for c in range(count):
        part = slice(c * LANE, (c + 1) * LANE)
        edge = sum(facing[l, fields - 3, :, part] for l in range(levels))
        total[c, PAD - 2 : PAD, :] = edge
        total[c, PAD + rows : PAD + rows + 2, :] = edge


def column_rims(scalars, own, cols, east, west, facing):
    return pl.pallas_call(
        functools.partial(rims_kernel, facing.shape[1], cols),
        grid_spec=pltpu.PrefetchScalarGridSpec(
            num_scalar_prefetch=1,
            grid=(1,),
            in_specs=[HELD] * 4,
            out_specs=pl.BlockSpec(own.shape, lambda i, s: (0, 0, 0)),
        ),
        out_shape=jax.ShapeDtypeStruct(own.shape, jnp.float32),
        cost_estimate=cost(2),
        compiler_params=params(),
        name="column_rims",
    )(scalars, own, east, west, facing)


def filter_kernel(n, s, *refs):
    pieces = refs[:n]
    limits, basis, slope, column, h, u, v, east, west, pole = refs[n : n + 10]
    h0_out, u0_out, v0_out, u1_out, v1_out, h1_out, total = refs[n + 10 : n + 17]
    held, lhs, rhs, cum, press = refs[n + 17 :]
    levels, count, slab = u0_out.shape[:3]
    cols = h.shape[2]
    last = cols - LANE * (count - 1)
    fields = pole.shape[1]
    lane = lanes()

    for l in range(levels):

        def bring(i):
            here, there = eight(i), at_row(8 * (i + s[POLAR_AT + 2]))
            rim_at = eight(i + s[POLAR_AT + 1])
            e, w = east[rim_at, :], west[rim_at, :]
            for f, (ref, out) in enumerate(((h, h0_out), (u, u0_out), (v, v0_out))):
                bring_rows(
                    fields * l + fields - 3 + f, (ref, (l,)), (out, (l,)), here, there,
                    lambda p: rim_lanes(e, w, p, last, lane), count, last,
                )

        sweep(0, BAND // 8 + 1, bring, 9)
        for ends in (True, False):

            @pl.when(s[0] == int(not ends))
            def _():
                at = PAD + BAND if ends else PAD - 2
                for c in range(count):
                    h0_out[l, c, at : at + 2, :] = pole[l, fields - 3, :, c * LANE : (c + 1) * LANE]

        pressure_rows(jnp.int32(l), column, cum, press, h0_out.at[l], count, slab)

        def later(i):
            row = 8 * i
            zonal, merid = gradient(press, row, count, lane)
            for c in range(count):
                u1_out[l, c, at_row(row), :] = u0_out[l, c, at_row(row), :] - zonal[c]
                v1_out[l, c, at_row(row), :] = v0_out[l, c, at_row(row), :] - merid[c]

        sweep(1, slab // 8 - 1, later, 5)

    waves = basis.shape[1]
    for d in range(n):
        held[lax.rem(s[1] + n - d, n)] = pieces[d][...]
    half = waves // 2
    wave = lax.broadcasted_iota(jnp.int32, (POLAR, waves), 1)
    wave = jnp.where(wave < half, wave, wave - half)
    scale = jnp.where(wave == 0, 1.0, 2.0) / (n * cols)
    keep = jnp.where(wave <= limits[0:POLAR, 0:1], scale, 0.0)
    turn = jnp.where(lax.rem(wave[0:2], 2) == 0, 1.0, -1.0)
    one = turn[0:1]
    for north in (True, False):

        @pl.when(s[0] == int(north))
        def _():
            after = 3 * POLAR + 4
            first = PAD if north else PAD + BAND - POLAR
            rim = PAD - 2 if north else PAD + BAND

            def level_step(l, cum):
                u = held[l, 0:POLAR, :] * keep
                v = held[l, POLAR : 2 * POLAR, :] * keep
                thick = held[l, 2 * POLAR : 3 * POLAR + 1, :]
                p = cum + 0.5 * thick
                if north:
                    before = jnp.concatenate([one * p[0:1], p[0 : POLAR - 1]], 0)
                    diff = (p[1:] - before) * keep
                    rhs[0:POLAR, :] = p[0:POLAR] * keep
                else:
                    after = jnp.concatenate([p[2:], one * p[POLAR:]], 0)
                    diff = (after - p[0:POLAR]) * keep
                    rhs[0:POLAR, :] = p[1:] * keep
                w = v - GRADIENT_COEF * diff
                lhs[0:POLAR, :] = u
                lhs[POLAR : 2 * POLAR, :] = v
                lhs[2 * POLAR : 3 * POLAR, :] = w
                for k, (x, sign) in enumerate(((u, 1.0), (v, -1.0), (w, -1.0))):
                    a, b = (x[1:2], x[0:1]) if north else (x[POLAR - 1 :], x[POLAR - 2 : POLAR - 1])
                    at = 3 * POLAR + 2 * k
                    lhs[at : at + 1, :] = sign * one * a
                    lhs[at + 1 : at + 2, :] = sign * one * b
                back = dot3(lhs[...], basis[0])
                grad = dot3(rhs[...], slope[0])
                zonal = back[0:POLAR]
                later = zonal - GRADIENT_COEF * grad[0:POLAR]
                for c in range(count):
                    part = slice(c * LANE, (c + 1) * LANE)
                    u0_out[l, c, first : first + POLAR, :] = zonal[:, part]
                    v0_out[l, c, first : first + POLAR, :] = back[POLAR : 2 * POLAR, part]
                    u1_out[l, c, first : first + POLAR, :] = later[:, part]
                    v1_out[l, c, first : first + POLAR, :] = back[2 * POLAR : 3 * POLAR, part]
                    u0_out[l, c, rim : rim + 2, :] = back[3 * POLAR : 3 * POLAR + 2, part]
                    v0_out[l, c, rim : rim + 2, :] = back[3 * POLAR + 2 : 3 * POLAR + 4, part]
                    v1_out[l, c, rim : rim + 2, :] = back[3 * POLAR + 4 : 3 * POLAR + 6, part]
                return cum + thick

            upper = sum(pieces[d][after : after + POLAR + 1, :] for d in range(n))
            lax.fori_loop(0, levels, level_step, upper)

    def step(k):
        l, i = k // (slab // 8 - 2), lax.rem(k, slab // 8 - 2) + 1
        here = eight(i)
        new = inflows_at(h0_out, u0_out, v0_out, 8 * i, count, ((l,), (l,)), lane)[4]
        for c in range(count):
            h1_out[l, c, here, :] = new[c]
            total[c, here, :] = jnp.where(l == 0, new[c], total[c, here, :] + new[c])

    sweep(0, levels * (slab // 8 - 2), step, UNROLL["step"])


def filtered_band(scalars, pieces, limits, basis, slope, column, h, u, v, east, west, pole):
    n = len(pieces)
    rows, waves = pieces[0].shape
    width = basis.shape[2]
    levels, height, cols = h.shape
    count = column.shape[0]
    slab = BAND + 2 * PAD
    E = pl.Element
    raw = pl.BlockSpec((E(levels), E(BAND + 8), E(cols)), lambda i, s: (0, s[POLAR_AT + 1] * 8, 0))
    out = jax.ShapeDtypeStruct((levels, count, slab, LANE), jnp.float32)
    whole = pl.BlockSpec((levels, count, slab, LANE), lambda i, s: (0, 0, 0, 0))
    return pl.pallas_call(
        functools.partial(filter_kernel, n),
        grid_spec=pltpu.PrefetchScalarGridSpec(
            num_scalar_prefetch=1,
            grid=(1,),
            in_specs=[HELD] * (n + 1)
            + [
                pl.BlockSpec((1, waves, width), lambda i, s: (s[1], 0, 0)),
                pl.BlockSpec((1, waves, width), lambda i, s: (s[1], 0, 0)),
                pl.BlockSpec((E(count), E(slab), E(LANE)), lambda i, s: (0, s[POLAR_AT] * 8, 0)),
            ]
            + [raw] * 3
            + [HELD] * 3,
            out_specs=[whole] * 6 + [pl.BlockSpec((count, slab, LANE), lambda i, s: (0, 0, 0))],
            scratch_shapes=[
                pltpu.VMEM((n, rows, waves), jnp.float32),
                pltpu.VMEM((3 * POLAR + 12, waves), jnp.float32),
                pltpu.VMEM((BAND, waves), jnp.float32),
            ]
            + [pltpu.VMEM((count, slab, LANE), jnp.float32)] * 2,
        ),
        out_shape=[out] * 6 + [jax.ShapeDtypeStruct((count, slab, LANE), jnp.float32)],
        cost_estimate=cost(12),
        compiler_params=params(),
        name="filtered_band",
    )(scalars, *pieces, limits, basis, slope, column, h, u, v, east, west, pole)


def slab_kernel(fields, group, rows, place, inner, s, *refs):
    if inner:
        tr, h, u, v, above, east, west, rim = refs[:8]
        tr_out, h_out, h1, u1, v1, total = refs[8:14]
        early, late, t0, t1, h0, u0, v0, cum, press = refs[14:]
        lead = ((), ())
        lead_one = (0,)
    else:
        tr, h0, u0, v0, u1, v1, east, west, rim = refs[:9]
        tr_out, h_out = refs[11:13]
        early, late, t0, t1, h1 = refs[13:]
        lead = ((0,), (0,))
        lead_one = ()
    level, part = pl.program_id(0), pl.program_id(1)
    lane = lanes()
    count = early.shape[1]
    cols = h_out.shape[2]
    last = cols - LANE * (count - 1)
    tiles = rows // 8

    def window(i):
        rim_at = eight(i + s[place + 1])
        e, w = east[rim_at, :], west[rim_at, :]
        return eight(i), at_row(8 * (i + s[place + 2])), lambda p: rim_lanes(e, w, p, last, lane)

    def rims(store):
        for ends in (True, False):

            @pl.when(s[place + 3] == int(ends))
            def _():
                at = PAD + rows if ends else PAD - 2
                for c in range(count):
                    store(c, slice(at, at + 2), slice(c * LANE, (c + 1) * LANE))

    def weights_from(target, here, flows, new):
        for c in range(count):
            inv = 1.0 / new[c]
            w = [x[c] * inv for x in flows]
            for k in range(4):
                target[k + 1, c, here, :] = w[k]
            target[0, c, here, :] = 1.0 - ((w[0] + w[1]) + (w[2] + w[3]))

    @pl.when(part == 0)
    def _():
        if inner:

            def bring(i):
                here, there, rim_of = window(i)
                for f, (ref, out) in enumerate(((h, h0), (u, u0), (v, v0))):
                    bring_rows(
                        fields * level + fields - 3 + f, (ref, (0,)), (out, ()), here, there, rim_of, count, last
                    )

            sweep(0, tiles + 1, bring, UNROLL["bring"])

            def store(c, at, part):
                for f, out in enumerate((h0, u0, v0)):
                    out[c, at, :] = rim[level, fields - 3 + f, :, part]

            rims(store)
            pressure_rows(level, above, cum, press, h0, count, rows + 2 * PAD)

        def one(i):
            row = 8 * i + PAD - 8
            there = at_row(row)
            *flows, new = inflows_at(h0, u0, v0, row, count, lead, lane)
            weights_from(early, eight(i), flows, new)
            for c in range(count):
                h1[lead_one + (c, there, slice(None))] = new[c]
            if inner:
                zonal, merid = gradient(press, row, count, lane)
                for c in range(count):
                    total[c, there, :] = jnp.where(level == 0, new[c], total[c, there, :] + new[c])
                    u1[0, c, there, :] = u0[c, there, :] - zonal[c]
                    v1[0, c, there, :] = v0[c, there, :] - merid[c]

        sweep(0, tiles + 2, one, UNROLL["coef"])

        def two(i):
            here = eight(i)
            *flows, new = inflows_at(h1, u1, v1, 8 * i + PAD, count, (lead_one, (0,)), lane)
            weights_from(late, here, flows, new)
            for c in range(count):
                wide = min(LANE, cols - c * LANE)
                h_out[0, here, c * LANE : c * LANE + wide] = new[c][:, 0:wide]

        sweep(0, tiles, two, UNROLL["coef"])

    def bring(i):
        here, there, rim_of = window(i)
        for j in range(group):
            bring_rows(
                fields * level + part * group + j, (tr, (j, 0)), (t0, (j,)), here, there, rim_of, count, last
            )

    sweep(0, tiles + 1, bring, UNROLL["bring"])

    def store(c, at, lanes_of):
        for j in range(group):
            t0[j, c, at, :] = rim[level, part * group + j, :, lanes_of]

    rims(store)

    def advance(source, j, row, weights):
        mid = tiles_at(source, at_row(row), count, (j,))
        up = tiles_at(source, pl.ds(row - 1, 8), count, (j,))
        down = tiles_at(source, pl.ds(row + 1, 8), count, (j,))
        right, left = from_east(mid, lane), from_west(mid, lane)
        return [
            weights[0][c] * mid[c]
            + weights[1][c] * right[c]
            + weights[2][c] * left[c]
            + weights[3][c] * up[c]
            + weights[4][c] * down[c]
            for c in range(count)
        ]

    def one(i):
        weights = [tiles_at(early, eight(i), count, (k,)) for k in range(5)]
        for j in range(group):
            new = advance(t0, j, 8 * i + PAD - 8, weights)
            for c in range(count):
                t1[j, c, at_row(8 * i + PAD - 8), :] = new[c]

    sweep(0, tiles + 2, one, UNROLL["one"])

    def two(i):
        here = eight(i)
        weights = [tiles_at(late, here, count, (k,)) for k in range(5)]
        for j in range(group):
            new = advance(t1, j, 8 * i + PAD, weights)
            for c in range(count):
                wide = min(LANE, cols - c * LANE)
                tr_out[j, 0, here, c * LANE : c * LANE + wide] = new[c][:, 0:wide]

    sweep(0, tiles, two, UNROLL["two"])


def tracer_slab(scalars, place, rows, group, tracers, fields, east, west, rim, base, micros, name):
    count, levels, height, cols = tracers.shape
    tiles = (cols - 1) // LANE + 1
    slab = rows + 2 * PAD
    inner = base is None
    E = pl.Element
    slabs = pl.BlockSpec((1, tiles, slab, LANE), lambda l, g, s: (l, 0, 0, 0))
    flat = pl.BlockSpec((tiles, slab, LANE), lambda l, g, s: (0, 0, 0))
    in_specs = [
        pl.BlockSpec(
            (E(group), E(1), E(rows + 8), E(cols)), lambda l, g, s: (g * group, l, s[place + 1] * 8, 0)
        )
    ]
    if inner:
        in_specs += [pl.BlockSpec((E(1), E(rows + 8), E(cols)), lambda l, g, s: (l, s[place + 1] * 8, 0))] * 3
        in_specs += [pl.BlockSpec((E(tiles), E(slab), E(LANE)), lambda l, g, s: (0, s[place] * 8, 0))]
    else:
        in_specs += [slabs] * 5
    in_specs += [HELD] * 3
    operands = [tracers, *fields, east, west, rim]
    out_specs = [
        pl.BlockSpec((E(group), E(1), E(rows), E(cols)), lambda l, g, s: (g * group, l, s[place] * 8, 0)),
        pl.BlockSpec((E(1), E(rows), E(cols)), lambda l, g, s: (l, s[place] * 8, 0)),
    ]
    out_shape = [
        jax.ShapeDtypeStruct(tracers.shape, jnp.float32),
        jax.ShapeDtypeStruct((levels, height, cols), jnp.float32),
    ]
    scratch = [
        pltpu.VMEM((5, tiles, rows + 16, LANE), jnp.float32),
        pltpu.VMEM((5, tiles, rows, LANE), jnp.float32),
        pltpu.VMEM((group, tiles, slab, LANE), jnp.float32),
        pltpu.VMEM((group, tiles, slab, LANE), jnp.float32),
    ]
    plane = pltpu.VMEM((tiles, slab, LANE), jnp.float32)
    aliases = {}
    if inner:
        out_specs += [slabs] * 3 + [flat]
        out_shape += [jax.ShapeDtypeStruct((levels, tiles, slab, LANE), jnp.float32)] * 3
        out_shape += [jax.ShapeDtypeStruct((tiles, slab, LANE), jnp.float32)]
        scratch += [plane] * 5
    else:
        in_specs += [pl.BlockSpec(memory_space=pl.ANY)] * 2
        operands += list(base)
        aliases = {len(operands) - 1: 0, len(operands): 1}
        scratch += [plane]
    return pl.pallas_call(
        functools.partial(slab_kernel, rim.shape[1], group, rows, place, inner),
        grid_spec=pltpu.PrefetchScalarGridSpec(
            num_scalar_prefetch=1,
            grid=(levels, count // group),
            in_specs=in_specs,
            out_specs=out_specs,
            scratch_shapes=scratch,
        ),
        out_shape=out_shape,
        input_output_aliases=aliases,
        cost_estimate=cost(micros),
        compiler_params=params(),
        name=name,
    )(scalars, *operands)


def winds_kernel(s, *refs):
    u_out, v_out = refs[8:10]
    lane = lanes()
    cols = u_out.shape[2]
    for k, place in enumerate((MIDDLE_AT, POLAR_AT)):
        h, u, v, above = refs[4 * k : 4 * k + 4]
        cum, press = refs[10 + 2 * k : 12 + 2 * k]
        count, slab = h.shape[1:3]
        pressure_rows(pl.program_id(0), above, cum, press, h.at[0], count, slab)

        def step(i):
            row = 8 * i + PAD
            to = eight(i + s[place])
            zonal, merid = gradient(press, row, count, lane)
            for c in range(count):
                wide = min(LANE, cols - c * LANE)
                part = slice(c * LANE, c * LANE + wide)
                u_out[0, to, part] = (u[0, c, at_row(row), :] - zonal[c])[:, 0:wide]
                v_out[0, to, part] = (v[0, c, at_row(row), :] - merid[c])[:, 0:wide]

        sweep(0, slab // 8 - 4, step, UNROLL["step"])


def last_winds(scalars, slabs, rows, cols):
    levels, tiles = slabs[0][0].shape[:2]
    in_specs, scratch = [], []
    for h, _, _, _ in slabs:
        tall = h.shape[2]
        in_specs += [pl.BlockSpec((1, tiles, tall, LANE), lambda l, s: (l, 0, 0, 0))] * 3
        in_specs += [HELD]
        scratch += [pltpu.VMEM((tiles, tall, LANE), jnp.float32)] * 2
    out = jax.ShapeDtypeStruct((levels, rows, cols), jnp.float32)
    return pl.pallas_call(
        winds_kernel,
        grid_spec=pltpu.PrefetchScalarGridSpec(
            num_scalar_prefetch=1,
            grid=(levels,),
            in_specs=in_specs,
            out_specs=[pl.BlockSpec((1, rows, cols), lambda l, s: (l, 0, 0))] * 2,
            scratch_shapes=scratch,
        ),
        out_shape=[out, out],
        cost_estimate=cost(8),
        compiler_params=params(),
        name="last_winds",
    )(scalars, *slabs[0], *slabs[1])


def bases(n, cols):
    total = n * cols
    wave = np.arange(KMAX + 1)
    cell = np.arange(total).reshape(n, cols)
    angle = (cell[:, :, None] * wave % total) * (2.0 * math.pi / total)
    forward = np.concatenate([np.cos(angle), np.sin(angle)], 2)
    width = LANE * ((cols - 1) // LANE + 1)
    lane = np.arange(width)
    lane = np.where(lane < width - 2, lane, lane - width)
    cell = np.arange(n)[:, None] * cols + lane[None, :]
    angle = (cell[:, None, :] * wave[:, None] % total) * (2.0 * math.pi / total)
    inverse = np.concatenate([np.cos(angle), np.sin(angle)], 1)
    steep = 2.0 * np.sin(wave * (2.0 * math.pi / total))[:, None]
    slope = np.concatenate([-steep * np.sin(angle), steep * np.cos(angle)], 1)
    return [jnp.asarray(x.astype(np.float32)) for x in (forward, inverse, slope)]


def shards_tiled(tracers, thickness, zonal, meridional, cutoff):
    count, levels, rows, cols = tracers.shape
    n = lax.axis_size("lon")
    me = lax.axis_index("lon").astype(jnp.int32)
    is_north = lax.axis_index("lat") == 0
    inner = rows - BAND

    band_at = rows // 8 - BAND // 8
    scalars = jnp.where(
        is_north,
        jnp.array([1, 0, 0, 0, PAD // 8, 0, BAND // 8, BAND // 8 - 1, PAD // 8 - 1, 1], jnp.int32),
        jnp.array([0, 0, band_at, band_at - 1, PAD // 8 - 1, 1, 0, 0, PAD // 8, 0], jnp.int32),
    )
    scalars = scalars + jnp.where(jnp.arange(10) == 1, me, 0)
    forward, inverse, slope = bases(n, cols)
    limits = jnp.where(is_north, cutoff[0], cutoff[1])
    limits = jnp.broadcast_to(jnp.pad(limits, (0, BAND - POLAR))[:, None], (BAND, LANE))

    def along(value, d):
        return lax.ppermute(value, "lon", [(i, (i + d) % n) for i in range(n)])

    def to_lower(value):
        return lax.ppermute(value, "lev", [(0, 1)])

    fields = (thickness, zonal, meridional)
    sent = band_rows(scalars, zonal, meridional, thickness, n)
    scalars, sent = lax.optimization_barrier((scalars, sent))
    pieces = [sent[0]] + [along(sent[d], d) for d in range(1, n)]

    packed = pack_columns(scalars, tracers, *fields)
    scalars, packed, deep = lax.optimization_barrier((scalars, packed, thickness))
    east, west = along(packed[0], n - 1), along(packed[1], 1)
    column = column_sum(deep)
    scalars, column, pieces, limits = lax.optimization_barrier((scalars, column, pieces, limits))

    pole, facing = edge_rows(scalars, tracers, *fields, east, west)
    scalars, pole, facing = lax.optimization_barrier((scalars, pole, facing))
    facing = lax.ppermute(facing, "lat", [(0, 1), (1, 0)])
    pole = along(pole, n // 2)

    own, upper = spectra(scalars, pieces, forward)
    scalars, own, upper = lax.optimization_barrier((scalars, own, upper))
    upper = to_lower(upper)
    column = column_rims(scalars, column, cols, east, west, facing)
    scalars, column, upper = lax.optimization_barrier((scalars, column, upper))
    column = to_lower(column)
    own = jnp.concatenate([own, upper], 0)
    pieces = [own] + [along(own, d) for d in range(1, n)]
    tr, h2, h1, u1, v1, total = tracer_slab(
        scalars, MIDDLE_AT, inner, 10, tracers, (*fields, column), east, west, facing, None, 50, "tracers_inner"
    )
    scalars, total, pieces, pole = lax.optimization_barrier((scalars, total, pieces, pole))
    total = to_lower(total)
    h0, u0, v0, u1b, v1b, h1b, band_total = filtered_band(
        scalars, pieces, limits, inverse, slope, column, thickness, zonal, meridional, east, west, pole
    )
    band_total = to_lower(band_total)
    tr, h2 = tracer_slab(
        scalars, POLAR_AT, BAND, 10, tracers, (h0, u0, v0, u1b, v1b), east, west, pole, (tr, h2), 13,
        "tracers_polar",
    )
    u2, v2 = last_winds(scalars, ((h1, u1, v1, total), (h1b, u1b, v1b, band_total)), rows, cols)
    return (tr, h2, u2, v2)


def tiles_fit(mesh, tracers):
    count, levels, rows, cols = tracers.shape
    rows, cols = rows // mesh.shape["lat"], cols // mesh.shape["lon"]
    count, levels = count // mesh.shape["member"], levels // mesh.shape["lev"]
    last = (cols - 1) % LANE + 1
    return (
        mesh.shape["lat"] == 2
        and mesh.shape["lev"] == 2
        and levels == mesh.shape["lon"]
        and mesh.shape["lon"] % 2 == 0
        and rows % 40 == 0
        and rows >= 2 * BAND + 8
        and last + 4 <= LANE
        and last - 2 >= LANE // 2
        and last + 2 * (count + 2) <= LANE
        and cols > LANE
        and 2 * (count + 3) * levels <= last + 2
        and count % 10 == 0
    )


def solution(mesh):
    placed = (
        P("member", "lev", "lat", "lon"),
        P(("member", "lev"), "lat", "lon"),
        P(("member", "lev"), "lat", "lon"),
        P(("member", "lev"), "lat", "lon"),
        P(),
    )
    outs = (
        P("member", "lev", "lat", "lon"),
        P(("member", "lev"), "lat", "lon"),
        P(("member", "lev"), "lat", "lon"),
        P(("member", "lev"), "lat", "lon"),
    )

    def program(*args):
        part = shards_tiled if tiles_fit(mesh, args[0]) else shards
        return jax.shard_map(part, mesh=mesh, in_specs=placed, out_specs=outs, check_vma=False)(*args)

    return program
```
